128 devices in a mesh: pts: 32 (over x, y, core), head: 4 (over z).
Axes of the slice: x: 4, y: 4, z: 4, core: 2. Of those that a mesh axis runs over, the one named last changes fastest.
Arguments:
- points: bfloat16 [262144, 256], P('pts'), may hold values from -6 to 6
- cotangent: bfloat16 [262144, 256], P('pts'), may hold values from -6 to 6
- gain_one: bfloat16 [256], replicated, may hold values from 0.25 to 1.75
- w_in: bfloat16 [256, 256], P(None, 'head'), may hold values from -0.375 to 0.375
- slice_weight: bfloat16 [32, 64], replicated, may hold values from -1 to 1
- sharp: bfloat16 [8], P('head'), may hold values from 0.5 to 3
- w_query: bfloat16 [32, 32], replicated, may hold values from -1 to 1
- w_key: bfloat16 [32, 32], replicated, may hold values from -1 to 1
- w_value: bfloat16 [32, 32], replicated, may hold values from -1 to 1
- w_out: bfloat16 [256, 256], P('head'), may hold values from -0.375 to 0.375
- gain_two: bfloat16 [256], replicated, may hold values from 0.25 to 1.75
- w_up: bfloat16 [256, 1024], P(None, 'head'), may hold values from -0.375 to 0.375
- w_down: bfloat16 [1024, 256], P('head'), may hold values from -0.1875 to 0.1875
Outputs:
- mixed: float32 [262144, 256], P('pts')
- grad_points: float32 [262144, 256], P('pts')
- grad_in: float32 [256, 256], P(None, 'head')
- grad_slice: float32 [32, 64], replicated
- grad_sharp: float32 [8], P('head')
- grad_query: float32 [32, 32], replicated
- grad_key: float32 [32, 32], replicated
- grad_value: float32 [32, 32], replicated
- grad_out: float32 [256, 256], P('head')
- grad_up: float32 [256, 1024], P(None, 'head')
- grad_down: float32 [1024, 256], P('head')
- grad_gain1: float32 [256], replicated
- grad_gain2: float32 [256], replicated
The draws below stay inside these ranges and needn't reach their ends.
All inputs are finite; a program needn't handle non-finite values.
Results may differ from the reference program's by a relative error of at most 0.024.
Values may be sent and summed in bfloat16 or wider, within the bound.
No kernel may reach another device: no remote copies, remote signals or barrier semaphores. Data moves between devices by JAX's collectives and lax.ppermute only.
A program may use at most 192 MiB of HBM per device.

```python
import math
import jax
import jax.numpy as jnp
from jax import lax

C = 256
H = 8
HEAD_DIM = 32
M = 64
F = 1024
ROWS_DEV = 8192
N = 262144


def draw_points(key, part):
    key = jax.random.fold_in(key, 11)
    key_common, key_block, key_noise, key_level = jax.random.split(key, 4)
    blocks = N // ROWS_DEV
    common = 1.2 * jax.random.normal(key_common, (C,), jnp.float32)
    offsets = 1.5 * jax.random.normal(key_block, (blocks, C), jnp.float32)
    noise = jax.random.normal(key_noise, (N, C), jnp.float32)
    level = jnp.exp(jax.random.uniform(key_level, (N, 1), jnp.float32, math.log(0.08), math.log(1.0)))
    block_rows = jnp.repeat(offsets, ROWS_DEV, axis=0)
    value = level * (common[None, :] + block_rows + noise)
    return jnp.clip(value, -6.0, 6.0).astype(jnp.bfloat16)


def shard_levels(rng, shape, cuts, low, high):
    def one(axis_at, blocks):
        draws = jax.random.uniform(jax.random.fold_in(jax.random.fold_in(rng, 6), axis_at), (blocks,), jnp.float32, low / len(cuts), high / len(cuts))
        return jnp.repeat(jnp.exp(draws), shape[axis_at] // blocks).reshape((-1,) + (1,) * (len(shape) - axis_at - 1))

    level = one(*cuts[0])
    for cut in cuts[1:]:
        level = level * one(*cut)
    return level


def normal_values(key, shape, deviation, bound, cuts=(), dtype=jnp.bfloat16):
    drawn = jax.random.normal(key, shape, jnp.float32) * deviation
    if len(cuts) > 0:
        drawn = shard_levels(key, shape, cuts, -0.22, 0.18) * drawn
    return jnp.clip(drawn, min=-bound, max=bound).astype(dtype)


def setup_inputs(seed: int = 0) -> dict:
    seeds = jax.random.split(jax.random.key(seed), 14)
    return {
        "points": draw_points(jax.random.fold_in(seeds[13], 71), 0),
        "cotangent": normal_values(seeds[1], (N, C), 1.0, 6.0, ((0, 32),)),
        "gain_one": jnp.clip(1.0 + 0.15 * jax.random.normal(seeds[2], (C,), jnp.float32), 0.25, 1.75).astype(jnp.bfloat16),
        "w_in": normal_values(seeds[3], (C, H * HEAD_DIM), C ** -0.5, 0.375, ((1, 4),)),
        "slice_weight": normal_values(seeds[4], (HEAD_DIM, M), HEAD_DIM ** -0.5, 1.0),
        "sharp": jnp.clip(jnp.exp(math.log(3.0) - 1.7917595 * jax.random.uniform(seeds[5], (H,), jnp.float32) ** shard_levels(seeds[5], (H,), ((0, 4),), -0.2, 0.2)), 0.5, 3.0).astype(jnp.bfloat16),
        "w_query": normal_values(seeds[6], (HEAD_DIM, HEAD_DIM), HEAD_DIM ** -0.5, 1.0),
        "w_key": normal_values(seeds[7], (HEAD_DIM, HEAD_DIM), HEAD_DIM ** -0.5, 1.0),
        "w_value": normal_values(seeds[8], (HEAD_DIM, HEAD_DIM), HEAD_DIM ** -0.5, 1.0),
        "w_out": normal_values(seeds[9], (H * HEAD_DIM, C), (H * HEAD_DIM) ** -0.5, 0.375, ((0, 4),)),
        "gain_two": jnp.clip(1.0 + 0.15 * jax.random.normal(seeds[10], (C,), jnp.float32), 0.25, 1.75).astype(jnp.bfloat16),
        "w_up": normal_values(seeds[11], (C, F), C ** -0.5, 0.375, ((1, 4),)),
        "w_down": normal_values(seeds[12], (F, C), F ** -0.5, 0.1875, ((0, 4),)),
    }


def multiplier(form, left, right):
    return jnp.einsum(form, left.astype(jnp.float32), right.astype(jnp.float32))

def norm_rows(value, gain):
    centred = value - lax.optimization_barrier(jnp.mean(value, -1, keepdims=True))
    scale = lax.rsqrt(lax.optimization_barrier(jnp.mean(centred * centred, -1, keepdims=True)) + 1e-05)
    normed = centred * scale
    return (normed, scale, normed * gain.astype(jnp.float32))

def norm_back(grad, normed, scale, gain):
    dgain = lax.optimization_barrier(jnp.sum(grad * normed, 0))
    scaled = grad * gain.astype(jnp.float32)
    rows = scale * (scaled - lax.optimization_barrier(jnp.mean(scaled, -1, keepdims=True)) - normed * lax.optimization_barrier(jnp.mean(scaled * normed, -1, keepdims=True)))
    return (dgain, rows)

def gelu_tanh(value):
    return 0.5 * value * (1.0 + jnp.tanh(0.7978845608028654 * (value + 0.044715 * value ** 3)))

def gelu_slope(value):
    inner = jnp.tanh(0.7978845608028654 * (value + 0.044715 * value ** 3))
    return 0.5 * (1.0 + inner) + 0.5 * value * (1.0 - inner * inner) * 0.7978845608028654 * (1.0 + 3.0 * 0.044715 * value * value)

def token_attention(slice_tokens, query_matrix, key_matrix, value_matrix):
    heads_points = lax.Precision.HIGHEST
    query_rows = jnp.einsum('nol,lb->nob', slice_tokens, query_matrix, precision=heads_points)
    key_rows = jnp.einsum('nol,lb->nob', slice_tokens, key_matrix, precision=heads_points)
    value_rows = jnp.einsum('nol,lb->nob', slice_tokens, value_matrix, precision=heads_points)
    scores = jnp.einsum('hme,hne->hmn', query_rows, key_rows, precision=heads_points) / jnp.sqrt(jnp.float32(slice_tokens.shape[-1]))
    probs = jnp.exp(scores - lax.optimization_barrier(jnp.max(scores, -1, keepdims=True)))
    probs = probs / lax.optimization_barrier(jnp.sum(probs, -1, keepdims=True))
    return jnp.einsum('hmn,hne->hme', probs, value_rows, precision=heads_points)

def layer_pass(points, cotangent, gain_one, w_in, slice_weight, sharp, w_query, w_key, w_value, w_out, gain_two, w_up, w_down, head_total, slice_weight_sum):
    slice_count = points.shape[0]
    point_heads = w_in.shape[1] // HEAD_DIM
    wide = points.astype(jnp.float32)
    normed_one, scale_one, shifted = norm_rows(wide, gain_one)
    normed_in = shifted.astype(jnp.bfloat16)
    middle = jnp.dot(normed_in, w_in, preferred_element_type=jnp.float32).astype(jnp.bfloat16)
    attended_heads = middle.reshape(slice_count, point_heads, HEAD_DIM)
    raw_logits = multiplier('rhd,dm->rhm', attended_heads, slice_weight)
    sharpness = sharp.astype(jnp.float32)
    logits = raw_logits * sharpness[None, :, None]
    weights = jnp.exp(logits - lax.optimization_barrier(jnp.max(logits, -1, keepdims=True)))
    weights = weights / lax.optimization_barrier(jnp.sum(weights, -1, keepdims=True))
    weights_lowered = weights.astype(jnp.bfloat16)
    numerator = multiplier('bce,bcn->cen', weights_lowered, attended_heads)
    denom = lax.optimization_barrier(jnp.sum(weights, 0))
    numerator, denom = slice_weight_sum((numerator, denom))
    tokens_mid = numerator / denom[:, :, None]
    mixed_tokens, token_back = jax.vjp(token_attention, tokens_mid, w_query.astype(jnp.float32), w_key.astype(jnp.float32), w_value.astype(jnp.float32))
    tokens_lowered = mixed_tokens.astype(jnp.bfloat16)
    spread_back = multiplier('zce,cea->zca', weights_lowered, tokens_lowered).astype(jnp.bfloat16).reshape(slice_count, point_heads * HEAD_DIM)
    resid = wide + head_total(jnp.dot(spread_back, w_out, preferred_element_type=jnp.float32))
    normed_two, scale_two, shifted_two = norm_rows(resid, gain_two)
    normed_mid = shifted_two.astype(jnp.bfloat16)
    hidden = jnp.dot(normed_mid, w_up, preferred_element_type=jnp.float32)
    active = gelu_tanh(hidden).astype(jnp.bfloat16)
    mixed = resid + head_total(jnp.dot(active, w_down, preferred_element_type=jnp.float32))
    grad_down = multiplier('rf,rc->fc', active, cotangent)
    grad_active = multiplier('rc,fc->rf', cotangent, w_down)
    grad_hidden = (grad_active * gelu_slope(hidden)).astype(jnp.bfloat16)
    grad_up = multiplier('rc,rf->cf', normed_mid, grad_hidden)
    grad_mid = head_total(multiplier('rf,cf->rc', grad_hidden, w_up))
    grad_gain2, resid_rows = norm_back(grad_mid, normed_two, scale_two, gain_two)
    grad_resid = cotangent.astype(jnp.float32) + resid_rows
    grad_resid_low = grad_resid.astype(jnp.bfloat16)
    grad_out = multiplier('rk,rc->kc', spread_back, grad_resid_low)
    gradient_spread_tokens = multiplier('rc,kc->rk', grad_resid_low, w_out).astype(jnp.bfloat16).reshape(slice_count, point_heads, HEAD_DIM)
    gradient_slice_weights = multiplier('pwc,wkc->pwk', gradient_spread_tokens, tokens_lowered)
    gradient_slice_tokens = slice_weight_sum(multiplier('bce,bcn->cen', weights_lowered, gradient_spread_tokens))
    grad_mid_tokens, grad_query, grad_key, grad_value = token_back(gradient_slice_tokens)
    gradient_numerator = (grad_mid_tokens / denom[:, :, None]).astype(jnp.bfloat16)
    gradient_denominator = -lax.optimization_barrier(jnp.sum(grad_mid_tokens * tokens_mid, -1)) / denom
    gradient_slice_weights = gradient_slice_weights + multiplier('pwc,wkc->pwk', attended_heads, gradient_numerator) + gradient_denominator[None]
    grad_logits = weights * (gradient_slice_weights - lax.optimization_barrier(jnp.sum(weights * gradient_slice_weights, -1, keepdims=True)))
    grad_sharp = lax.optimization_barrier(jnp.sum(grad_logits * raw_logits, axis=(0, 2)))
    gradient_raw_logits = (grad_logits * sharpness[None, :, None]).astype(jnp.bfloat16)
    grad_slice = multiplier('rhd,rhm->dm', attended_heads, gradient_raw_logits)
    gradient_middle_heads = (multiplier('zce,cea->zca', weights_lowered, gradient_numerator) + multiplier('wli,qi->wlq', gradient_raw_logits, slice_weight)).astype(jnp.bfloat16)
    gradient_middle_heads = gradient_middle_heads.reshape(slice_count, point_heads * HEAD_DIM)
    grad_in = multiplier('rc,rk->ck', normed_in, gradient_middle_heads)
    grad_normed = head_total(multiplier('rk,ck->rc', gradient_middle_heads, w_in))
    grad_gain1, point_rows = norm_back(grad_normed, normed_one, scale_one, gain_one)
    grad_points = grad_resid + point_rows
    return (mixed, grad_points, grad_in, grad_slice, grad_sharp, grad_query, grad_key, grad_value, grad_out, grad_up, grad_down, grad_gain1, grad_gain2)

def unchanged(value):
    return value

def reference(points, cotangent, gain_one, w_in, slice_weight, sharp, w_query, w_key, w_value, w_out, gain_two, w_up, w_down):
    result = layer_pass(points, cotangent, gain_one, w_in, slice_weight, sharp, w_query, w_key, w_value, w_out, gain_two, w_up, w_down, unchanged, unchanged)
    return (result[0], result[1], result[2], result[3], result[4], result[5], result[6], result[7], result[8], result[9], result[10], result[11], result[12])
```

```python
import functools
import jax
import jax.numpy as jnp
from jax import lax
from jax.experimental import pallas as pl
from jax.experimental.pallas import tpu as pltpu
from jax.sharding import PartitionSpec as P

HEAD_DIM = 32
SLICES = 64
C = 256
HEADS = 8
BLOCKS = 4
GH = HEADS // BLOCKS
HM = HEADS * SLICES
ROWS = 512
C0 = 0.7978845608028654
C1 = 0.7978845608028654 * 0.044715
BF = jnp.bfloat16
F32 = jnp.float32
VMEM_LIMIT = 56 * 1024 * 1024


def dot(a, b, precision=None):
    return lax.dot_general(
        a, b, (((1,), (0,)), ((), ())), preferred_element_type=F32, precision=precision
    )


def dot_nt(a, b, precision=None):
    return lax.dot_general(
        a, b, (((1,), (1,)), ((), ())), preferred_element_type=F32, precision=precision
    )


def norm_parts(value):
    centred = value - jnp.mean(value, -1, keepdims=True)
    scale = lax.rsqrt(jnp.mean(centred * centred, -1, keepdims=True) + 1e-05)
    return centred * scale, scale


def norm_back_rows(grad, normed, scale, gain):
    scaled = grad * gain
    return scale * (
        scaled
        - jnp.mean(scaled, -1, keepdims=True)
        - normed * jnp.mean(scaled * normed, -1, keepdims=True)
    )


def sharp_row(block, which, width):
    row = block[which : which + 1, :].astype(F32)
    return jnp.concatenate([row] * (width // C), axis=1)


def softmax_slices(raw, sharp):
    logits = raw * sharp
    grown = jnp.exp(logits - jnp.max(logits, 0, keepdims=True))
    return grown * (1.0 / jnp.sum(grown, 0, keepdims=True))


def fold_rows(value):
    return jnp.sum(value.reshape(value.shape[0] // 8, 8, value.shape[1]), 0)


def own_sums_kernel(pts, gain, w_in, spread_slices, sharp, out, acc, den):
    step = pl.program_id(0)

    @pl.when(step == 0)
    def _():
        acc[...] = jnp.zeros_like(acc)
        den[...] = jnp.zeros_like(den)

    normed, _ = norm_parts(pts[...].astype(F32))
    normed_in = (normed * gain[...]).astype(BF)
    middle = dot_nt(normed_in, w_in[...]).astype(BF)
    raw = dot_nt(spread_slices[...], middle)
    rows = raw.shape[1]
    sharps = sharp[...]
    parts = [
        softmax_slices(raw[h * SLICES : (h + 1) * SLICES], sharp_row(sharps, h, rows))
        for h in range(GH)
    ]
    weights = jnp.concatenate(parts, 0)
    total = weights[:, 0:128]
    for j in range(1, rows // 128):
        total = total + weights[:, j * 128 : (j + 1) * 128]
    den[...] += total
    acc[...] += dot(weights.astype(BF), middle)

    @pl.when(step == pl.num_programs(0) - 1)
    def _():
        flipped = acc[...].T
        lane = lax.broadcasted_iota(jnp.int32, (HEAD_DIM, 128), 1)
        out[0:HEAD_DIM, :] = jnp.where(lane < SLICES, flipped[:HEAD_DIM], flipped[HEAD_DIM:])
        row = jnp.sum(den[...].T, 0, keepdims=True)
        out[HEAD_DIM : HEAD_DIM + 8, :] = jnp.broadcast_to(row, (8, 128))


def weights_kernel(z, pts, gain, in0, in1, in2, in3, spread_slices, s0, s1, s2, s3, *rest):
    wt, mid, w_in = rest[-3:]
    @pl.when(pl.program_id(0) == 0)
    def _():
        for k, ref in enumerate((in0, in1, in2, in3)):
            w_in[k * 64 : (k + 1) * 64, :] = ref[...]

    normed, _ = norm_parts(pts[...].astype(F32))
    normed_in = (normed * gain[...]).astype(BF)
    middle = dot_nt(normed_in, w_in[...]).astype(BF)
    mid[...] = middle
    raw = dot_nt(spread_slices[...], middle)
    rows = raw.shape[1]
    for h in range(HEADS):
        sharp = sharp_row((s0, s1, s2, s3)[h // GH][...], h % GH, rows)
        wt[h * SLICES : (h + 1) * SLICES, :] = softmax_slices(
            raw[h * SLICES : (h + 1) * SLICES], sharp
        ).astype(BF)


def place_tokens(flat, tokens):
    flat[...] = jnp.zeros_like(flat)
    lane = lax.broadcasted_iota(jnp.int32, (HEAD_DIM, 128), 1)
    for k, ref in enumerate(tokens):
        t = ref[0:HEAD_DIM, :]
        flat[k * 64 : k * 64 + 32, k * 128 : (k + 1) * 128] = jnp.where(lane < SLICES, t, 0.0)
        flat[k * 64 + 32 : k * 64 + 64, k * 128 : (k + 1) * 128] = jnp.where(
            lane < SLICES, 0.0, t
        )


def own_block(flipped, k):
    lane = lax.broadcasted_iota(jnp.int32, (HEAD_DIM, 128), 1)
    block = flipped[k * 64 : (k + 1) * 64, k * 128 : (k + 1) * 128]
    return jnp.where(lane < SLICES, block[:HEAD_DIM], block[HEAD_DIM:])


def mlp_kernel(with_sums, z, pts, cot, wt, *refs):
    tokens, refs = refs[:4], refs[4:]
    gain, refs = refs[0], refs[1:]
    ups, downs, outs, refs = refs[:4], refs[4:8], refs[8:12], refs[12:]
    if with_sums:
        (mixed, gres, gspread, gt0, gt1, gt2, gt3, wg0, wg1, wg2, wg3, g2) = refs[:12]
        flat, tok_t, w_out, acc_tok, acc_w, acc_out, acc_g = refs[12:]
    else:
        mixed, gres, gspread, flat, tok_t, w_out = refs[3:]
    step = pl.program_id(0)

    @pl.when(step == 0)
    def _():
        place_tokens(flat, tokens)
        tok_t[...] = flat[...].astype(BF)
        for k, ref in enumerate(outs):
            w_out[k * 64 : (k + 1) * 64, :] = ref[...]
        if with_sums:
            acc_tok[...] = jnp.zeros_like(acc_tok)
            acc_w[...] = jnp.zeros_like(acc_w)
            acc_out[...] = jnp.zeros_like(acc_out)
            acc_g[...] = jnp.zeros_like(acc_g)

    weights = wt[...]
    spread_t = dot(tok_t[...], weights).astype(BF)
    spread = spread_t.T
    resid = pts[...].astype(F32) + dot(spread, w_out[...])
    normed, scale = norm_parts(resid)
    gain_row = gain[...]
    normed_mid = (normed * gain_row).astype(BF)
    cotangent = cot[...]
    total = resid
    gmid = None
    if with_sums:
        cot_t = cotangent.T
        normed_t = normed_mid.T
    for k in range(BLOCKS):
        up, down = ups[k][...], downs[k][...]
        hidden = dot_nt(normed_mid, up)
        square = hidden * hidden
        inner = jnp.tanh(hidden * (C0 + C1 * square))
        half = 0.5 + 0.5 * inner
        active = (hidden * half).astype(BF)
        total = total + dot(active, down)
        slope = half + (hidden * (1.0 - inner * inner)) * (0.5 * C0 + 1.5 * C1 * square)
        ghid = (dot_nt(cotangent, down) * slope).astype(BF)
        part = dot(ghid, up)
        gmid = part if gmid is None else gmid + part
        if with_sums:
            acc_w[k, 0:C, :] += dot(cot_t, active)
            acc_w[k, C : 2 * C, :] += dot(normed_t, ghid)
    mixed[...] = total
    grad = cotangent.astype(F32) + norm_back_rows(gmid, normed, scale, gain_row)
    low = grad.astype(BF)
    gres[...] = low
    gsp = dot_nt(low, w_out[...]).astype(BF)
    gspread[...] = gsp
    if with_sums:
        acc_tok[...] += dot(weights, gsp)
        acc_out[...] += dot(spread_t, low)
        acc_g[...] += fold_rows(gmid * normed)

        @pl.when(step == pl.num_programs(0) - 1)
        def _():
            flipped = acc_tok[...].T
            for k, ref in enumerate((gt0, gt1, gt2, gt3)):
                ref[...] = own_block(flipped, k)
            for k, ref in enumerate((wg0, wg1, wg2, wg3)):
                ref[0 : 2 * C, :] = acc_w[k].astype(ref.dtype)
                ref[2 * C : 2 * C + 64, :] = acc_out[k * 64 : (k + 1) * 64, :].astype(ref.dtype)
            g2[...] = acc_g[...]


def points_kernel(with_sums, z, pts, wt, mid, gspread, gres, *refs):
    tokens, gnums, refs = refs[:4], refs[4:8], refs[8:]
    gain, slices_t, slices, refs = refs[0], refs[1], refs[2], refs[3:]
    ins, sharps, refs = refs[:4], refs[4:8], refs[8:]
    if with_sums:
        qkv, g2, gpts, o0, o1, o2, o3 = refs[:7]
        flat, tok, gn_t, gn, gden, w_in, acc_in, acc_s, acc_g, acc_h = refs[7:]
    else:
        gpts, flat, tok, gn_t, gn, gden, w_in = refs[1:]
    step = pl.program_id(0)

    @pl.when(step == 0)
    def _():
        place_tokens(flat, tokens)
        tok[...] = flat[...].T.astype(BF)
        place_tokens(flat, gnums)
        gn_t[...] = flat[...].astype(BF)
        gn[...] = flat[...].T.astype(BF)
        for k, ref in enumerate(gnums):
            row = ref[HEAD_DIM : HEAD_DIM + 1, :]
            gden[k * 128 : (k + 1) * 128, :] = jnp.broadcast_to(row, (128, 128)).T
        for k, ref in enumerate(ins):
            w_in[k * 64 : (k + 1) * 64, :] = ref[...]
        if with_sums:
            acc_in[...] = jnp.zeros_like(acc_in)
            acc_s[...] = jnp.zeros_like(acc_s)
            acc_g[...] = jnp.zeros_like(acc_g)
            acc_h[...] = jnp.zeros_like(acc_h)

    normed, scale = norm_parts(pts[...].astype(F32))
    gain_row = gain[...]
    weights = wt[...]
    middle = mid[...]
    rows = weights.shape[1]
    gw = dot_nt(tok[...], gspread[...]) + dot_nt(gn[...], middle)
    pieces, sharp_sums = [], []
    if with_sums:
        raw = dot_nt(slices_t[...], middle)
    for h in range(HEADS):
        at = slice(h * SLICES, (h + 1) * SLICES)
        sharp = sharp_row(sharps[h // GH][...], h % GH, rows)
        w = softmax_slices(raw[at], sharp) if with_sums else weights[at].astype(F32)
        g = gw[at] + jnp.concatenate([gden[at, :]] * (rows // 128), axis=1)
        gl = w * (g - jnp.sum(w * g, 0, keepdims=True))
        pieces.append((gl * sharp).astype(BF))
        if with_sums:
            sharp_sums.append(jnp.sum(gl * raw[at], 0, keepdims=True))
    graw = jnp.concatenate(pieces, 0)
    gmid_t = (dot(gn_t[...], weights) + dot(slices[...], graw)).astype(BF)
    gmid = gmid_t.T
    gnormed = dot(gmid, w_in[...])
    gpts[...] = gres[...].astype(F32) + norm_back_rows(gnormed, normed, scale, gain_row)
    if with_sums:
        normed_in = (normed * gain_row).astype(BF)
        acc_in[...] += dot(gmid_t, normed_in)
        acc_s[...] += dot(graw, middle)
        acc_g[...] += fold_rows(gnormed * normed)
        acc_h[...] += jnp.concatenate(sharp_sums, 0)

        @pl.when(step == pl.num_programs(0) - 1)
        def _():
            flipped = acc_s[...].T
            gsharp = acc_h[:, 0:128]
            for j in range(1, rows // 128):
                gsharp = gsharp + acc_h[:, j * 128 : (j + 1) * 128]
            gslice = jnp.zeros((HEAD_DIM, 128), F32)
            for k in range(BLOCKS):
                gslice = gslice + own_block(flipped, k)
            gain1 = jnp.sum(acc_g[...], 0, keepdims=True)
            gain2 = jnp.sum(g2[...], 0, keepdims=True)
            for k, ref in enumerate((o0, o1, o2, o3)):
                ref[0:64, :] = acc_in[k * 64 : (k + 1) * 64, :]
                ref[64:96, 0:128] = gslice
                ref[64:96, 128:256] = qkv[...]
                wide = jnp.concatenate([gsharp[2 * k : 2 * k + 1], gsharp[2 * k + 1 : 2 * k + 2]], 1)
                ref[96:104, :] = jnp.concatenate(
                    [wide, gain1, gain2, jnp.zeros((5, C), F32)], 0
                )


HIGH = lax.Precision.HIGHEST


def token_parts(nd, wq, wk, wv):
    padded = jnp.concatenate([nd, jnp.zeros((88, 128), F32)], 0).T
    denom = padded[:, HEAD_DIM : HEAD_DIM + 1]
    tok = padded[:, :HEAD_DIM] / denom
    q, k, v = dot(tok, wq, HIGH), dot(tok, wk, HIGH), dot(tok, wv, HIGH)
    scores = dot_nt(q, k, HIGH) * (1.0 / HEAD_DIM**0.5)
    row = lax.broadcasted_iota(jnp.int32, (128, 128), 0) < SLICES
    col = lax.broadcasted_iota(jnp.int32, (128, 128), 1) < SLICES
    same = row == col
    scores = jnp.where(same, scores, -jnp.inf)
    p = jnp.exp(scores - jnp.max(scores, -1, keepdims=True))
    p = p / jnp.sum(p, -1, keepdims=True)
    return denom, tok, q, k, v, p


def flip(value):
    n = value.shape[1]
    return jnp.concatenate([value, jnp.zeros((128, 128 - n), F32)], 1).T[:n]


def tokens_kernel(a, b, c, d, wq, wk, wv, total, tokens):
    nd = (a[...] + c[...]) + (b[...] + d[...])
    total[...] = nd
    _, _, _, _, v, p = token_parts(nd, wq[...], wk[...], wv[...])
    mixed = dot(p, v, HIGH).astype(BF).astype(F32)
    tokens[...] = flip(mixed)


def tokens_back_kernel(scale, nd, a, b, c, d, wq, wk, wv, gn, qkv):
    gt = (a[...] + c[...]) + (b[...] + d[...])
    g = jnp.concatenate([gt, jnp.zeros((96, 128), F32)], 0).T[:, :HEAD_DIM]
    wq, wk, wv = wq[...], wk[...], wv[...]
    denom, tok, q, k, v, p = token_parts(nd[...], wq, wk, wv)
    dv = dot(p.T, g, HIGH)
    dp = dot_nt(g, v, HIGH)
    ds = p * (dp - jnp.sum(p * dp, -1, keepdims=True)) * (1.0 / HEAD_DIM**0.5)
    dq = dot(ds, k, HIGH)
    dk = dot(ds.T, q, HIGH)
    gmt = dot_nt(dq, wq, HIGH) + dot_nt(dk, wk, HIGH) + dot_nt(dv, wv, HIGH)
    gnum = (gmt / denom).astype(BF).astype(F32)
    gden = -jnp.sum(gmt * tok, -1, keepdims=True) / denom
    gn[0:HEAD_DIM, :] = flip(gnum)
    gn[HEAD_DIM : HEAD_DIM + 8, :] = flip(jnp.broadcast_to(gden, (128, 8)))
    tok_t = flip(tok)
    qkv[...] = scale * jnp.concatenate(
        [dot(tok_t, dq, HIGH), dot(tok_t, dk, HIGH), dot(tok_t, dv, HIGH), jnp.zeros((32, 32), F32)],
        1,
    )


def full(shape):
    return pl.BlockSpec(shape, lambda *_: (0,) * len(shape))


def part(shape, row):
    return pl.BlockSpec(shape, lambda *_: (row, 0))


def shape_of(shape, dtype):
    return jax.ShapeDtypeStruct(shape, dtype)


def cost(us, moved=1 << 20):
    return pl.CostEstimate(flops=int(us * 1.0e9), bytes_accessed=moved, transcendentals=0)


UP, DOWN, WIN, WOUT, SHARP = (256, 0), (256, 1), (64, 8), (64, 9), (16, 40)


def pack_specs(kind):
    return [part((kind[0], C), kind[1])] * BLOCKS


def local(
    pts_size,
    points,
    cotangent,
    gain_one,
    w_in,
    slice_weight,
    sharp,
    w_query,
    w_key,
    w_value,
    w_out,
    gain_two,
    w_up,
    w_down,
):
    axes = ("pts", "head")
    rows = points.shape[0]
    nblk = rows // ROWS
    own = nblk // BLOCKS

    def pull(value, dx=0, dy=0, dc=0, dz=0):
        pairs = []
        for p in range(pts_size):
            x, y, c = p // 8, (p // 2) % 4, p % 2
            there = p
            if pts_size > 1:
                there = (((x + dx) % 4) * 4 + (y + dy) % 4) * 2 + (c + dc) % 2
            for z in range(BLOCKS):
                pairs.append((there * BLOCKS + (z + dz) % BLOCKS, p * BLOCKS + z))
        return lax.ppermute(value, axes, pairs)

    def pulls(value, axis):
        return [pull(value, **{axis: k}) for k in (1, 2, 3)]

    def tie(*values):
        return lax.optimization_barrier(values)

    def add4(a, r):
        return (a + r[1].astype(F32)) + (r[0].astype(F32) + r[2].astype(F32))

    def core_sum(value):
        return value + pull(value, dc=1) if pts_size > 1 else value

    def rounded(value):
        return lax.reduce_precision(value, 8, 7)

    zeros_peer = pts_size == 1

    def axis_peers(value, axis):
        if zeros_peer:
            return [jnp.zeros_like(value)] * 3
        return pulls(value, axis)

    z = lax.axis_index("head").astype(jnp.int32).reshape(1)

    def block_at(first):
        return lambda i, z: lax.rem(z[0] * own + first + i, nblk)

    def row_spec(first):
        at = block_at(first)
        return pl.BlockSpec((ROWS, C), lambda i, z: (at(i, z), 0))

    def col_spec(first):
        at = block_at(first)
        return pl.BlockSpec((HM, ROWS), lambda i, z: (0, at(i, z)))

    any_spec = pl.BlockSpec(memory_space=pl.ANY)
    params = pltpu.CompilerParams(vmem_limit_bytes=VMEM_LIMIT)

    gain1 = gain_one.astype(F32).reshape(1, C)
    gain2 = gain_two.astype(F32).reshape(1, C)
    slice_t = slice_weight.T
    r = lax.broadcasted_iota(jnp.int32, (HM, C), 0) // SLICES
    c = lax.broadcasted_iota(jnp.int32, (HM, C), 1) // HEAD_DIM
    slices_t = jnp.where(r == c, jnp.tile(slice_t, (HEADS, HEADS)), 0).astype(BF)
    slices = jnp.where((r == c).T, jnp.tile(slice_weight, (HEADS, HEADS)), 0).astype(BF)
    wq, wk, wv = w_query.astype(F32), w_key.astype(F32), w_value.astype(F32)
    sharp_rows = jnp.broadcast_to(jnp.pad(sharp, (0, 14))[:, None], (16, C))
    pack = jnp.concatenate([w_up.T, w_down, w_in.T, w_out, sharp_rows], 0)
    packs = [pack] + pulls(pack, "dz")

    nd = pl.pallas_call(
        own_sums_kernel,
        grid=(nblk,),
        in_specs=[
            pl.BlockSpec((ROWS, C), lambda i: (i, 0)),
            full((1, C)),
            part((64, C), WIN[1]),
            full((128, 64)),
            part((16, C), SHARP[1]),
        ],
        out_specs=full((40, 128)),
        out_shape=shape_of((40, 128), F32),
        scratch_shapes=[pltpu.VMEM((128, 64), F32), pltpu.VMEM((128, 128), F32)],
        compiler_params=params,
        cost_estimate=cost(8),
        name="own_sums",
    )(points, gain1, pack, slices_t[:128, :64], pack)

    def weights_piece(first, count, before):
        kept = [] if before is None else list(before)
        return pl.pallas_call(
            weights_kernel,
            grid_spec=pltpu.PrefetchScalarGridSpec(
                num_scalar_prefetch=1,
                grid=(count,),
                in_specs=[row_spec(first), full((1, C))]
                + pack_specs(WIN)
                + [full((HM, C))]
                + pack_specs(SHARP)
                + [any_spec] * len(kept),
                out_specs=[col_spec(first), row_spec(first)],
                scratch_shapes=[pltpu.VMEM((C, C), BF)],
            ),
            out_shape=[shape_of((HM, rows), BF), shape_of((rows, C), BF)],
            input_output_aliases={12: 0, 13: 1} if kept else {},
            compiler_params=params,
            cost_estimate=cost(0.8 * count),
            name="weights",
        )(z, points, gain1, *packs, slices_t, *packs, *kept)

    def mlp_call(first, count, tokens, state, with_sums):
        wt, before = state
        scratch = [pltpu.VMEM((C, HM), F32), pltpu.VMEM((C, HM), BF), pltpu.VMEM((C, C), BF)]
        out_shape = [shape_of((rows, C), F32), shape_of((rows, C), BF), shape_of((rows, C), BF)]
        out_specs = [row_spec(first)] * 3
        if with_sums:
            scratch += [
                pltpu.VMEM((HM, C), F32),
                pltpu.VMEM((BLOCKS, 2 * C, C), F32),
                pltpu.VMEM((C, C), F32),
                pltpu.VMEM((8, C), F32),
            ]
            out_shape += [shape_of((HEAD_DIM, 128), F32)] * 4
            out_shape += [shape_of((576, C), F32)] + [shape_of((576, C), BF)] * 3
            out_shape += [shape_of((8, C), F32)]
            out_specs += [full((HEAD_DIM, 128))] * 4 + [full((576, C))] * 4 + [full((8, C))]
        return pl.pallas_call(
            functools.partial(mlp_kernel, with_sums),
            grid_spec=pltpu.PrefetchScalarGridSpec(
                num_scalar_prefetch=1,
                grid=(count,),
                in_specs=[row_spec(first), row_spec(first), col_spec(first)]
                + [full((HEAD_DIM, 128))] * 4
                + [full((1, C))]
                + pack_specs(UP)
                + pack_specs(DOWN)
                + pack_specs(WOUT)
                + [any_spec] * len(before),
                out_specs=out_specs,
                scratch_shapes=scratch,
            ),
            out_shape=out_shape,
            input_output_aliases={21: 0, 22: 1, 23: 2} if before else {},
            compiler_params=params,
            cost_estimate=cost(2.5 * count),
            name="mlp",
        )(z, points, cotangent, wt, *tokens, gain2, *packs, *packs, *packs, *before)

    def points_call(first, count, tokens, gnums, state, sums, before):
        wt, mid, gspread, gres = state
        scratch = [
            pltpu.VMEM((C, HM), F32),
            pltpu.VMEM((HM, C), BF),
            pltpu.VMEM((C, HM), BF),
            pltpu.VMEM((HM, C), BF),
            pltpu.VMEM((HM, 128), F32),
            pltpu.VMEM((C, C), BF),
        ]
        out_shape = [shape_of((rows, C), F32)]
        out_specs = [row_spec(first)]
        extra, extra_specs = list(before), [any_spec] * len(before)
        if sums:
            scratch += [
                pltpu.VMEM((C, C), F32),
                pltpu.VMEM((HM, C), F32),
                pltpu.VMEM((8, C), F32),
                pltpu.VMEM((HEADS, ROWS), F32),
            ]
            out_shape += [shape_of((104, C), F32)] * 4
            out_specs += [full((104, C))] * 4
            extra = list(sums)
            extra_specs = [full((HEAD_DIM, 128)), full((8, C))]
        return pl.pallas_call(
            functools.partial(points_kernel, bool(sums)),
            grid_spec=pltpu.PrefetchScalarGridSpec(
                num_scalar_prefetch=1,
                grid=(count,),
                in_specs=[row_spec(first), col_spec(first)]
                + [row_spec(first)] * 3
                + [full((HEAD_DIM, 128))] * 4
                + [full((40, 128))] * 4
                + [full((1, C)), full((HM, C)), full((C, HM))]
                + pack_specs(WIN)
                + pack_specs(SHARP)
                + extra_specs,
                out_specs=out_specs,
                scratch_shapes=scratch,
            ),
            out_shape=out_shape,
            input_output_aliases={25: 0} if before else {},
            compiler_params=params,
            cost_estimate=cost(1.5 * count),
            name="points",
        )(
            z, points, wt, mid, gspread, gres, *tokens, *gnums, gain1, slices_t, slices,
            *packs, *packs, *extra
        )

    nd = core_sum(nd)
    got = axis_peers(nd, "dx")
    split = (own + 1, nblk - 2 * (own + 1))
    nd, points_t = tie(nd, points)
    state = weights_piece(0, own + 1, None)
    got, state = tie(got, state)
    nd = add4(nd, got)
    got = axis_peers(nd, "dy")
    nd, state = tie(nd, state)
    state = weights_piece(own + 1, own + 1, state)
    got, state = tie(got, state)
    nd, own_tokens = pl.pallas_call(
        tokens_kernel,
        out_shape=[shape_of((40, 128), F32), shape_of((HEAD_DIM, 128), F32)],
        compiler_params=params,
        cost_estimate=cost(3),
        name="tokens",
    )(nd, *got, wq, wk, wv)
    got = pulls(own_tokens, "dz")
    own_tokens, state = tie(own_tokens, state)
    state = weights_piece(2 * (own + 1), split[1], state)
    got, state = tie(got, state)
    wt, mid = state
    tokens = [own_tokens] + list(got)

    result = mlp_call(0, own, tokens, (wt, ()), True)
    rest, gts, wgs, g2 = result[:3], result[3:7], result[7:11], result[11]

    others = nblk - own
    q = others // 4
    counts = [others - 3 * q, q, q, q]
    at = own
    got = [pull(gts[BLOCKS - k], dz=k) for k in (1, 2, 3)]
    rest, gts = tie(rest, gts)
    rest = mlp_call(at, counts[0], tokens, (wt, rest), False)
    at += counts[0]
    got, rest = tie(got, rest)
    gt = core_sum(add4(gts[0], got))
    got = axis_peers(gt, "dx")
    rest, gt = tie(rest, gt)
    wgot = [pull(wgs[BLOCKS - k], dz=k) for k in (1, 2, 3)]
    rest = mlp_call(at, counts[1], tokens, (wt, rest), False)
    at += counts[1]
    got, rest = tie(got, rest)
    gt = add4(gt, got)
    got = axis_peers(gt, "dy")
    rest, gt = tie(rest, gt)
    rest = mlp_call(at, counts[2], tokens, (wt, rest), False)
    at += counts[2]
    got, rest, wgot = tie(got, rest, wgot)
    own_gn, qkv = pl.pallas_call(
        functools.partial(tokens_back_kernel, 1.0 / pts_size),
        out_shape=[shape_of((40, 128), F32), shape_of((HEAD_DIM, 128), F32)],
        compiler_params=params,
        cost_estimate=cost(4),
        name="tokens_back",
    )(nd, gt, *got, wq, wk, wv)
    got = pulls(own_gn, "dz")
    rest, own_gn = tie(rest, own_gn)
    rest = mlp_call(at, counts[3], tokens, (wt, rest), False)
    got, rest = tie(got, rest)
    gnums = [own_gn] + list(got)
    mixed, gres, gspread = rest

    wsum = add4(wgs[0], wgot)
    core = lax.axis_index("pts") % 2
    if pts_size > 1:
        low = wsum.astype(BF)
        wsum = rounded(wsum) + pull(low, dc=1).astype(F32)
        wsum = lax.dynamic_slice_in_dim(wsum, core * 288, 288, 0)

    state = (wt, mid, gspread, gres)
    result = points_call(0, own, tokens, gnums, state, (qkv, g2), ())
    gpts, outs = result[0], result[1:]
    q = others // 3
    counts = [others - 2 * q, q, q]
    at = own
    got = [pull(outs[BLOCKS - k], dz=k) for k in (1, 2, 3)]
    wgot = axis_peers(wsum.astype(BF), "dx")
    gpts, outs = tie(gpts, outs)
    (gpts,) = points_call(at, counts[0], tokens, gnums, state, (), (gpts,))
    at += counts[0]
    got, gpts, wgot = tie(got, gpts, wgot)
    tail = core_sum(add4(outs[0], got))
    wsum = add4(rounded(wsum), wgot)
    got = axis_peers(tail, "dx")
    wgot = axis_peers(wsum.astype(BF), "dy")
    gpts, tail = tie(gpts, tail)
    (gpts,) = points_call(at, counts[1], tokens, gnums, state, (), (gpts,))
    at += counts[1]
    got, gpts, wgot = tie(got, gpts, wgot)
    tail = add4(tail, got)
    wsum = add4(rounded(wsum), wgot)
    got = axis_peers(tail, "dy")
    if pts_size > 1:
        other = pull(wsum, dc=1)
        wsum = jnp.where(
            core == 0,
            jnp.concatenate([wsum, other], 0),
            jnp.concatenate([other, wsum], 0),
        )
    gpts, tail = tie(gpts, tail)
    (gpts,) = points_call(at, counts[2], tokens, gnums, state, (), (gpts,))
    got, gpts = tie(got, gpts)
    tail = add4(tail, got)

    grad_down = wsum[0:C].T
    grad_up = wsum[C : 2 * C]
    grad_out = wsum[2 * C :]
    grad_in = tail[0:64].T
    grad_slice = tail[64:96, 0:64] + tail[64:96, 64:128]
    grad_query = tail[64:96, 128:160]
    grad_key = tail[64:96, 160:192]
    grad_value = tail[64:96, 192:224]
    grad_sharp = jnp.sum(tail[96].reshape(GH, 128), -1)
    return (
        mixed,
        gpts,
        grad_in,
        grad_slice,
        grad_sharp,
        grad_query,
        grad_key,
        grad_value,
        grad_out,
        grad_up,
        grad_down,
        tail[97],
        tail[98],
    )


def solution(mesh):
    row, none, cols, heads = P("pts", None), P(), P(None, "head"), P("head")
    down = P("head", None)
    placed = (row, row, none, cols, none, heads, none, none, none, down, none, cols, down)
    given = (row, row, cols, none, heads, none, none, none, down, cols, down, none, none)
    return jax.shard_map(
        functools.partial(local, mesh.shape["pts"]),
        mesh=mesh,
        in_specs=placed,
        out_specs=given,
        check_vma=False,
    )
```

```python
import functools
import jax
import jax.numpy as jnp
from jax import lax
from jax.experimental import pallas as pl
from jax.experimental.pallas import tpu as pltpu
from jax.sharding import PartitionSpec as P

HEAD_DIM = 32
SLICES = 64
C = 256
HEADS = 8
BLOCKS = 4
GH = HEADS // BLOCKS
HM = HEADS * SLICES
C0 = 0.7978845608028654
C1 = 0.7978845608028654 * 0.044715
BF = jnp.bfloat16
F32 = jnp.float32
VMEM_LIMIT = 56 * 1024 * 1024


def dot(a, b, precision=None):
    return lax.dot_general(
        a, b, (((1,), (0,)), ((), ())), preferred_element_type=F32, precision=precision
    )


def dot_nt(a, b, precision=None):
    return lax.dot_general(
        a, b, (((1,), (1,)), ((), ())), preferred_element_type=F32, precision=precision
    )


def norm_parts(value):
    centred = value - jnp.mean(value, -1, keepdims=True)
    scale = lax.rsqrt(jnp.mean(centred * centred, -1, keepdims=True) + 1e-05)
    return centred * scale, scale


def norm_back_rows(grad, normed, scale, gain):
    scaled = grad * gain
    return scale * (
        scaled
        - jnp.mean(scaled, -1, keepdims=True)
        - normed * jnp.mean(scaled * normed, -1, keepdims=True)
    )


def sharp_row(block, which, width):
    row = block[which : which + 1, :].astype(F32)
    return jnp.concatenate([row] * (width // C), axis=1)


def softmax_slices(raw, sharp):
    logits = raw * sharp
    grown = jnp.exp(logits - jnp.max(logits, 0, keepdims=True))
    return grown * (1.0 / jnp.sum(grown, 0, keepdims=True))


def fold_rows(value):
    return jnp.sum(value.reshape(value.shape[0] // 8, 8, value.shape[1]), 0)


def prep_kernel(w_up, w_down, w_in, w_out, sharp, slice_weight, pack, slices_t, slices, s_scr):
    pack[0:256, :] = w_up[...].T
    pack[256:512, :] = w_down[...]
    pack[512:576, :] = w_in[...].T
    pack[576:640, :] = w_out[...]
    pack[640:656, :] = sharp[...]
    s_scr[...] = jnp.zeros_like(s_scr)
    weight = slice_weight[...].astype(F32)
    twice = jnp.concatenate([weight, weight], 1)
    lane = lax.broadcasted_iota(jnp.int32, (HEAD_DIM, 128), 1)
    for k in range(BLOCKS):
        at = slice(k * 128, (k + 1) * 128)
        s_scr[k * 64 : k * 64 + 32, at] = jnp.where(lane < SLICES, twice, 0.0)
        s_scr[k * 64 + 32 : k * 64 + 64, at] = jnp.where(lane < SLICES, 0.0, twice)
    slices[...] = s_scr[...].astype(BF)
    slices_t[...] = s_scr[...].T.astype(BF)


def fill_kernel(z, first, second, before, out):
    @pl.when(pl.program_id(0) == 0)
    def _():
        out[...] = first[...].astype(F32)

    @pl.when(pl.program_id(0) == 1)
    def _():
        out[...] = second[...].astype(F32)


def finish_kernel(z, first, second, before, t0, t1, t2, t3, w0, w1, *refs):
    out, gin, gslice, gsharp, gq, gk, gv, gout, gup, gdown, g1, g2, whole = refs
    fill_kernel(z, first, second, before, out)

    @pl.when((pl.program_id(0) == 0) & (pl.program_id(1) == 0))
    def _():
        tail = (t0[...] + t2[...]) + (t1[...] + t3[...])
        gin[...] = tail[0:64].T
        gslice[...] = tail[64:96, 0:64] + tail[64:96, 64:128]
        gq[...] = tail[64:96, 128:160]
        gk[...] = tail[64:96, 160:192]
        gv[...] = tail[64:96, 192:224]
        gsharp[...] = jnp.concatenate(
            [
                jnp.sum(tail[96:97, 0:128], 1, keepdims=True),
                jnp.sum(tail[96:97, 128:256], 1, keepdims=True),
            ],
            1,
        )
        g1[...] = tail[97:98]
        g2[...] = tail[98:99]

        @pl.when(z[1] == 0)
        def _():
            whole[0:288, :] = w0[...]
            whole[288:576, :] = w1[...]

        @pl.when(z[1] == 1)
        def _():
            whole[0:288, :] = w1[...]
            whole[288:576, :] = w0[...]

        gdown[...] = whole[0:256, :].T
        gup[...] = whole[256:512, :]
        gout[...] = whole[512:576, :]


def own_sums_kernel(pts, gain, w_in, spread_slices, sharp, out, acc, den):
    step = pl.program_id(0)

    @pl.when(step == 0)
    def _():
        acc[...] = jnp.zeros_like(acc)
        den[...] = jnp.zeros_like(den)

    normed, _ = norm_parts(pts[...].astype(F32))
    normed_in = (normed * gain[...]).astype(BF)
    middle = dot_nt(normed_in, w_in[...]).astype(BF)
    raw = dot_nt(spread_slices[:, 0:64], middle)
    rows = raw.shape[1]
    sharps = sharp[...]
    parts = [
        softmax_slices(raw[h * SLICES : (h + 1) * SLICES], sharp_row(sharps, h, rows))
        for h in range(GH)
    ]
    weights = jnp.concatenate(parts, 0)
    total = weights[:, 0:128]
    for j in range(1, rows // 128):
        total = total + weights[:, j * 128 : (j + 1) * 128]
    den[...] += total
    acc[...] += dot(weights.astype(BF), middle)

    @pl.when(step == pl.num_programs(0) - 1)
    def _():
        flipped = acc[...].T
        lane = lax.broadcasted_iota(jnp.int32, (HEAD_DIM, 128), 1)
        out[0:HEAD_DIM, :] = jnp.where(lane < SLICES, flipped[:HEAD_DIM], flipped[HEAD_DIM:])
        row = jnp.sum(den[...].T, 0, keepdims=True)
        out[HEAD_DIM : HEAD_DIM + 8, :] = jnp.broadcast_to(row, (8, 128))


def weights_kernel(z, pts, gain, in0, in1, in2, in3, spread_slices, s0, s1, s2, s3, *rest):
    wt, mid, w_in = rest

    @pl.when(pl.program_id(0) == 0)
    def _():
        for k, ref in enumerate((in0, in1, in2, in3)):
            w_in[k * 64 : (k + 1) * 64, :] = ref[...]

    normed, _ = norm_parts(pts[...].astype(F32))
    normed_in = (normed * gain[...]).astype(BF)
    middle = dot_nt(normed_in, w_in[...]).astype(BF)
    mid[...] = middle
    raw = dot_nt(spread_slices[...], middle)
    rows = raw.shape[1]
    for h in range(HEADS):
        sharp = sharp_row((s0, s1, s2, s3)[h // GH][...], h % GH, rows)
        wt[h * SLICES : (h + 1) * SLICES, :] = softmax_slices(
            raw[h * SLICES : (h + 1) * SLICES], sharp
        ).astype(BF)


def place_tokens(flat, tokens):
    flat[...] = jnp.zeros_like(flat)
    lane = lax.broadcasted_iota(jnp.int32, (HEAD_DIM, 128), 1)
    for k, ref in enumerate(tokens):
        t = ref[0:HEAD_DIM, :]
        flat[k * 64 : k * 64 + 32, k * 128 : (k + 1) * 128] = jnp.where(lane < SLICES, t, 0.0)
        flat[k * 64 + 32 : k * 64 + 64, k * 128 : (k + 1) * 128] = jnp.where(
            lane < SLICES, 0.0, t
        )


def own_block(flipped, k):
    lane = lax.broadcasted_iota(jnp.int32, (HEAD_DIM, 128), 1)
    block = flipped[k * 64 : (k + 1) * 64, k * 128 : (k + 1) * 128]
    return jnp.where(lane < SLICES, block[:HEAD_DIM], block[HEAD_DIM:])


def mlp_kernel(with_sums, z, pts, cot, wt, *refs):
    tokens, refs = refs[:4], refs[4:]
    gain, refs = refs[0], refs[1:]
    ups, downs, outs, refs = refs[:4], refs[4:8], refs[8:12], refs[12:]
    if with_sums:
        (mixed, gres, gspread, low_mixed, gt0, gt1, gt2, gt3, wg0, wg1, wg2, wg3, g2) = refs[:13]
        flat, tok_t, w_out, acc_tok, acc_w, acc_out, acc_g = refs[13:]
    else:
        mixed, gres, gspread, flat, tok_t, w_out = refs[1:]
    step = pl.program_id(0)

    @pl.when(step == 0)
    def _():
        place_tokens(flat, tokens)
        tok_t[...] = flat[...].astype(BF)
        for k, ref in enumerate(outs):
            w_out[k * 64 : (k + 1) * 64, :] = ref[...]
        if with_sums:
            acc_tok[...] = jnp.zeros_like(acc_tok)
            acc_w[...] = jnp.zeros_like(acc_w)
            acc_out[...] = jnp.zeros_like(acc_out)
            acc_g[...] = jnp.zeros_like(acc_g)

    weights = wt[...]
    spread_t = dot(tok_t[...], weights).astype(BF)
    spread = spread_t.T
    resid = pts[...].astype(F32) + dot(spread, w_out[...])
    normed, scale = norm_parts(resid)
    gain_row = gain[...]
    normed_mid = (normed * gain_row).astype(BF)
    cotangent = cot[...]
    total = resid
    gmid = None
    if with_sums:
        cot_t = cotangent.T
        normed_t = normed_mid.T
    for k in range(BLOCKS):
        up, down = ups[k][...], downs[k][...]
        hidden = dot_nt(normed_mid, up)
        square = hidden * hidden
        inner = jnp.tanh(hidden * (C0 + C1 * square))
        half = 0.5 + 0.5 * inner
        gelu = hidden * half
        active = gelu.astype(BF)
        total = total + dot(active, down)
        slope = half + gelu * (1.0 - half) * (2.0 * C0 + 6.0 * C1 * square)
        ghid = (dot_nt(cotangent, down) * slope).astype(BF)
        part = dot(ghid, up)
        gmid = part if gmid is None else gmid + part
        if with_sums:
            acc_w[k, 0:C, :] += dot(cot_t, active)
            acc_w[k, C : 2 * C, :] += dot(normed_t, ghid)
    mixed[...] = total
    grad = cotangent.astype(F32) + norm_back_rows(gmid, normed, scale, gain_row)
    low = grad.astype(BF)
    gres[...] = low
    gsp = dot_nt(low, w_out[...]).astype(BF)
    gspread[...] = gsp
    if with_sums:
        low_mixed[...] = total.astype(BF)
        acc_tok[...] += dot(weights, gsp)
        acc_out[...] += dot(spread_t, low)
        acc_g[...] += fold_rows(gmid * normed)

        @pl.when(step == pl.num_programs(0) - 1)
        def _():
            flipped = acc_tok[...].T
            for k, ref in enumerate((gt0, gt1, gt2, gt3)):
                ref[...] = own_block(flipped, k)
            for k, ref in enumerate((wg0, wg1, wg2, wg3)):
                ref[0 : 2 * C, :] = acc_w[k].astype(ref.dtype)
                ref[2 * C : 2 * C + 64, :] = acc_out[k * 64 : (k + 1) * 64, :].astype(ref.dtype)
            g2[...] = acc_g[...]


def points_kernel(with_sums, z, pts, wt, mid, gspread, gres, *refs):
    tokens, gnums, refs = refs[:4], refs[4:8], refs[8:]
    gain, slices_t, slices, refs = refs[0], refs[1], refs[2], refs[3:]
    ins, sharps, refs = refs[:4], refs[4:8], refs[8:]
    if with_sums:
        qkv, g2, gpts, low_gpts, o0, o1, o2, o3 = refs[:8]
        flat, tok, gn_t, gn, gden, w_in, acc_in, acc_s, acc_g, acc_h = refs[8:]
    else:
        gpts, flat, tok, gn_t, gn, gden, w_in = refs[1:]
    step = pl.program_id(0)

    @pl.when(step == 0)
    def _():
        place_tokens(flat, tokens)
        tok[...] = flat[...].T.astype(BF)
        place_tokens(flat, gnums)
        gn_t[...] = flat[...].astype(BF)
        gn[...] = flat[...].T.astype(BF)
        for k, ref in enumerate(gnums):
            row = ref[HEAD_DIM : HEAD_DIM + 1, :]
            gden[k * 128 : (k + 1) * 128, :] = jnp.broadcast_to(row, (128, 128)).T
        for k, ref in enumerate(ins):
            w_in[k * 64 : (k + 1) * 64, :] = ref[...]
        if with_sums:
            acc_in[...] = jnp.zeros_like(acc_in)
            acc_s[...] = jnp.zeros_like(acc_s)
            acc_g[...] = jnp.zeros_like(acc_g)
            acc_h[...] = jnp.zeros_like(acc_h)

    normed, scale = norm_parts(pts[...].astype(F32))
    gain_row = gain[...]
    weights = wt[...]
    middle = mid[...]
    rows = weights.shape[1]
    gw = dot_nt(tok[...], gspread[...]) + dot_nt(gn[...], middle)
    pieces, sharp_sums = [], []
    if with_sums:
        raw = dot_nt(slices_t[...], middle)
    for h in range(HEADS):
        at = slice(h * SLICES, (h + 1) * SLICES)
        sharp = sharp_row(sharps[h // GH][...], h % GH, rows)
        w = softmax_slices(raw[at], sharp) if with_sums else weights[at].astype(F32)
        g = gw[at] + jnp.concatenate([gden[at, :]] * (rows // 128), axis=1)
        gl = w * (g - jnp.sum(w * g, 0, keepdims=True))
        pieces.append((gl * sharp).astype(BF))
        if with_sums:
            sharp_sums.append(jnp.sum(gl * raw[at], 0, keepdims=True))
    graw = jnp.concatenate(pieces, 0)
    gmid_t = (dot(gn_t[...], weights) + dot(slices[...], graw)).astype(BF)
    gmid = gmid_t.T
    gnormed = dot(gmid, w_in[...])
    result = gres[...].astype(F32) + norm_back_rows(gnormed, normed, scale, gain_row)
    gpts[...] = result
    if with_sums:
        low_gpts[...] = result.astype(BF)
        normed_in = (normed * gain_row).astype(BF)
        acc_in[...] += dot(gmid_t, normed_in)
        acc_s[...] += dot(graw, middle)
        acc_g[...] += fold_rows(gnormed * normed)
        acc_h[...] += jnp.concatenate(sharp_sums, 0)

        @pl.when(step == pl.num_programs(0) - 1)
        def _():
            flipped = acc_s[...].T
            gsharp = acc_h[:, 0:128]
            for j in range(1, rows // 128):
                gsharp = gsharp + acc_h[:, j * 128 : (j + 1) * 128]
            gslice = jnp.zeros((HEAD_DIM, 128), F32)
            for k in range(BLOCKS):
                gslice = gslice + own_block(flipped, k)
            gain1 = jnp.sum(acc_g[...], 0, keepdims=True)
            gain2 = jnp.sum(g2[...], 0, keepdims=True)
            for k, ref in enumerate((o0, o1, o2, o3)):
                ref[0:64, :] = acc_in[k * 64 : (k + 1) * 64, :]
                ref[64:96, 0:128] = gslice
                ref[64:96, 128:256] = qkv[...]
                wide = jnp.concatenate([gsharp[2 * k : 2 * k + 1], gsharp[2 * k + 1 : 2 * k + 2]], 1)
                ref[96:104, :] = jnp.concatenate(
                    [wide, gain1, gain2, jnp.zeros((5, C), F32)], 0
                )


HIGH = lax.Precision.HIGHEST


def token_parts(nd, wq, wk, wv):
    padded = jnp.concatenate([nd, jnp.zeros((88, 128), F32)], 0).T
    denom = padded[:, HEAD_DIM : HEAD_DIM + 1]
    tok = padded[:, :HEAD_DIM] / denom
    q, k, v = dot(tok, wq, HIGH), dot(tok, wk, HIGH), dot(tok, wv, HIGH)
    scores = dot_nt(q, k, HIGH) * (1.0 / HEAD_DIM**0.5)
    row = lax.broadcasted_iota(jnp.int32, (128, 128), 0) < SLICES
    col = lax.broadcasted_iota(jnp.int32, (128, 128), 1) < SLICES
    same = row == col
    scores = jnp.where(same, scores, -jnp.inf)
    p = jnp.exp(scores - jnp.max(scores, -1, keepdims=True))
    p = p / jnp.sum(p, -1, keepdims=True)
    return denom, tok, q, k, v, p


def flip(value):
    n = value.shape[1]
    return jnp.concatenate([value, jnp.zeros((128, 128 - n), F32)], 1).T[:n]


def tokens_kernel(a, b, c, d, wq, wk, wv, total, tokens):
    nd = (a[...] + c[...]) + (b[...] + d[...])
    total[...] = nd
    _, _, _, _, v, p = token_parts(nd, wq[...], wk[...], wv[...])
    mixed = dot(p, v, HIGH).astype(BF).astype(F32)
    tokens[...] = flip(mixed)


def tokens_back_kernel(scale, nd, a, b, c, d, wq, wk, wv, gn, qkv):
    gt = (a[...] + c[...]) + (b[...] + d[...])
    g = jnp.concatenate([gt, jnp.zeros((96, 128), F32)], 0).T[:, :HEAD_DIM]
    wq, wk, wv = wq[...], wk[...], wv[...]
    denom, tok, q, k, v, p = token_parts(nd[...], wq, wk, wv)
    dv = dot(p.T, g, HIGH)
    dp = dot_nt(g, v, HIGH)
    ds = p * (dp - jnp.sum(p * dp, -1, keepdims=True)) * (1.0 / HEAD_DIM**0.5)
    dq = dot(ds, k, HIGH)
    dk = dot(ds.T, q, HIGH)
    gmt = dot_nt(dq, wq, HIGH) + dot_nt(dk, wk, HIGH) + dot_nt(dv, wv, HIGH)
    gnum = (gmt / denom).astype(BF).astype(F32)
    gden = -jnp.sum(gmt * tok, -1, keepdims=True) / denom
    gn[0:HEAD_DIM, :] = flip(gnum)
    gn[HEAD_DIM : HEAD_DIM + 8, :] = flip(jnp.broadcast_to(gden, (128, 8)))
    tok_t = flip(tok)
    qkv[...] = scale * jnp.concatenate(
        [dot(tok_t, dq, HIGH), dot(tok_t, dk, HIGH), dot(tok_t, dv, HIGH), jnp.zeros((32, 32), F32)],
        1,
    )


def full(shape):
    return pl.BlockSpec(shape, lambda *_: (0,) * len(shape))


def part(shape, row):
    return pl.BlockSpec(shape, lambda *_: (row, 0))


def shape_of(shape, dtype):
    return jax.ShapeDtypeStruct(shape, dtype)


def cost(us, moved=1 << 20):
    return pl.CostEstimate(flops=int(us * 1.0e9), bytes_accessed=moved, transcendentals=0)


UP, DOWN, WIN, WOUT, SHARP = (256, 0), (256, 1), (64, 8), (64, 9), (16, 40)
WIDE, NARROW = 1024, 512


def pack_specs(kind):
    return [part((kind[0], C), kind[1])] * BLOCKS


def local(
    pts_size,
    points,
    cotangent,
    gain_one,
    w_in,
    slice_weight,
    sharp,
    w_query,
    w_key,
    w_value,
    w_out,
    gain_two,
    w_up,
    w_down,
):
    axes = ("pts", "head")
    rows = points.shape[0]
    quarter = rows // BLOCKS

    def pull(value, dx=0, dy=0, dc=0, dz=0):
        pairs = []
        for p in range(pts_size):
            x, y, c = p // 8, (p // 2) % 4, p % 2
            there = p
            if pts_size > 1:
                there = (((x + dx) % 4) * 4 + (y + dy) % 4) * 2 + (c + dc) % 2
            for z in range(BLOCKS):
                pairs.append((there * BLOCKS + (z + dz) % BLOCKS, p * BLOCKS + z))
        return lax.ppermute(value, axes, pairs)

    def pulls(value, axis):
        return [pull(value, **{axis: k}) for k in (1, 2, 3)]

    def tie(*values):
        return lax.optimization_barrier(values)

    def add4(a, r):
        return (a + r[1].astype(F32)) + (r[0].astype(F32) + r[2].astype(F32))

    def core_sum(value):
        return value + pull(value, dc=1) if pts_size > 1 else value

    def rounded(value):
        return lax.reduce_precision(value, 8, 7)

    def axis_peers(value, axis):
        if pts_size == 1:
            return [jnp.zeros_like(value)] * 3
        return pulls(value, axis)

    core = lax.axis_index("pts").astype(jnp.int32) % 2
    z = jnp.stack([lax.axis_index("head").astype(jnp.int32), core])

    def row_spec(size, away, first=0):
        n = quarter // size
        return pl.BlockSpec(
            (size, C), lambda i, z: (lax.rem(z[0] + away, BLOCKS) * n + first // size + i, 0)
        )

    def own_spec(size, first=0):
        return pl.BlockSpec((size, C), lambda i, z: (first // size + i, 0))

    def own_cols(size, first=0):
        return pl.BlockSpec((HM, size), lambda i, z: (0, first // size + i))

    def grid(steps, in_specs, out_specs, scratch=()):
        return pltpu.PrefetchScalarGridSpec(
            num_scalar_prefetch=1,
            grid=steps,
            in_specs=in_specs,
            out_specs=out_specs,
            scratch_shapes=scratch,
        )

    any_spec = pl.BlockSpec(memory_space=pl.ANY)
    params = pltpu.CompilerParams(vmem_limit_bytes=VMEM_LIMIT)

    gain1 = gain_one.astype(F32).reshape(1, C)
    gain2 = gain_two.astype(F32).reshape(1, C)
    wq, wk, wv = w_query.astype(F32), w_key.astype(F32), w_value.astype(F32)
    sharp_rows = jnp.broadcast_to(jnp.pad(sharp, (0, 14))[:, None], (16, C))
    pack, slices_t, slices = pl.pallas_call(
        prep_kernel,
        out_shape=[shape_of((656, C), BF), shape_of((HM, C), BF), shape_of((C, HM), BF)],
        scratch_shapes=[pltpu.VMEM((C, HM), F32)],
        compiler_params=params,
        cost_estimate=cost(2),
        name="prep",
    )(w_up, w_down, w_in, w_out, sharp_rows, slice_weight)
    packs = [pack] + pulls(pack, "dz")

    nd = pl.pallas_call(
        own_sums_kernel,
        grid=(rows // WIDE,),
        in_specs=[
            pl.BlockSpec((WIDE, C), lambda i: (i, 0)),
            full((1, C)),
            part((64, C), WIN[1]),
            part((128, C), 0),
            part((16, C), SHARP[1]),
        ],
        out_specs=full((40, 128)),
        out_shape=shape_of((40, 128), F32),
        scratch_shapes=[pltpu.VMEM((128, 64), F32), pltpu.VMEM((128, 128), F32)],
        compiler_params=params,
        cost_estimate=cost(8),
        name="own_sums",
    )(points, gain1, pack, slices_t, pack)

    def weights_call(away):
        return pl.pallas_call(
            weights_kernel,
            grid_spec=grid(
                (quarter // WIDE,),
                [row_spec(WIDE, away), full((1, C))]
                + pack_specs(WIN)
                + [full((HM, C))]
                + pack_specs(SHARP),
                [own_cols(WIDE), own_spec(WIDE)],
                [pltpu.VMEM((C, C), BF)],
            ),
            out_shape=[shape_of((HM, quarter), BF), shape_of((quarter, C), BF)],
            compiler_params=params,
            cost_estimate=cost(5),
            name="weights",
        )(z, points, gain1, *packs, slices_t, *packs)

    def mlp_call(away, first, count, size, tokens, wt, before):
        with_sums = before is None
        scratch = [pltpu.VMEM((C, HM), F32), pltpu.VMEM((C, HM), BF), pltpu.VMEM((C, C), BF)]
        out_shape = [shape_of((rows, C), F32), shape_of((count, C), BF), shape_of((count, C), BF)]
        out_specs = [row_spec(size, away, first), own_spec(size), own_spec(size)]
        kept = []
        if with_sums:
            scratch += [
                pltpu.VMEM((HM, C), F32),
                pltpu.VMEM((BLOCKS, 2 * C, C), F32),
                pltpu.VMEM((C, C), F32),
                pltpu.VMEM((8, C), F32),
            ]
            out_shape += [shape_of((count, C), BF)]
            out_shape += [shape_of((HEAD_DIM, 128), F32)] * 4
            out_shape += [shape_of((576, C), F32)] + [shape_of((576, C), BF)] * 3
            out_shape += [shape_of((8, C), F32)]
            out_specs += [own_spec(size)]
            out_specs += [full((HEAD_DIM, 128))] * 4 + [full((576, C))] * 4 + [full((8, C))]
        else:
            kept = [before]
        rest = row_spec(size, away, first)
        return pl.pallas_call(
            functools.partial(mlp_kernel, with_sums),
            grid_spec=grid(
                (count // size,),
                [rest, rest, own_cols(size, first)]
                + [full((HEAD_DIM, 128))] * 4
                + [full((1, C))]
                + pack_specs(UP)
                + pack_specs(DOWN)
                + pack_specs(WOUT)
                + [any_spec] * len(kept),
                out_specs,
                scratch,
            ),
            out_shape=out_shape,
            input_output_aliases={21: 0} if kept else {},
            compiler_params=params,
            cost_estimate=cost(count / 150),
            name="mlp",
        )(z, points, cotangent, wt, *tokens, gain2, *packs, *packs, *packs, *kept)

    def points_call(away, first, count, size, tokens, gnums, state, sums, before):
        wt, mid, gspread, gres = state
        scratch = [
            pltpu.VMEM((C, HM), F32),
            pltpu.VMEM((HM, C), BF),
            pltpu.VMEM((C, HM), BF),
            pltpu.VMEM((HM, C), BF),
            pltpu.VMEM((HM, 128), F32),
            pltpu.VMEM((C, C), BF),
        ]
        out_shape = [shape_of((rows, C), F32)]
        out_specs = [row_spec(size, away, first)]
        extra, extra_specs = [before], [any_spec]
        if sums:
            scratch += [
                pltpu.VMEM((C, C), F32),
                pltpu.VMEM((HM, C), F32),
                pltpu.VMEM((8, C), F32),
                pltpu.VMEM((HEADS, size), F32),
            ]
            out_shape += [shape_of((count, C), BF)] + [shape_of((104, C), F32)] * 4
            out_specs += [own_spec(size)] + [full((104, C))] * 4
            extra = list(sums)
            extra_specs = [full((HEAD_DIM, 128)), full((8, C))]
        return pl.pallas_call(
            functools.partial(points_kernel, bool(sums)),
            grid_spec=grid(
                (count // size,),
                [row_spec(size, away, first), own_cols(size, first), own_spec(size, first)]
                + [own_spec(size)] * 2
                + [full((HEAD_DIM, 128))] * 4
                + [full((40, 128))] * 4
                + [full((1, C)), full((HM, C)), full((C, HM))]
                + pack_specs(WIN)
                + pack_specs(SHARP)
                + extra_specs,
                out_specs,
                scratch,
            ),
            out_shape=out_shape,
            input_output_aliases={} if sums else {25: 0},
            compiler_params=params,
            cost_estimate=cost(count / 200),
            name="points",
        )(
            z, points, wt, mid, gspread, gres, *tokens, *gnums, gain1, slices_t, slices,
            *packs, *packs, *extra
        )

    steps = quarter // NARROW
    fill_specs = [
        pl.BlockSpec((NARROW, C), lambda q, i, z: (jnp.where(q == 0, i, steps - 1), 0)),
        pl.BlockSpec((NARROW, C), lambda q, i, z: (jnp.where(q == 0, 0, i), 0)),
        any_spec,
    ]
    fill_out = pl.BlockSpec(
        (NARROW, C), lambda q, i, z: (lax.rem(z[0] + 1 + 2 * q, BLOCKS) * steps + i, 0)
    )

    nd = core_sum(nd)
    got = axis_peers(nd, "dx")
    nd, packs[0] = tie(nd, packs[0])
    mine = weights_call(0)
    got, mine = tie(got, mine)
    nd = add4(nd, got)
    got = axis_peers(nd, "dy")
    nd, packs[0] = tie(nd, packs[0])
    opposite = weights_call(2)
    got, opposite = tie(got, opposite)
    nd, own_tokens = pl.pallas_call(
        tokens_kernel,
        out_shape=[shape_of((40, 128), F32), shape_of((HEAD_DIM, 128), F32)],
        compiler_params=params,
        cost_estimate=cost(3),
        name="tokens",
    )(nd, *got, wq, wk, wv)
    tokens = [own_tokens] + pulls(own_tokens, "dz")

    result = mlp_call(0, 0, quarter, WIDE, tokens, mine[0], None)
    (mixed, gres, gspread, send), gts, wgs, g2 = result[:4], result[4:8], result[8:12], result[12]

    got = [pull(gts[BLOCKS - k], dz=k) for k in (1, 2, 3)]
    gt = core_sum(add4(gts[0], got))
    got = axis_peers(gt, "dx")
    gt, send, mixed = tie(gt, send, mixed)
    near = [pull(send, dz=1), pull(send, dz=3)]
    half = quarter // 2
    mixed, gres_a, gspread_a = mlp_call(2, 0, half, NARROW, tokens, opposite[0], mixed)
    got, mixed = tie(got, mixed)
    gt = add4(gt, got)
    got = axis_peers(gt, "dy")
    gt, mixed = tie(gt, mixed)
    mixed, gres_b, gspread_b = mlp_call(2, half, half, NARROW, tokens, opposite[0], mixed)
    got, mixed = tie(got, mixed)
    own_gn, qkv = pl.pallas_call(
        functools.partial(tokens_back_kernel, 1.0 / pts_size),
        out_shape=[shape_of((40, 128), F32), shape_of((HEAD_DIM, 128), F32)],
        compiler_params=params,
        cost_estimate=cost(4),
        name="tokens_back",
    )(nd, gt, *got, wq, wk, wv)
    gnums = [own_gn] + pulls(own_gn, "dz")

    gnums[1], wgs = tie(gnums[1], wgs)
    wgot = [pull(wgs[BLOCKS - k], dz=k) for k in (1, 2, 3)]
    state = (mine[0], mine[1], gspread, gres)
    result = points_call(0, 0, quarter, NARROW, tokens, gnums, state, (qkv, g2), None)
    gpts, send, outs = result[0], result[1], result[2:]
    wgot, gpts, outs, send = tie(wgot, gpts, outs, send)

    got = [pull(outs[BLOCKS - k], dz=k) for k in (1, 2, 3)]
    far = [pull(send, dz=1), pull(send, dz=3)]
    wsum = add4(wgs[0], wgot)
    if pts_size > 1:
        low = wsum.astype(BF)
        wsum = rounded(wsum) + pull(low, dc=1).astype(F32)
        wsum = lax.dynamic_slice_in_dim(wsum, core * 288, 288, 0)
    wgot = axis_peers(wsum.astype(BF), "dx")
    state = (opposite[0], opposite[1], gspread_a, gres_a)
    (gpts,) = points_call(2, 0, half, NARROW, tokens, gnums, state, (), gpts)
    got, gpts, wgot = tie(got, gpts, wgot)
    tail = core_sum(add4(outs[0], got))
    wsum = add4(rounded(wsum), wgot)
    got = axis_peers(tail, "dx")
    wgot = axis_peers(wsum.astype(BF), "dy")
    gpts, tail = tie(gpts, tail)
    state = (opposite[0], opposite[1], gspread_b, gres_b)
    (gpts,) = points_call(2, half, half, NARROW, tokens, gnums, state, (), gpts)
    got, gpts, wgot = tie(got, gpts, wgot)
    tail = add4(tail, got)
    wsum = add4(rounded(wsum), wgot)
    got = axis_peers(tail, "dy")
    other = pull(wsum, dc=1) if pts_size > 1 else wsum[288:]
    wsum = wsum[:288]
    tail, mixed, near = tie(tail, mixed, near)
    mixed = pl.pallas_call(
        fill_kernel,
        grid_spec=grid((2, steps), fill_specs, fill_out),
        out_shape=shape_of((rows, C), F32),
        input_output_aliases={3: 0},
        compiler_params=params,
        cost_estimate=cost(4),
        name="fill",
    )(z, *near, mixed)
    got, mixed, other = tie(got, mixed, other)
    shapes = [(C, 64), (32, 64), (1, GH), (32, 32), (32, 32), (32, 32)]
    shapes += [(64, C), (C, C), (C, C), (1, C), (1, C)]
    result = pl.pallas_call(
        finish_kernel,
        grid_spec=grid(
            (2, steps),
            fill_specs + [full((104, C))] * 4 + [full((288, C))] * 2,
            [fill_out] + [full(s) for s in shapes],
            [pltpu.VMEM((576, C), F32)],
        ),
        out_shape=[shape_of((rows, C), F32)] + [shape_of(s, F32) for s in shapes],
        input_output_aliases={3: 0},
        compiler_params=params,
        cost_estimate=cost(4),
        name="finish",
    )(z, *far, gpts, tail, *got, wsum, other)
    gpts, gin, gslice, gsharp, gq, gk, gv, gout, gup, gdown, g1, g2 = result
    return (
        mixed, gpts, gin, gslice, gsharp.reshape(GH), gq, gk, gv, gout, gup, gdown,
        g1.reshape(C), g2.reshape(C),
    )


def solution(mesh):
    row, none, cols, heads = P("pts", None), P(), P(None, "head"), P("head")
    down = P("head", None)
    placed = (row, row, none, cols, none, heads, none, none, none, down, none, cols, down)
    given = (row, row, cols, none, heads, none, none, none, down, cols, down, none, none)
    return jax.shard_map(
        functools.partial(local, mesh.shape["pts"]),
        mesh=mesh,
        in_specs=placed,
        out_specs=given,
        check_vma=False,
    )
```

```python
import functools
import jax
import jax.numpy as jnp
from jax import lax
from jax.experimental import pallas as pl
from jax.experimental.pallas import tpu as pltpu
from jax.sharding import PartitionSpec as P

HEAD_DIM = 32
SLICES = 64
C = 256
HEADS = 8
BLOCKS = 4
GH = HEADS // BLOCKS
HM = HEADS * SLICES
C0 = 0.7978845608028654
C1 = 0.7978845608028654 * 0.044715
BF = jnp.bfloat16
F32 = jnp.float32
VMEM_LIMIT = 56 * 1024 * 1024


def dot(a, b, precision=None):
    return lax.dot_general(
        a, b, (((1,), (0,)), ((), ())), preferred_element_type=F32, precision=precision
    )


def dot_nt(a, b, precision=None):
    return lax.dot_general(
        a, b, (((1,), (1,)), ((), ())), preferred_element_type=F32, precision=precision
    )


def norm_parts(value):
    centred = value - jnp.mean(value, -1, keepdims=True)
    scale = lax.rsqrt(jnp.mean(centred * centred, -1, keepdims=True) + 1e-05)
    return centred * scale, scale


def norm_back_rows(grad, normed, scale, gain):
    scaled = grad * gain
    return scale * (
        scaled
        - jnp.mean(scaled, -1, keepdims=True)
        - normed * jnp.mean(scaled * normed, -1, keepdims=True)
    )


def sharp_row(block, which, width):
    row = block[which : which + 1, :].astype(F32)
    return jnp.concatenate([row] * (width // C), axis=1)


def softmax_slices(raw, sharp):
    logits = raw * sharp
    grown = jnp.exp(logits - jnp.max(logits, 0, keepdims=True))
    return grown * (1.0 / jnp.sum(grown, 0, keepdims=True))


def fold_rows(value):
    return jnp.sum(value.reshape(value.shape[0] // 8, 8, value.shape[1]), 0)


def prep_kernel(w_up, w_down, w_in, w_out, sharp, slice_weight, pack, slices_t, slices, s_scr):
    pack[0:256, :] = w_up[...].T
    pack[256:512, :] = w_down[...]
    pack[512:576, :] = w_in[...]
    pack[576:640, :] = w_out[...]
    row = lax.broadcasted_iota(jnp.int32, (16, C), 0)
    pack[640:656, :] = jnp.where(row == 0, sharp[0], jnp.where(row == 1, sharp[1], 0.0)).astype(BF)
    s_scr[...] = jnp.zeros_like(s_scr)
    weight = slice_weight[...].astype(F32)
    twice = jnp.concatenate([weight, weight], 1)
    lane = lax.broadcasted_iota(jnp.int32, (HEAD_DIM, 128), 1)
    for k in range(BLOCKS):
        at = slice(k * 128, (k + 1) * 128)
        s_scr[k * 64 : k * 64 + 32, at] = jnp.where(lane < SLICES, twice, 0.0)
        s_scr[k * 64 + 32 : k * 64 + 64, at] = jnp.where(lane < SLICES, 0.0, twice)
    slices[...] = s_scr[...].astype(BF)
    slices_t[...] = s_scr[...].T.astype(BF)


def fill_kernel(z, first, second, before, out):
    @pl.when(pl.program_id(0) == 0)
    def _():
        out[...] = first[...].astype(F32)

    @pl.when(pl.program_id(0) == 1)
    def _():
        out[...] = second[...].astype(F32)


def finish_kernel(z, first, second, before, t0, t1, t2, t3, w0, w1, *refs):
    out, gin, gslice, gsharp, gq, gk, gv, gout, gup, gdown, g1, g2 = refs
    fill_kernel(z, first, second, before, out)

    @pl.when((pl.program_id(0) == 0) & (pl.program_id(1) == 0))
    def _():
        a, b, c, d = (t[...].astype(F32) for t in (t0, t1, t2, t3))
        tail = (a + c) + (b + d)
        gin[...] = tail[0:64]
        gslice[...] = tail[64:96, 0:64] + tail[64:96, 64:128]
        gq[...] = tail[64:96, 128:160]
        gk[...] = tail[64:96, 160:192]
        gv[...] = tail[64:96, 192:224]
        gsharp[...] = jnp.concatenate(
            [
                jnp.sum(tail[96:97, 0:128], 1, keepdims=True),
                jnp.sum(tail[96:97, 128:256], 1, keepdims=True),
            ],
            1,
        )
        g1[...] = tail[97:98]
        g2[...] = tail[98:99]
        gout[...] = tail[104:168]

        @pl.when(z[1] == 0)
        def _():
            gdown[...] = w0[...].T
            gup[...] = w1[...]

        @pl.when(z[1] == 1)
        def _():
            gdown[...] = w1[...].T
            gup[...] = w0[...]


def own_sums_kernel(pts, gain, w_in, spread_slices, sharp, out, acc, den):
    step = pl.program_id(0)

    @pl.when(step == 0)
    def _():
        acc[...] = jnp.zeros_like(acc)
        den[...] = jnp.zeros_like(den)

    normed, _ = norm_parts(pts[...].astype(F32))
    normed_in = (normed * gain[...].astype(F32)).astype(BF)
    middle = dot_nt(normed_in, w_in[...]).astype(BF)
    raw = dot_nt(spread_slices[:, 0:64], middle)
    rows = raw.shape[1]
    sharps = sharp[...]
    parts = [
        softmax_slices(raw[h * SLICES : (h + 1) * SLICES], sharp_row(sharps, h, rows))
        for h in range(GH)
    ]
    weights = jnp.concatenate(parts, 0)
    total = weights[:, 0:128]
    for j in range(1, rows // 128):
        total = total + weights[:, j * 128 : (j + 1) * 128]
    den[...] += total
    acc[...] += dot(weights.astype(BF), middle)

    @pl.when(step == pl.num_programs(0) - 1)
    def _():
        flipped = acc[...].T
        lane = lax.broadcasted_iota(jnp.int32, (HEAD_DIM, 128), 1)
        out[0:HEAD_DIM, :] = jnp.where(lane < SLICES, flipped[:HEAD_DIM], flipped[HEAD_DIM:])
        row = jnp.sum(den[...].T, 0, keepdims=True)
        out[HEAD_DIM : HEAD_DIM + 8, :] = jnp.broadcast_to(row, (8, 128))


def weights_kernel(z, pts, gain, in0, in1, in2, in3, spread_slices, s0, s1, s2, s3, *rest):
    wt, mid, w_in = rest[-3:]

    @pl.when(pl.program_id(0) == 0)
    def _():
        for k, ref in enumerate((in0, in1, in2, in3)):
            w_in[k * 64 : (k + 1) * 64, :] = ref[...]

    normed, _ = norm_parts(pts[...].astype(F32))
    normed_in = (normed * gain[...].astype(F32)).astype(BF)
    middle = dot_nt(normed_in, w_in[...]).astype(BF)
    mid[...] = middle
    raw = dot_nt(spread_slices[...], middle)
    rows = raw.shape[1]
    for h in range(HEADS):
        sharp = sharp_row((s0, s1, s2, s3)[h // GH][...], h % GH, rows)
        wt[h * SLICES : (h + 1) * SLICES, :] = softmax_slices(
            raw[h * SLICES : (h + 1) * SLICES], sharp
        ).astype(BF)


def place_tokens(flat, tokens):
    flat[...] = jnp.zeros_like(flat)
    lane = lax.broadcasted_iota(jnp.int32, (HEAD_DIM, 128), 1)
    for k, ref in enumerate(tokens):
        t = ref[0:HEAD_DIM, :]
        flat[k * 64 : k * 64 + 32, k * 128 : (k + 1) * 128] = jnp.where(lane < SLICES, t, 0.0)
        flat[k * 64 + 32 : k * 64 + 64, k * 128 : (k + 1) * 128] = jnp.where(
            lane < SLICES, 0.0, t
        )


def own_block(flipped, k):
    lane = lax.broadcasted_iota(jnp.int32, (HEAD_DIM, 128), 1)
    block = flipped[k * 64 : (k + 1) * 64, k * 128 : (k + 1) * 128]
    return jnp.where(lane < SLICES, block[:HEAD_DIM], block[HEAD_DIM:])


def mlp_kernel(with_sums, steps, z, pts, cot, wt, *refs):
    tokens, refs = refs[:4], refs[4:]
    gain, refs = refs[0], refs[1:]
    ups, downs, outs, refs = refs[:4], refs[4:8], refs[8:12], refs[12:]
    if with_sums:
        mixed, gres, gspread, send1, send3, gt0, gt1, gt2, gt3, wg0, wg2, gout, g2 = refs[:13]
        flat, tok_t, w_out, acc_tok, acc_w = refs[13:]
    else:
        mixed, gres, gspread, flat, tok_t, w_out = refs[1:]
    step = pl.program_id(0)

    @pl.when(step == 0)
    def _():
        place_tokens(flat, tokens)
        tok_t[...] = flat[...].astype(BF)
        for k, ref in enumerate(outs):
            w_out[k * 64 : (k + 1) * 64, :] = ref[...]
        if with_sums:
            acc_tok[...] = jnp.zeros_like(acc_tok)
            acc_w[...] = jnp.zeros_like(acc_w)
            gout[...] = jnp.zeros_like(gout)
            g2[...] = jnp.zeros_like(g2)

    def rows_step():
        weights = wt[...]
        spread_t = dot(tok_t[...], weights).astype(BF)
        spread = spread_t.T
        resid = pts[...].astype(F32) + dot(spread, w_out[...])
        normed, scale = norm_parts(resid)
        gain_row = gain[...].astype(F32)
        normed_mid = (normed * gain_row).astype(BF)
        cotangent = cot[...]
        total = resid
        gmid = None
        if with_sums:
            cot_t = cotangent.T
            normed_t = normed_mid.T
        for k in range(BLOCKS):
            up, down = ups[k][...], downs[k][...]
            hidden = dot_nt(normed_mid, up)
            square = hidden * hidden
            inner = jnp.tanh(hidden * (C0 + C1 * square))
            half = 0.5 + 0.5 * inner
            gelu = hidden * half
            active = gelu.astype(BF)
            total = total + dot(active, down)
            slope = half + gelu * (1.0 - half) * (2.0 * C0 + 6.0 * C1 * square)
            ghid = (dot_nt(cotangent, down) * slope).astype(BF)
            part = dot(ghid, up)
            gmid = part if gmid is None else gmid + part
            if with_sums:
                acc_w[k, 0:C, :] += dot(cot_t, active)
                acc_w[k, C : 2 * C, :] += dot(normed_t, ghid)
        mixed[...] = total
        grad = cotangent.astype(F32) + norm_back_rows(gmid, normed, scale, gain_row)
        low = grad.astype(BF)
        gres[...] = low
        gsp = dot_nt(low, w_out[...]).astype(BF)
        gspread[...] = gsp
        if with_sums:
            send1[...] = total.astype(BF)
            send3[...] = total.astype(BF)
            acc_tok[...] += dot(weights, gsp)
            gout[...] += dot(spread_t, low)
            g2[...] += fold_rows(gmid * normed)

    if not with_sums:
        rows_step()
        return
    pl.when(step < steps)(rows_step)

    @pl.when(step == steps)
    def _():
        flipped = acc_tok[...].T
        for k, ref in enumerate((gt0, gt1, gt2, gt3)):
            ref[...] = own_block(flipped, k)
        wg0[...] = acc_w[0]
        wg2[...] = acc_w[2].astype(BF)
        send1[...] = acc_w[1].astype(BF)
        send3[...] = acc_w[3].astype(BF)


def points_kernel(with_sums, z, pts, wt, mid, gspread, gres, *refs):
    tokens, gnums, refs = refs[:4], refs[4:8], refs[8:]
    gain, slices_t, slices, refs = refs[0], refs[1], refs[2], refs[3:]
    ins, sharps, refs = refs[:4], refs[4:8], refs[8:]
    if with_sums:
        qkv, g2, gout, gpts, low_gpts, o0, o1, o2, o3 = refs[:9]
        flat, tok, gn_t, gn, gden, w_in, acc_in, acc_s, acc_g, acc_h = refs[9:]
    else:
        gpts, flat, tok, gn_t, gn, gden, w_in = refs[1:]
    step = pl.program_id(0)

    @pl.when(step == 0)
    def _():
        place_tokens(flat, tokens)
        tok[...] = flat[...].T.astype(BF)
        place_tokens(flat, gnums)
        gn_t[...] = flat[...].astype(BF)
        gn[...] = flat[...].T.astype(BF)
        for k, ref in enumerate(gnums):
            row = ref[HEAD_DIM : HEAD_DIM + 1, :]
            gden[k * 128 : (k + 1) * 128, :] = jnp.broadcast_to(row, (128, 128)).T
        for k, ref in enumerate(ins):
            w_in[k * 64 : (k + 1) * 64, :] = ref[...]
        if with_sums:
            acc_in[...] = jnp.zeros_like(acc_in)
            acc_s[...] = jnp.zeros_like(acc_s)
            acc_g[...] = jnp.zeros_like(acc_g)
            acc_h[...] = jnp.zeros_like(acc_h)

    normed, scale = norm_parts(pts[...].astype(F32))
    gain_row = gain[...].astype(F32)
    weights = wt[...]
    middle = mid[...]
    rows = weights.shape[1]
    gw = dot_nt(tok[...], gspread[...]) + dot_nt(gn[...], middle)
    pieces, sharp_sums = [], []
    if with_sums:
        raw = dot_nt(slices_t[...], middle)
    for h in range(HEADS):
        at = slice(h * SLICES, (h + 1) * SLICES)
        sharp = sharp_row(sharps[h // GH][...], h % GH, rows)
        w = softmax_slices(raw[at], sharp) if with_sums else weights[at].astype(F32)
        g = gw[at] + jnp.concatenate([gden[at, :]] * (rows // 128), axis=1)
        gl = w * (g - jnp.sum(w * g, 0, keepdims=True))
        pieces.append((gl * sharp).astype(BF))
        if with_sums:
            sharp_sums.append(jnp.sum(gl * raw[at], 0, keepdims=True))
    graw = jnp.concatenate(pieces, 0)
    gmid_t = (dot(gn_t[...], weights) + dot(slices[...], graw)).astype(BF)
    gmid = gmid_t.T
    gnormed = dot(gmid, w_in[...])
    result = gres[...].astype(F32) + norm_back_rows(gnormed, normed, scale, gain_row)
    gpts[...] = result
    if with_sums:
        low_gpts[...] = result.astype(BF)
        normed_in = (normed * gain_row).astype(BF)
        acc_in[...] += dot(gmid_t, normed_in)
        acc_s[...] += dot(graw, middle)
        acc_g[...] += fold_rows(gnormed * normed)
        acc_h[...] += jnp.concatenate(sharp_sums, 0)

        @pl.when(step == pl.num_programs(0) - 1)
        def _():
            flipped = acc_s[...].T
            gsharp = acc_h[:, 0:128]
            for j in range(1, rows // 128):
                gsharp = gsharp + acc_h[:, j * 128 : (j + 1) * 128]
            gslice = jnp.zeros((HEAD_DIM, 128), F32)
            for k in range(BLOCKS):
                gslice = gslice + own_block(flipped, k)
            gain1 = jnp.sum(acc_g[...], 0, keepdims=True)
            gain2 = jnp.sum(g2[...], 0, keepdims=True)
            for k, ref in enumerate((o0, o1, o2, o3)):
                ref[0:64, :] = acc_in[k * 64 : (k + 1) * 64, :].astype(ref.dtype)
                ref[64:96, 0:128] = gslice.astype(ref.dtype)
                ref[64:96, 128:256] = qkv[...].astype(ref.dtype)
                wide = jnp.concatenate([gsharp[2 * k : 2 * k + 1], gsharp[2 * k + 1 : 2 * k + 2]], 1)
                ref[96:104, :] = jnp.concatenate(
                    [wide, gain1, gain2, jnp.zeros((5, C), F32)], 0
                ).astype(ref.dtype)
                ref[104:168, :] = gout[k * 64 : (k + 1) * 64, :].astype(ref.dtype)


HIGH = lax.Precision.HIGHEST


def token_parts(nd, wq, wk, wv):
    padded = jnp.concatenate([nd, jnp.zeros((88, 128), F32)], 0).T
    denom = padded[:, HEAD_DIM : HEAD_DIM + 1]
    tok = padded[:, :HEAD_DIM] / denom
    q, k, v = dot(tok, wq, HIGH), dot(tok, wk, HIGH), dot(tok, wv, HIGH)
    scores = dot_nt(q, k, HIGH) * (1.0 / HEAD_DIM**0.5)
    row = lax.broadcasted_iota(jnp.int32, (128, 128), 0) < SLICES
    col = lax.broadcasted_iota(jnp.int32, (128, 128), 1) < SLICES
    same = row == col
    scores = jnp.where(same, scores, -jnp.inf)
    p = jnp.exp(scores - jnp.max(scores, -1, keepdims=True))
    p = p / jnp.sum(p, -1, keepdims=True)
    return denom, tok, q, k, v, p


def flip(value):
    n = value.shape[1]
    return jnp.concatenate([value, jnp.zeros((128, 128 - n), F32)], 1).T[:n]


def tokens_kernel(a, b, c, d, wq, wk, wv, total, tokens):
    nd = (a[...] + c[...]) + (b[...] + d[...])
    total[...] = nd
    _, _, _, _, v, p = token_parts(nd, *(w[...].astype(F32) for w in (wq, wk, wv)))
    mixed = dot(p, v, HIGH).astype(BF).astype(F32)
    tokens[...] = flip(mixed)


def tokens_back_kernel(scale, nd, a, b, c, d, wq, wk, wv, gn, qkv):
    gt = (a[...] + c[...]) + (b[...] + d[...])
    g = jnp.concatenate([gt, jnp.zeros((96, 128), F32)], 0).T[:, :HEAD_DIM]
    wq, wk, wv = (w[...].astype(F32) for w in (wq, wk, wv))
    denom, tok, q, k, v, p = token_parts(nd[...], wq, wk, wv)
    dv = dot(p.T, g, HIGH)
    dp = dot_nt(g, v, HIGH)
    ds = p * (dp - jnp.sum(p * dp, -1, keepdims=True)) * (1.0 / HEAD_DIM**0.5)
    dq = dot(ds, k, HIGH)
    dk = dot(ds.T, q, HIGH)
    gmt = dot_nt(dq, wq, HIGH) + dot_nt(dk, wk, HIGH) + dot_nt(dv, wv, HIGH)
    gnum = (gmt / denom).astype(BF).astype(F32)
    gden = -jnp.sum(gmt * tok, -1, keepdims=True) / denom
    gn[0:HEAD_DIM, :] = flip(gnum)
    gn[HEAD_DIM : HEAD_DIM + 8, :] = flip(jnp.broadcast_to(gden, (128, 8)))
    tok_t = flip(tok)
    qkv[...] = scale * jnp.concatenate(
        [dot(tok_t, dq, HIGH), dot(tok_t, dk, HIGH), dot(tok_t, dv, HIGH), jnp.zeros((32, 32), F32)],
        1,
    )


def full(shape):
    return pl.BlockSpec(shape, lambda *_: (0,) * len(shape))


def part(shape, row):
    return pl.BlockSpec(shape, lambda *_: (row, 0))


def shape_of(shape, dtype):
    return jax.ShapeDtypeStruct(shape, dtype)


def cost(us):
    return pl.CostEstimate(flops=int(us * 1.0e6), bytes_accessed=1024, transcendentals=0)


UP, DOWN, WIN, WOUT, SHARP = (256, 0), (256, 1), (64, 8), (64, 9), (16, 40)
WIDE, NARROW = 1024, 512
TAIL = 168


def pack_specs(kind):
    return [part((kind[0], C), kind[1])] * BLOCKS


def local(
    pts_size,
    points,
    cotangent,
    gain_one,
    w_in,
    slice_weight,
    sharp,
    w_query,
    w_key,
    w_value,
    w_out,
    gain_two,
    w_up,
    w_down,
):
    axes = ("pts", "head")
    rows = points.shape[0]
    quarter = rows // BLOCKS

    def pull(value, dx=0, dy=0, dc=0, dz=0):
        pairs = []
        for p in range(pts_size):
            x, y, c = p // 8, (p // 2) % 4, p % 2
            there = p
            if pts_size > 1:
                there = (((x + dx) % 4) * 4 + (y + dy) % 4) * 2 + (c + dc) % 2
            for z in range(BLOCKS):
                pairs.append((there * BLOCKS + (z + dz) % BLOCKS, p * BLOCKS + z))
        return lax.ppermute(value, axes, pairs)

    def pulls(value, axis):
        return [pull(value, **{axis: k}) for k in (1, 2, 3)]

    def tie(*values):
        return lax.optimization_barrier(values)

    def add4(a, r):
        return (a + r[1].astype(F32)) + (r[0].astype(F32) + r[2].astype(F32))

    def core_sum(value):
        return value + pull(value, dc=1) if pts_size > 1 else value

    def rounded(value):
        return lax.reduce_precision(value, 8, 7)

    def axis_peers(value, axis):
        if pts_size == 1:
            return [jnp.zeros_like(value)] * 3
        return pulls(value, axis)

    core = lax.axis_index("pts").astype(jnp.int32) % 2
    z = jnp.stack([lax.axis_index("head").astype(jnp.int32), core])

    def row_spec(size, away, first=0):
        n = quarter // size
        return pl.BlockSpec(
            (size, C), lambda i, z: (lax.rem(z[0] + away, BLOCKS) * n + first // size + i, 0)
        )

    def own_spec(size, first=0):
        return pl.BlockSpec((size, C), lambda i, z: (first // size + i, 0))

    def own_cols(size, first=0):
        return pl.BlockSpec((HM, size), lambda i, z: (0, first // size + i))

    def grid(steps, in_specs, out_specs, scratch=()):
        return pltpu.PrefetchScalarGridSpec(
            num_scalar_prefetch=1,
            grid=steps,
            in_specs=in_specs,
            out_specs=out_specs,
            scratch_shapes=scratch,
        )

    any_spec = pl.BlockSpec(memory_space=pl.ANY)
    params = pltpu.CompilerParams(vmem_limit_bytes=VMEM_LIMIT)

    gain1, gain2 = gain_one.reshape(1, C), gain_two.reshape(1, C)
    wq, wk, wv = w_query, w_key, w_value
    pack, slices_t, slices = pl.pallas_call(
        prep_kernel,
        out_shape=[shape_of((656, C), BF), shape_of((HM, C), BF), shape_of((C, HM), BF)],
        in_specs=[pl.BlockSpec(memory_space=pltpu.VMEM)] * 4
        + [pl.BlockSpec(memory_space=pltpu.SMEM), pl.BlockSpec(memory_space=pltpu.VMEM)],
        scratch_shapes=[pltpu.VMEM((C, HM), F32)],
        compiler_params=params,
        cost_estimate=cost(2),
        name="prep",
    )(w_up, w_down, w_in.T, w_out, sharp.astype(F32), slice_weight)
    packs = [pack] + pulls(pack, "dz")

    nd = pl.pallas_call(
        own_sums_kernel,
        grid=(rows // WIDE,),
        in_specs=[
            pl.BlockSpec((WIDE, C), lambda i: (i, 0)),
            full((1, C)),
            part((64, C), WIN[1]),
            part((128, C), 0),
            part((16, C), SHARP[1]),
        ],
        out_specs=full((40, 128)),
        out_shape=shape_of((40, 128), F32),
        scratch_shapes=[pltpu.VMEM((128, 64), F32), pltpu.VMEM((128, 128), F32)],
        compiler_params=params,
        cost_estimate=cost(8),
        name="own_sums",
    )(points, gain1, pack, slices_t, pack)

    half = quarter // 2

    def weights_call(away, first, before):
        kept = [] if before is None else list(before)
        return pl.pallas_call(
            weights_kernel,
            grid_spec=grid(
                (half // NARROW,),
                [row_spec(NARROW, away, first), full((1, C))]
                + pack_specs(WIN)
                + [full((HM, C))]
                + pack_specs(SHARP)
                + [any_spec] * len(kept),
                [own_cols(NARROW, first), own_spec(NARROW, first)],
                [pltpu.VMEM((C, C), BF)],
            ),
            out_shape=[shape_of((HM, quarter), BF), shape_of((quarter, C), BF)],
            input_output_aliases={12: 0, 13: 1} if kept else {},
            compiler_params=params,
            cost_estimate=cost(3),
            name="weights",
        )(z, points, gain1, *packs, slices_t, *packs, *kept)

    def mlp_call(away, first, count, size, tokens, wt, before):
        with_sums = before is None
        steps = count // size
        scratch = [pltpu.VMEM((C, HM), F32), pltpu.VMEM((C, HM), BF), pltpu.VMEM((C, C), BF)]
        out_shape = [shape_of((rows, C), F32), shape_of((count, C), BF), shape_of((count, C), BF)]
        kept = [] if with_sums else [before]

        def last(i):
            return jnp.minimum(i, steps - 1) if with_sums else i

        def at(i, z):
            n = quarter // size
            return (lax.rem(z[0] + away, BLOCKS) * n + first // size + last(i), 0)

        rest = pl.BlockSpec((size, C), at)
        here = pl.BlockSpec((size, C), lambda i, z: (last(i), 0))
        cols = pl.BlockSpec((HM, size), lambda i, z: (0, first // size + last(i)))
        out_specs = [rest, here, here]
        if with_sums:
            scratch += [pltpu.VMEM((HM, C), F32), pltpu.VMEM((BLOCKS, 2 * C, C), F32)]
            out_shape += [shape_of((count + 2 * C, C), BF)] * 2
            out_shape += [shape_of((HEAD_DIM, 128), F32)] * 4
            out_shape += [shape_of((2 * C, C), F32), shape_of((2 * C, C), BF)]
            out_shape += [shape_of((C, C), F32), shape_of((8, C), F32)]
            out_specs += [own_spec(size)] * 2
            out_specs += [full((HEAD_DIM, 128))] * 4 + [full((2 * C, C))] * 2
            out_specs += [full((C, C)), full((8, C))]
        return pl.pallas_call(
            functools.partial(mlp_kernel, with_sums, steps),
            grid_spec=grid(
                (steps + 1 if with_sums else steps,),
                [rest, rest, cols]
                + [full((HEAD_DIM, 128))] * 4
                + [full((1, C))]
                + pack_specs(UP)
                + pack_specs(DOWN)
                + pack_specs(WOUT)
                + [any_spec] * len(kept),
                out_specs,
                scratch,
            ),
            out_shape=out_shape,
            input_output_aliases={21: 0} if kept else {},
            compiler_params=params,
            cost_estimate=cost(count / 150),
            name="mlp",
        )(z, points, cotangent, wt, *tokens, gain2, *packs, *packs, *packs, *kept)

    def points_call(away, first, count, size, tokens, gnums, state, sums, before):
        wt, mid, gspread, gres = state
        scratch = [
            pltpu.VMEM((C, HM), F32),
            pltpu.VMEM((HM, C), BF),
            pltpu.VMEM((C, HM), BF),
            pltpu.VMEM((HM, C), BF),
            pltpu.VMEM((HM, 128), F32),
            pltpu.VMEM((C, C), BF),
        ]
        out_shape = [shape_of((rows, C), F32)]
        out_specs = [row_spec(size, away, first)]
        extra, extra_specs = [before], [any_spec]
        if sums:
            scratch += [
                pltpu.VMEM((C, C), F32),
                pltpu.VMEM((HM, C), F32),
                pltpu.VMEM((8, C), F32),
                pltpu.VMEM((HEADS, size), F32),
            ]
            out_shape += [shape_of((count, C), BF), shape_of((TAIL, C), F32)]
            out_shape += [shape_of((TAIL, C), BF)] * 3
            out_specs += [own_spec(size)] + [full((TAIL, C))] * 4
            extra = list(sums)
            extra_specs = [full((HEAD_DIM, 128)), full((8, C)), full((C, C))]
        return pl.pallas_call(
            functools.partial(points_kernel, bool(sums)),
            grid_spec=grid(
                (count // size,),
                [row_spec(size, away, first), own_cols(size, first), own_spec(size, first)]
                + [own_spec(size)] * 2
                + [full((HEAD_DIM, 128))] * 4
                + [full((40, 128))] * 4
                + [full((1, C)), full((HM, C)), full((C, HM))]
                + pack_specs(WIN)
                + pack_specs(SHARP)
                + extra_specs,
                out_specs,
                scratch,
            ),
            out_shape=out_shape,
            input_output_aliases={} if sums else {25: 0},
            compiler_params=params,
            cost_estimate=cost(count / 200),
            name="points",
        )(
            z, points, wt, mid, gspread, gres, *tokens, *gnums, gain1, slices_t, slices,
            *packs, *packs, *extra
        )

    steps = quarter // WIDE
    fill_specs = [
        pl.BlockSpec((WIDE, C), lambda q, i, z: (jnp.where(q == 0, i, steps - 1), 0)),
        pl.BlockSpec((WIDE, C), lambda q, i, z: (jnp.where(q == 0, 0, i), 0)),
        any_spec,
    ]
    fill_out = pl.BlockSpec(
        (WIDE, C), lambda q, i, z: (lax.rem(z[0] + 1 + 2 * q, BLOCKS) * steps + i, 0)
    )

    nd = core_sum(nd)
    got = axis_peers(nd, "dx")
    nd, packs[0] = tie(nd, packs[0])
    mine = weights_call(0, 0, None)
    got, mine = tie(got, mine)
    nd = add4(nd, got)
    got = axis_peers(nd, "dy")
    nd, mine = tie(nd, mine)
    mine = weights_call(0, half, mine)
    got, mine = tie(got, mine)
    nd, own_tokens = pl.pallas_call(
        tokens_kernel,
        out_shape=[shape_of((40, 128), F32), shape_of((HEAD_DIM, 128), F32)],
        compiler_params=params,
        cost_estimate=cost(3),
        name="tokens",
    )(nd, *got, wq, wk, wv)
    got = pulls(own_tokens, "dz")
    own_tokens, packs[0] = tie(own_tokens, packs[0])
    opposite = weights_call(2, 0, None)
    got, opposite = tie(got, opposite)
    tokens = [own_tokens] + list(got)

    result = mlp_call(0, 0, quarter, NARROW, tokens, mine[0], None)
    mixed, gres, gspread, send1, send3 = result[:5]
    gts, (wg0, wg2, gout, g2) = result[5:9], result[9:]

    got = [pull(gts[BLOCKS - k], dz=k) for k in (1, 2, 3)]
    wg2 = pull(wg2, dz=2)
    gts, opposite = tie(gts, opposite)
    opposite = weights_call(2, half, opposite)
    got, opposite, wg2 = tie(got, opposite, wg2)
    gt = core_sum(add4(gts[0], got))
    got = axis_peers(gt, "dx")
    gt, send1, send3, mixed = tie(gt, send1, send3, mixed)
    near = [pull(send3, dz=1), pull(send1, dz=3)]
    mixed, gres_a, gspread_a = mlp_call(2, 0, half, NARROW, tokens, opposite[0], mixed)
    got, mixed = tie(got, mixed)
    gt = add4(gt, got)
    got = axis_peers(gt, "dy")
    gt, mixed = tie(gt, mixed)
    mixed, gres_b, gspread_b = mlp_call(2, half, half, NARROW, tokens, opposite[0], mixed)
    got, mixed = tie(got, mixed)
    own_gn, qkv = pl.pallas_call(
        functools.partial(tokens_back_kernel, 1.0 / pts_size),
        out_shape=[shape_of((40, 128), F32), shape_of((HEAD_DIM, 128), F32)],
        compiler_params=params,
        cost_estimate=cost(4),
        name="tokens_back",
    )(nd, gt, *got, wq, wk, wv)
    got = pulls(own_gn, "dz")
    own_gn, near = tie(own_gn, near)
    wsum = (wg0 + wg2.astype(F32)) + (
        near[0][quarter:].astype(F32) + near[1][quarter:].astype(F32)
    )
    wlow = wsum.astype(BF)
    if pts_size > 1:
        wsum = rounded(wsum) + pull(wlow, dc=1).astype(F32)
        wlow = lax.dynamic_slice_in_dim(wsum, core * C, C, 0).astype(BF)
    got, wlow = tie(got, wlow)
    wgot = axis_peers(wlow[:C], "dx")
    gnums = [own_gn] + list(got)

    state = (mine[0], mine[1], gspread, gres)
    result = points_call(0, 0, quarter, NARROW, tokens, gnums, state, (qkv, g2, gout), None)
    gpts, send, outs = result[0], result[1], result[2:]
    gpts, outs, send, wgot = tie(gpts, outs, send, wgot)

    got = [pull(outs[BLOCKS - k], dz=k) for k in (1, 2, 3)]
    far = [pull(send, dz=1), pull(send, dz=3)]
    state = (opposite[0], opposite[1], gspread_a, gres_a)
    (gpts,) = points_call(2, 0, half, NARROW, tokens, gnums, state, (), gpts)
    got, gpts = tie(got, gpts)
    tail = core_sum(add4(outs[0], got))
    both = jnp.concatenate([tail, add4(wlow[:C].astype(F32), wgot)], 0).astype(BF)
    got = axis_peers(both, "dy")
    gpts, both = tie(gpts, both)
    state = (opposite[0], opposite[1], gspread_b, gres_b)
    (gpts,) = points_call(2, half, half, NARROW, tokens, gnums, state, (), gpts)
    got, gpts = tie(got, gpts)
    both = add4(both.astype(F32), got)
    tail, wsum = both[:TAIL].astype(BF), both[TAIL:]
    if pts_size > 1:
        other = pull(wsum, dc=1)
    else:
        other = wlow[C:].astype(F32)
    wsum, other, tail = tie(wsum, other, tail)
    got = axis_peers(tail, "dx")
    tail, mixed, far = tie(tail, mixed, far)
    mixed = pl.pallas_call(
        fill_kernel,
        grid_spec=grid((2, steps), fill_specs, fill_out),
        out_shape=shape_of((rows, C), F32),
        input_output_aliases={3: 0},
        compiler_params=params,
        cost_estimate=cost(4),
        name="fill",
    )(z, *near, mixed)
    got, mixed = tie(got, mixed)
    shapes = [(64, C), (32, 64), (1, GH), (32, 32), (32, 32), (32, 32)]
    shapes += [(64, C), (C, C), (C, C), (1, C), (1, C)]
    result = pl.pallas_call(
        finish_kernel,
        grid_spec=grid(
            (2, steps),
            fill_specs + [full((TAIL, C))] * 4 + [full((C, C))] * 2,
            [fill_out] + [full(s) for s in shapes],
        ),
        out_shape=[shape_of((rows, C), F32)] + [shape_of(s, F32) for s in shapes],
        input_output_aliases={3: 0},
        compiler_params=params,
        cost_estimate=cost(4),
        name="finish",
    )(z, *far, gpts, tail, *got, wsum, other)
    gpts, gin, gslice, gsharp, gq, gk, gv, gout, gup, gdown, g1, g2 = result
    return (
        mixed, gpts, gin.T, gslice, gsharp.reshape(GH), gq, gk, gv, gout, gup, gdown,
        g1.reshape(C), g2.reshape(C),
    )


def solution(mesh):
    row, none, cols, heads = P("pts", None), P(), P(None, "head"), P("head")
    down = P("head", None)
    placed = (row, row, none, cols, none, heads, none, none, none, down, none, cols, down)
    given = (row, row, cols, none, heads, none, none, none, down, cols, down, none, none)
    return jax.shard_map(
        functools.partial(local, mesh.shape["pts"]),
        mesh=mesh,
        in_specs=placed,
        out_specs=given,
        check_vma=False,
    )
```

```python
import functools
import jax
import jax.numpy as jnp
from jax import lax
from jax.experimental import pallas as pl
from jax.experimental.pallas import tpu as pltpu
from jax.sharding import PartitionSpec as P

HEAD_DIM = 32
SLICES = 64
C = 256
HEADS = 8
BLOCKS = 4
GH = HEADS // BLOCKS
HM = HEADS * SLICES
C0 = 0.7978845608028654
C1 = 0.7978845608028654 * 0.044715
BF = jnp.bfloat16
F32 = jnp.float32
VMEM_LIMIT = 56 * 1024 * 1024


def dot(a, b, precision=None):
    return lax.dot_general(
        a, b, (((1,), (0,)), ((), ())), preferred_element_type=F32, precision=precision
    )


def dot_nt(a, b, precision=None):
    return lax.dot_general(
        a, b, (((1,), (1,)), ((), ())), preferred_element_type=F32, precision=precision
    )


def norm_parts(value):
    centred = value - jnp.mean(value, -1, keepdims=True)
    scale = lax.rsqrt(jnp.mean(centred * centred, -1, keepdims=True) + 1e-05)
    return centred * scale, scale


def norm_back_rows(grad, normed, scale, gain):
    scaled = grad * gain
    return scale * (
        scaled
        - jnp.mean(scaled, -1, keepdims=True)
        - normed * jnp.mean(scaled * normed, -1, keepdims=True)
    )


def sharp_row(block, which, width):
    row = block[which : which + 1, :].astype(F32)
    return jnp.concatenate([row] * (width // C), axis=1)


def softmax_slices(raw, sharp):
    logits = raw * sharp
    grown = jnp.exp(logits - jnp.max(logits, 0, keepdims=True))
    return grown * (1.0 / jnp.sum(grown, 0, keepdims=True))


def fold_rows(value):
    return jnp.sum(value.reshape(value.shape[0] // 8, 8, value.shape[1]), 0)


def prep_kernel(
    w_up, w_down, w_in, w_out, sharp, slice_weight, one, two, pack, slices_t, slices, gain1, gain2, s_scr
):
    gain1[...] = one[...].astype(F32).reshape(1, C)
    gain2[...] = two[...].astype(F32).reshape(1, C)
    pack[0:256, :] = w_up[...].T
    pack[256:512, :] = w_down[...]
    pack[512:576, :] = w_in[...]
    pack[576:640, :] = w_out[...]
    row = lax.broadcasted_iota(jnp.int32, (16, C), 0)
    pack[640:656, :] = jnp.where(row == 0, sharp[0], jnp.where(row == 1, sharp[1], 0.0)).astype(BF)
    s_scr[...] = jnp.zeros_like(s_scr)
    weight = slice_weight[...].astype(F32)
    twice = jnp.concatenate([weight, weight], 1)
    lane = lax.broadcasted_iota(jnp.int32, (HEAD_DIM, 128), 1)
    for k in range(BLOCKS):
        at = slice(k * 128, (k + 1) * 128)
        s_scr[k * 64 : k * 64 + 32, at] = jnp.where(lane < SLICES, twice, 0.0)
        s_scr[k * 64 + 32 : k * 64 + 64, at] = jnp.where(lane < SLICES, 0.0, twice)
    slices[...] = s_scr[...].astype(BF)
    slices_t[...] = s_scr[...].T.astype(BF)


def fill_kernel(z, *refs):
    out = refs[-1]
    for k, ref in enumerate(refs[:-2]):

        @pl.when(pl.program_id(0) == k)
        def _():
            out[...] = ref[...].astype(F32)


def finish_kernel(z, first, second, before, t0, t1, t2, t3, w0, w1, *refs):
    out, gin, gslice, gsharp, gq, gk, gv, gout, gup, gdown, g1, g2 = refs
    fill_kernel(z, first, second, before, out)

    @pl.when(pl.program_id(0) == 0)
    def _():
        a, b, c, d = (t[...].astype(F32) for t in (t0, t1, t2, t3))
        tail = (a + c) + (b + d)
        gin[...] = tail[0:64]
        gslice[...] = tail[64:96, 0:64] + tail[64:96, 64:128]
        gq[...] = tail[64:96, 128:160]
        gk[...] = tail[64:96, 160:192]
        gv[...] = tail[64:96, 192:224]
        gsharp[...] = jnp.concatenate(
            [
                jnp.sum(tail[96:97, 0:128], 1, keepdims=True),
                jnp.sum(tail[96:97, 128:256], 1, keepdims=True),
            ],
            1,
        )
        g1[...] = tail[97:98]
        g2[...] = tail[98:99]
        gout[...] = tail[104:168]

        @pl.when(z[1] == 0)
        def _():
            gdown[...] = w0[...].T
            gup[...] = w1[...]

        @pl.when(z[1] == 1)
        def _():
            gdown[...] = w1[...].T
            gup[...] = w0[...]


def own_sums_kernel(pts, gain, w_in, spread_slices, sharp, out, acc, den):
    step = pl.program_id(0)

    @pl.when(step == 0)
    def _():
        acc[...] = jnp.zeros_like(acc)
        den[...] = jnp.zeros_like(den)

    normed, _ = norm_parts(pts[...].astype(F32))
    normed_in = (normed * gain[...].astype(F32)).astype(BF)
    middle = dot_nt(normed_in, w_in[...]).astype(BF)
    raw = dot_nt(spread_slices[:, 0:64], middle)
    rows = raw.shape[1]
    sharps = sharp[...]
    parts = [
        softmax_slices(raw[h * SLICES : (h + 1) * SLICES], sharp_row(sharps, h, rows))
        for h in range(GH)
    ]
    weights = jnp.concatenate(parts, 0)
    total = weights[:, 0:128]
    for j in range(1, rows // 128):
        total = total + weights[:, j * 128 : (j + 1) * 128]
    den[...] += total
    acc[...] += dot(weights.astype(BF), middle)

    @pl.when(step == pl.num_programs(0) - 1)
    def _():
        flipped = acc[...].T
        lane = lax.broadcasted_iota(jnp.int32, (HEAD_DIM, 128), 1)
        out[0:HEAD_DIM, :] = jnp.where(lane < SLICES, flipped[:HEAD_DIM], flipped[HEAD_DIM:])
        row = jnp.sum(den[...].T, 0, keepdims=True)
        out[HEAD_DIM : HEAD_DIM + 8, :] = jnp.broadcast_to(row, (8, 128))


def weights_kernel(z, pts, gain, in0, in1, in2, in3, spread_slices, s0, s1, s2, s3, *rest):
    wt, mid, w_in = rest

    @pl.when(pl.program_id(0) == 0)
    def _():
        for k, ref in enumerate((in0, in1, in2, in3)):
            w_in[k * 64 : (k + 1) * 64, :] = ref[...]

    normed, _ = norm_parts(pts[...].astype(F32))
    normed_in = (normed * gain[...].astype(F32)).astype(BF)
    middle = dot_nt(normed_in, w_in[...]).astype(BF)
    mid[...] = middle
    raw = dot_nt(spread_slices[...], middle)
    rows = raw.shape[1]
    for h in range(HEADS):
        sharp = sharp_row((s0, s1, s2, s3)[h // GH][...], h % GH, rows)
        wt[h * SLICES : (h + 1) * SLICES, :] = softmax_slices(
            raw[h * SLICES : (h + 1) * SLICES], sharp
        ).astype(BF)


def place_tokens(flat, tokens):
    flat[...] = jnp.zeros_like(flat)
    lane = lax.broadcasted_iota(jnp.int32, (HEAD_DIM, 128), 1)
    for k, ref in enumerate(tokens):
        t = ref[0:HEAD_DIM, :]
        flat[k * 64 : k * 64 + 32, k * 128 : (k + 1) * 128] = jnp.where(lane < SLICES, t, 0.0)
        flat[k * 64 + 32 : k * 64 + 64, k * 128 : (k + 1) * 128] = jnp.where(
            lane < SLICES, 0.0, t
        )


def own_block(flipped, k):
    lane = lax.broadcasted_iota(jnp.int32, (HEAD_DIM, 128), 1)
    block = flipped[k * 64 : (k + 1) * 64, k * 128 : (k + 1) * 128]
    return jnp.where(lane < SLICES, block[:HEAD_DIM], block[HEAD_DIM:])


def mlp_kernel(z, pts, cot, wt, *refs):
    tokens, refs = refs[:4], refs[4:]
    gain, refs = refs[0], refs[1:]
    ups, downs, outs, refs = refs[:4], refs[4:8], refs[8:12], refs[12:]
    mixed, gres, gspread, low_mixed, gt0, gt1, gt2, gt3, wg0, wg1, wg2, wg3, gout, g2 = refs[:14]
    flat, tok_t, w_out, acc_tok, acc_w = refs[14:]
    step = pl.program_id(0)

    @pl.when(step == 0)
    def _():
        place_tokens(flat, tokens)
        tok_t[...] = flat[...].astype(BF)
        for k, ref in enumerate(outs):
            w_out[k * 64 : (k + 1) * 64, :] = ref[...]
        acc_tok[...] = jnp.zeros_like(acc_tok)
        acc_w[...] = jnp.zeros_like(acc_w)
        gout[...] = jnp.zeros_like(gout)
        g2[...] = jnp.zeros_like(g2)

    weights = wt[...]
    spread_t = dot(tok_t[...], weights).astype(BF)
    spread = spread_t.T
    resid = pts[...].astype(F32) + dot(spread, w_out[...])
    normed, scale = norm_parts(resid)
    gain_row = gain[...].astype(F32)
    normed_mid = (normed * gain_row).astype(BF)
    cotangent = cot[...]
    total = resid
    gmid = None
    cot_t = cotangent.T
    normed_t = normed_mid.T
    for k in range(BLOCKS):
        up, down = ups[k][...], downs[k][...]
        hidden = dot_nt(normed_mid, up)
        square = hidden * hidden
        inner = jnp.tanh(hidden * (C0 + C1 * square))
        half = 0.5 + 0.5 * inner
        gelu = hidden * half
        active = gelu.astype(BF)
        total = total + dot(active, down)
        slope = half + gelu * (1.0 - half) * (2.0 * C0 + 6.0 * C1 * square)
        ghid = (dot_nt(cotangent, down) * slope).astype(BF)
        part = dot(ghid, up)
        gmid = part if gmid is None else gmid + part
        acc_w[k, 0:C, :] += dot(cot_t, active)
        acc_w[k, C : 2 * C, :] += dot(normed_t, ghid)
    mixed[...] = total
    grad = cotangent.astype(F32) + norm_back_rows(gmid, normed, scale, gain_row)
    low = grad.astype(BF)
    gres[...] = low
    gsp = dot_nt(low, w_out[...]).astype(BF)
    gspread[...] = gsp
    low_mixed[...] = total.astype(BF)
    acc_tok[...] += dot(weights, gsp)
    gout[...] += dot(spread_t, low)
    g2[...] += fold_rows(gmid * normed)

    @pl.when(step == pl.num_programs(0) - 1)
    def _():
        flipped = acc_tok[...].T
        for k, ref in enumerate((gt0, gt1, gt2, gt3)):
            ref[...] = own_block(flipped, k)
        for k, ref in enumerate((wg0, wg1, wg2, wg3)):
            ref[...] = acc_w[k].astype(ref.dtype)


def points_kernel(z, pts, wt, mid, gspread, gres, *refs):
    tokens, gnums, refs = refs[:4], refs[4:8], refs[8:]
    gain, slices_t, slices, refs = refs[0], refs[1], refs[2], refs[3:]
    ins, sharps, refs = refs[:4], refs[4:8], refs[8:]
    qkv, g2, gout, gpts, low_a, low_b, o0, o1, o2, o3 = refs[:10]
    flat, tok, gn_t, gn, gden, w_in, acc_in, acc_s, acc_g, acc_h = refs[10:]
    step = pl.program_id(0)

    @pl.when(step == 0)
    def _():
        place_tokens(flat, tokens)
        tok[...] = flat[...].T.astype(BF)
        place_tokens(flat, gnums)
        gn_t[...] = flat[...].astype(BF)
        gn[...] = flat[...].T.astype(BF)
        for k, ref in enumerate(gnums):
            row = ref[HEAD_DIM : HEAD_DIM + 1, :]
            gden[k * 128 : (k + 1) * 128, :] = jnp.broadcast_to(row, (128, 128)).T
        for k, ref in enumerate(ins):
            w_in[k * 64 : (k + 1) * 64, :] = ref[...]
        acc_in[...] = jnp.zeros_like(acc_in)
        acc_s[...] = jnp.zeros_like(acc_s)
        acc_g[...] = jnp.zeros_like(acc_g)
        acc_h[...] = jnp.zeros_like(acc_h)

    normed, scale = norm_parts(pts[...].astype(F32))
    gain_row = gain[...].astype(F32)
    weights = wt[...]
    middle = mid[...]
    rows = weights.shape[1]
    gw = dot_nt(tok[...], gspread[...]) + dot_nt(gn[...], middle)
    pieces, sharp_sums = [], []
    raw = dot_nt(slices_t[...], middle)
    for h in range(HEADS):
        at = slice(h * SLICES, (h + 1) * SLICES)
        sharp = sharp_row(sharps[h // GH][...], h % GH, rows)
        w = softmax_slices(raw[at], sharp)
        g = gw[at] + jnp.concatenate([gden[at, :]] * (rows // 128), axis=1)
        gl = w * (g - jnp.sum(w * g, 0, keepdims=True))
        pieces.append((gl * sharp).astype(BF))
        sharp_sums.append(jnp.sum(gl * raw[at], 0, keepdims=True))
    graw = jnp.concatenate(pieces, 0)
    gmid_t = (dot(gn_t[...], weights) + dot(slices[...], graw)).astype(BF)
    gmid = gmid_t.T
    gnormed = dot(gmid, w_in[...])
    result = gres[...].astype(F32) + norm_back_rows(gnormed, normed, scale, gain_row)
    gpts[...] = result

    @pl.when(step < pl.num_programs(0) // 2)
    def _():
        low_a[...] = result.astype(BF)

    @pl.when(step >= pl.num_programs(0) // 2)
    def _():
        low_b[...] = result.astype(BF)

    normed_in = (normed * gain_row).astype(BF)
    acc_in[...] += dot(gmid_t, normed_in)
    acc_s[...] += dot(graw, middle)
    acc_g[...] += fold_rows(gnormed * normed)
    acc_h[...] += jnp.concatenate(sharp_sums, 0)

    @pl.when(step == pl.num_programs(0) - 1)
    def _():
        flipped = acc_s[...].T
        gsharp = acc_h[:, 0:128]
        for j in range(1, rows // 128):
            gsharp = gsharp + acc_h[:, j * 128 : (j + 1) * 128]
        gslice = jnp.zeros((HEAD_DIM, 128), F32)
        for k in range(BLOCKS):
            gslice = gslice + own_block(flipped, k)
        gain1 = jnp.sum(acc_g[...], 0, keepdims=True)
        gain2 = jnp.sum(g2[...], 0, keepdims=True)
        for k, ref in enumerate((o0, o1, o2, o3)):
            ref[0:64, :] = acc_in[k * 64 : (k + 1) * 64, :].astype(ref.dtype)
            ref[64:96, 0:128] = gslice.astype(ref.dtype)
            ref[64:96, 128:256] = qkv[...].astype(ref.dtype)
            wide = jnp.concatenate([gsharp[2 * k : 2 * k + 1], gsharp[2 * k + 1 : 2 * k + 2]], 1)
            ref[96:104, :] = jnp.concatenate(
                [wide, gain1, gain2, jnp.zeros((5, C), F32)], 0
            ).astype(ref.dtype)
            ref[104:168, :] = gout[k * 64 : (k + 1) * 64, :].astype(ref.dtype)


HIGH = lax.Precision.HIGHEST


def token_parts(nd, wq, wk, wv):
    padded = jnp.concatenate([nd, jnp.zeros((88, 128), F32)], 0).T
    denom = padded[:, HEAD_DIM : HEAD_DIM + 1]
    tok = padded[:, :HEAD_DIM] / denom
    q, k, v = dot(tok, wq, HIGH), dot(tok, wk, HIGH), dot(tok, wv, HIGH)
    scores = dot_nt(q, k, HIGH) * (1.0 / HEAD_DIM**0.5)
    row = lax.broadcasted_iota(jnp.int32, (128, 128), 0) < SLICES
    col = lax.broadcasted_iota(jnp.int32, (128, 128), 1) < SLICES
    same = row == col
    scores = jnp.where(same, scores, -jnp.inf)
    p = jnp.exp(scores - jnp.max(scores, -1, keepdims=True))
    p = p / jnp.sum(p, -1, keepdims=True)
    return denom, tok, q, k, v, p


def flip(value):
    n = value.shape[1]
    return jnp.concatenate([value, jnp.zeros((128, 128 - n), F32)], 1).T[:n]


def tokens_kernel(a, b, c, d, wq, wk, wv, total, tokens):
    nd = (a[...] + c[...]) + (b[...] + d[...])
    total[...] = nd
    _, _, _, _, v, p = token_parts(nd, *(w[...].astype(F32) for w in (wq, wk, wv)))
    mixed = dot(p, v, HIGH).astype(BF).astype(F32)
    tokens[...] = flip(mixed)


def tokens_back_kernel(scale, nd, a, b, c, d, wq, wk, wv, gn, qkv):
    gt = (a[...] + c[...]) + (b[...] + d[...])
    g = jnp.concatenate([gt, jnp.zeros((96, 128), F32)], 0).T[:, :HEAD_DIM]
    wq, wk, wv = (w[...].astype(F32) for w in (wq, wk, wv))
    denom, tok, q, k, v, p = token_parts(nd[...], wq, wk, wv)
    dv = dot(p.T, g, HIGH)
    dp = dot_nt(g, v, HIGH)
    ds = p * (dp - jnp.sum(p * dp, -1, keepdims=True)) * (1.0 / HEAD_DIM**0.5)
    dq = dot(ds, k, HIGH)
    dk = dot(ds.T, q, HIGH)
    gmt = dot_nt(dq, wq, HIGH) + dot_nt(dk, wk, HIGH) + dot_nt(dv, wv, HIGH)
    gnum = (gmt / denom).astype(BF).astype(F32)
    gden = -jnp.sum(gmt * tok, -1, keepdims=True) / denom
    gn[0:HEAD_DIM, :] = flip(gnum)
    gn[HEAD_DIM : HEAD_DIM + 8, :] = flip(jnp.broadcast_to(gden, (128, 8)))
    tok_t = flip(tok)
    qkv[...] = scale * jnp.concatenate(
        [dot(tok_t, dq, HIGH), dot(tok_t, dk, HIGH), dot(tok_t, dv, HIGH), jnp.zeros((32, 32), F32)],
        1,
    )


def full(shape):
    return pl.BlockSpec(shape, lambda *_: (0,) * len(shape))


def part(shape, row):
    return pl.BlockSpec(shape, lambda *_: (row, 0))


def shape_of(shape, dtype):
    return jax.ShapeDtypeStruct(shape, dtype)


def cost(us):
    return pl.CostEstimate(flops=int(us * 1.0e6), bytes_accessed=1024, transcendentals=0)


UP, DOWN, WIN, WOUT, SHARP = (256, 0), (256, 1), (64, 8), (64, 9), (16, 40)
WIDE, NARROW = 1024, 512
TAIL = 168


def pack_specs(kind):
    return [part((kind[0], C), kind[1])] * BLOCKS


def local(
    pts_size,
    points,
    cotangent,
    gain_one,
    w_in,
    slice_weight,
    sharp,
    w_query,
    w_key,
    w_value,
    w_out,
    gain_two,
    w_up,
    w_down,
):
    axes = ("pts", "head")
    rows = points.shape[0]
    quarter = rows // BLOCKS

    def pull(value, dx=0, dy=0, dc=0, dz=0):
        pairs = []
        for p in range(pts_size):
            x, y, c = p // 8, (p // 2) % 4, p % 2
            there = p
            if pts_size > 1:
                there = (((x + dx) % 4) * 4 + (y + dy) % 4) * 2 + (c + dc) % 2
            for z in range(BLOCKS):
                pairs.append((there * BLOCKS + (z + dz) % BLOCKS, p * BLOCKS + z))
        return lax.ppermute(value, axes, pairs)

    def pulls(value, axis):
        return [pull(value, **{axis: k}) for k in (1, 2, 3)]

    def tie(*values):
        return lax.optimization_barrier(values)

    def add4(a, r):
        return (a + r[1].astype(F32)) + (r[0].astype(F32) + r[2].astype(F32))

    def core_sum(value):
        return value + pull(value, dc=1) if pts_size > 1 else value

    def rounded(value):
        return lax.reduce_precision(value, 8, 7)

    def axis_peers(value, axis):
        if pts_size == 1:
            return [jnp.zeros_like(value)] * 3
        return pulls(value, axis)

    core = lax.axis_index("pts").astype(jnp.int32) % 2
    z = jnp.stack([lax.axis_index("head").astype(jnp.int32), core])

    def row_spec(size, away, first=0):
        n = quarter // size
        return pl.BlockSpec(
            (size, C), lambda i, z: (lax.rem(z[0] + away, BLOCKS) * n + first // size + i, 0)
        )

    def own_spec(size, first=0):
        return pl.BlockSpec((size, C), lambda i, z: (first // size + i, 0))

    def own_cols(size, first=0):
        return pl.BlockSpec((HM, size), lambda i, z: (0, first // size + i))

    def grid(steps, in_specs, out_specs, scratch=()):
        return pltpu.PrefetchScalarGridSpec(
            num_scalar_prefetch=1,
            grid=steps,
            in_specs=in_specs,
            out_specs=out_specs,
            scratch_shapes=scratch,
        )

    any_spec = pl.BlockSpec(memory_space=pl.ANY)
    params = pltpu.CompilerParams(vmem_limit_bytes=VMEM_LIMIT)

    wq, wk, wv = w_query, w_key, w_value
    pack, slices_t, slices, gain1, gain2 = pl.pallas_call(
        prep_kernel,
        out_shape=[shape_of((656, C), BF), shape_of((HM, C), BF), shape_of((C, HM), BF)]
        + [shape_of((1, C), F32)] * 2,
        in_specs=[pl.BlockSpec(memory_space=pltpu.VMEM)] * 4
        + [pl.BlockSpec(memory_space=pltpu.SMEM)]
        + [pl.BlockSpec(memory_space=pltpu.VMEM)] * 3,
        scratch_shapes=[pltpu.VMEM((C, HM), F32)],
        compiler_params=params,
        cost_estimate=cost(2),
        name="prep",
    )(w_up, w_down, w_in.T, w_out, sharp.astype(F32), slice_weight, gain_one, gain_two)
    packs = [pack] + pulls(pack, "dz")

    nd = pl.pallas_call(
        own_sums_kernel,
        grid=(rows // (2 * WIDE),),
        in_specs=[
            pl.BlockSpec((2 * WIDE, C), lambda i: (i, 0)),
            full((1, C)),
            part((64, C), WIN[1]),
            part((128, C), 0),
            part((16, C), SHARP[1]),
        ],
        out_specs=full((40, 128)),
        out_shape=shape_of((40, 128), F32),
        scratch_shapes=[pltpu.VMEM((128, 64), F32), pltpu.VMEM((128, 128), F32)],
        compiler_params=params,
        cost_estimate=cost(8),
        name="own_sums",
    )(points, gain1, pack, slices_t, pack)

    half = quarter // 2

    def weights_call():
        return pl.pallas_call(
            weights_kernel,
            grid_spec=grid(
                (quarter // WIDE,),
                [row_spec(WIDE, 0), full((1, C))]
                + pack_specs(WIN)
                + [full((HM, C))]
                + pack_specs(SHARP),
                [own_cols(WIDE), own_spec(WIDE)],
                [pltpu.VMEM((C, C), BF)],
            ),
            out_shape=[shape_of((HM, quarter), BF), shape_of((quarter, C), BF)],
            compiler_params=params,
            cost_estimate=cost(5),
            name="weights",
        )(z, points, gain1, *packs, slices_t, *packs)

    def mlp_call(tokens, wt):
        size = WIDE
        out_shape = [shape_of((rows, C), F32)] + [shape_of((quarter, C), BF)] * 3
        out_shape += [shape_of((HEAD_DIM, 128), F32)] * 4
        out_shape += [shape_of((2 * C, C), F32)] + [shape_of((2 * C, C), BF)] * 3
        out_shape += [shape_of((C, C), F32), shape_of((8, C), F32)]
        out_specs = [row_spec(size, 0)] + [own_spec(size)] * 3
        out_specs += [full((HEAD_DIM, 128))] * 4 + [full((2 * C, C))] * 4
        out_specs += [full((C, C)), full((8, C))]
        return pl.pallas_call(
            mlp_kernel,
            grid_spec=grid(
                (quarter // size,),
                [row_spec(size, 0), row_spec(size, 0), own_cols(size)]
                + [full((HEAD_DIM, 128))] * 4
                + [full((1, C))]
                + pack_specs(UP)
                + pack_specs(DOWN)
                + pack_specs(WOUT),
                out_specs,
                [
                    pltpu.VMEM((C, HM), F32),
                    pltpu.VMEM((C, HM), BF),
                    pltpu.VMEM((C, C), BF),
                    pltpu.VMEM((HM, C), F32),
                    pltpu.VMEM((BLOCKS, 2 * C, C), F32),
                ],
            ),
            out_shape=out_shape,
            compiler_params=params,
            cost_estimate=cost(16),
            name="mlp",
        )(z, points, cotangent, wt, *tokens, gain2, *packs, *packs, *packs)

    def points_call(tokens, gnums, wt, mid, gspread, gres, qkv, g2, gout):
        size = NARROW
        steps = quarter // size
        halves = [
            pl.BlockSpec((size, C), lambda i, z: (jnp.minimum(i, steps // 2 - 1), 0)),
            pl.BlockSpec((size, C), lambda i, z: (jnp.maximum(i - steps // 2, 0), 0)),
        ]
        return pl.pallas_call(
            points_kernel,
            grid_spec=grid(
                (steps,),
                [row_spec(size, 0), own_cols(size)]
                + [own_spec(size)] * 3
                + [full((HEAD_DIM, 128))] * 4
                + [full((40, 128))] * 4
                + [full((1, C)), full((HM, C)), full((C, HM))]
                + pack_specs(WIN)
                + pack_specs(SHARP)
                + [full((HEAD_DIM, 128)), full((8, C)), full((C, C))],
                [row_spec(size, 0)] + halves + [full((TAIL, C))] * 4,
                [
                    pltpu.VMEM((C, HM), F32),
                    pltpu.VMEM((HM, C), BF),
                    pltpu.VMEM((C, HM), BF),
                    pltpu.VMEM((HM, C), BF),
                    pltpu.VMEM((HM, 128), F32),
                    pltpu.VMEM((C, C), BF),
                    pltpu.VMEM((C, C), F32),
                    pltpu.VMEM((HM, C), F32),
                    pltpu.VMEM((8, C), F32),
                    pltpu.VMEM((HEADS, size), F32),
                ],
            ),
            out_shape=[shape_of((rows, C), F32)]
            + [shape_of((half, C), BF)] * 2
            + [shape_of((TAIL, C), F32)]
            + [shape_of((TAIL, C), BF)] * 3,
            compiler_params=params,
            cost_estimate=cost(12),
            name="points",
        )(
            z, points, wt, mid, gspread, gres, *tokens, *gnums, gain1, slices_t, slices,
            *packs, *packs, qkv, g2, gout
        )

    half = quarter // 2

    def fill_out(at):
        return pl.BlockSpec(
            (half, C), lambda i, z: (lax.rem(2 * z[0] + at(i), 2 * BLOCKS), 0)
        )

    def fill_call(at, parts, before):
        n = len(parts)
        return pl.pallas_call(
            fill_kernel,
            grid_spec=grid((n,), [s for _, s in parts] + [any_spec], fill_out(at)),
            out_shape=shape_of((rows, C), F32),
            input_output_aliases={n + 1: 0},
            compiler_params=params,
            cost_estimate=cost(3),
            name="fill",
        )(z, *[p for p, _ in parts], before)

    def halves_of(value):
        return [(value, part((half, C), 0)), (value, part((half, C), 1))]

    def whole(*values):
        return [(v, full((half, C))) for v in values]

    nd = core_sum(nd)
    got = axis_peers(nd, "dx")
    nd, packs[0] = tie(nd, packs[0])
    wt, mid = weights_call()
    got, wt = tie(got, wt)
    nd = add4(nd, got)
    got = axis_peers(nd, "dy")
    nd, own_tokens = pl.pallas_call(
        tokens_kernel,
        out_shape=[shape_of((40, 128), F32), shape_of((HEAD_DIM, 128), F32)],
        compiler_params=params,
        cost_estimate=cost(3),
        name="tokens",
    )(nd, *got, wq, wk, wv)
    tokens = [own_tokens] + pulls(own_tokens, "dz")

    result = mlp_call(tokens, wt)
    mixed, gres, gspread, send = result[:4]
    gts, wgs, (gout, g2) = result[4:8], result[8:12], result[12:]

    got = [pull(gts[BLOCKS - k], dz=k) for k in (1, 2, 3)]
    wgot = [pull(wgs[3], dz=1), pull(wgs[2], dz=2)]
    gt = add4(gts[0], got)
    gt, wg1 = tie(gt, wgs[1])
    wgot.append(pull(wg1, dz=3))
    gt = core_sum(gt)
    got = axis_peers(gt, "dx")
    got, wgot = tie(got, wgot)
    gt = add4(gt, got)
    got = axis_peers(gt, "dy")
    gt, send = tie(gt, send)
    near = [pull(send, dz=1), pull(send, dz=3)]
    wsum = add4(wgs[0], wgot)
    wlow = wsum.astype(BF)
    own_gn, qkv = pl.pallas_call(
        functools.partial(tokens_back_kernel, 1.0 / pts_size),
        out_shape=[shape_of((40, 128), F32), shape_of((HEAD_DIM, 128), F32)],
        compiler_params=params,
        cost_estimate=cost(4),
        name="tokens_back",
    )(nd, gt, *got, wq, wk, wv)
    got = pulls(own_gn, "dz")
    own_gn, wsum, wlow = tie(own_gn, wsum, wlow)
    if pts_size > 1:
        wsum = rounded(wsum) + pull(wlow, dc=1).astype(F32)
        wlow = lax.dynamic_slice_in_dim(wsum, core * C, C, 0).astype(BF)
    got, wlow = tie(got, wlow)
    wgot = axis_peers(wlow[:C], "dx")
    got, near = tie(got, near)
    near2 = [pull(near[0][:half], dz=1), pull(near[1][half:], dz=3)]
    gnums = [own_gn] + list(got)

    result = points_call(tokens, gnums, wt, mid, gspread, gres, qkv, g2, gout)
    gpts, low_a, low_b, outs = result[0], result[1], result[2], result[3:]
    gpts, outs, low_a, low_b, wgot, near2 = tie(gpts, outs, low_a, low_b, wgot, near2)

    got = [pull(outs[BLOCKS - k], dz=k) for k in (1, 2, 3)]
    a1, b3 = pull(low_a, dz=1), pull(low_b, dz=3)
    outs, mixed = tie(outs, mixed)
    mixed = fill_call(lambda i: 2 + i, halves_of(near[0]) + whole(*near2), mixed)
    got, mixed = tie(got, mixed)
    tail = core_sum(add4(outs[0], got))
    both = jnp.concatenate([tail, add4(wlow[:C].astype(F32), wgot)], 0).astype(BF)
    both, a1, b3 = tie(both, a1, b3)
    far2 = [pull(a1, dz=1), pull(b3, dz=3)]
    got = axis_peers(both, "dy")
    both, mixed = tie(both, mixed)
    mixed = fill_call(lambda i: 6 + i, halves_of(near[1]), mixed)
    got, mixed, far2 = tie(got, mixed, far2)
    both = add4(both.astype(F32), got)
    both, low_a, low_b = tie(both, low_a, low_b)
    b1, a3 = pull(low_b, dz=1), pull(low_a, dz=3)
    tail, wsum = both[:TAIL].astype(BF), both[TAIL:]
    if pts_size > 1:
        other = pull(wsum, dc=1)
    else:
        other = wlow[C:].astype(F32)
    wsum, other, tail = tie(wsum, other, tail)
    got = axis_peers(tail, "dx")
    tail, gpts = tie(tail, gpts)
    gpts = fill_call(
        lambda i: 2 + i + jnp.minimum(i, 1) + i // 3, whole(a1, *far2, b3), gpts
    )
    got, gpts, b1, a3 = tie(got, gpts, b1, a3)
    shapes = [(64, C), (32, 64), (1, GH), (32, 32), (32, 32), (32, 32)]
    shapes += [(64, C), (C, C), (C, C), (1, C), (1, C)]
    result = pl.pallas_call(
        finish_kernel,
        grid_spec=grid(
            (2,),
            [full((half, C))] * 2 + [any_spec] + [full((TAIL, C))] * 4 + [full((C, C))] * 2,
            [fill_out(lambda i: 3 + 3 * i)] + [full(s) for s in shapes],
        ),
        out_shape=[shape_of((rows, C), F32)] + [shape_of(s, F32) for s in shapes],
        input_output_aliases={3: 0},
        compiler_params=params,
        cost_estimate=cost(4),
        name="finish",
    )(z, b1, a3, gpts, tail, *got, wsum, other)
    gpts, gin, gslice, gsharp, gq, gk, gv, gout, gup, gdown, g1, g2 = result
    return (
        mixed, gpts, gin.T, gslice, gsharp.reshape(GH), gq, gk, gv, gout, gup, gdown,
        g1.reshape(C), g2.reshape(C),
    )


def solution(mesh):
    row, none, cols, heads = P("pts", None), P(), P(None, "head"), P("head")
    down = P("head", None)
    placed = (row, row, none, cols, none, heads, none, none, none, down, none, cols, down)
    given = (row, row, cols, none, heads, none, none, none, down, cols, down, none, none)
    return jax.shard_map(
        functools.partial(local, mesh.shape["pts"]),
        mesh=mesh,
        in_specs=placed,
        out_specs=given,
        check_vma=False,
    )
```

```python
import functools
import jax
import jax.numpy as jnp
from jax import lax
from jax.experimental import pallas as pl
from jax.experimental.pallas import tpu as pltpu
from jax.sharding import PartitionSpec as P

HEAD_DIM = 32
SLICES = 64
C = 256
HEADS = 8
BLOCKS = 4
GH = HEADS // BLOCKS
HM = HEADS * SLICES
C0 = 0.7978845608028654
C1 = 0.7978845608028654 * 0.044715
BF = jnp.bfloat16
F32 = jnp.float32
VMEM_LIMIT = 56 * 1024 * 1024


def dot(a, b, precision=None):
    return lax.dot_general(
        a, b, (((1,), (0,)), ((), ())), preferred_element_type=F32, precision=precision
    )


def dot_nt(a, b, precision=None):
    return lax.dot_general(
        a, b, (((1,), (1,)), ((), ())), preferred_element_type=F32, precision=precision
    )


def norm_parts(value):
    centred = value - jnp.mean(value, -1, keepdims=True)
    scale = lax.rsqrt(jnp.mean(centred * centred, -1, keepdims=True) + 1e-05)
    return centred * scale, scale


def norm_back_rows(grad, normed, scale, gain):
    scaled = grad * gain
    return scale * (
        scaled
        - jnp.mean(scaled, -1, keepdims=True)
        - normed * jnp.mean(scaled * normed, -1, keepdims=True)
    )


def sharp_row(block, which, width):
    row = block[which : which + 1, :].astype(F32)
    return jnp.concatenate([row] * (width // C), axis=1)


def softmax_slices(raw, sharp):
    logits = raw * sharp
    grown = jnp.exp(logits - jnp.max(logits, 0, keepdims=True))
    return grown * (1.0 / jnp.sum(grown, 0, keepdims=True))


def fold_rows(value):
    return jnp.sum(value.reshape(value.shape[0] // 8, 8, value.shape[1]), 0)


def prep_kernel(
    w_up, w_down, w_in, w_out, sharp, slice_weight, one, two, pack, slices_t, slices, gain1, gain2, s_scr
):
    gain1[...] = one[...].astype(F32).reshape(1, C)
    gain2[...] = two[...].astype(F32).reshape(1, C)
    pack[0:256, :] = w_up[...].T
    pack[256:512, :] = w_down[...]
    pack[512:576, :] = w_in[...]
    pack[576:640, :] = w_out[...]
    row = lax.broadcasted_iota(jnp.int32, (16, C), 0)
    both = sharp[...].astype(F32).reshape(1, GH)
    pack[640:656, :] = jnp.where(row == 0, both[:, 0:1], both[:, 1:2]).astype(BF)
    s_scr[...] = jnp.zeros_like(s_scr)
    weight = slice_weight[...].astype(F32)
    twice = jnp.concatenate([weight, weight], 1)
    lane = lax.broadcasted_iota(jnp.int32, (HEAD_DIM, 128), 1)
    for k in range(BLOCKS):
        at = slice(k * 128, (k + 1) * 128)
        s_scr[k * 64 : k * 64 + 32, at] = jnp.where(lane < SLICES, twice, 0.0)
        s_scr[k * 64 + 32 : k * 64 + 64, at] = jnp.where(lane < SLICES, 0.0, twice)
    slices[...] = s_scr[...].astype(BF)
    slices_t[...] = s_scr[...].T.astype(BF)


def fill_kernel(z, *refs):
    out = refs[-1]
    for k, ref in enumerate(refs[:-2]):

        @pl.when(pl.program_id(0) == k)
        def _():
            out[...] = ref[...].astype(F32)


def finish_kernel(z, first, second, before, t0, t1, t2, t3, w0, w1, *refs):
    out, gin, gslice, gsharp, gq, gk, gv, gout, gup, gdown, g1, g2 = refs
    fill_kernel(z, first, second, before, out)

    @pl.when(pl.program_id(0) == 0)
    def _():
        a, b, c, d = (t[...].astype(F32) for t in (t0, t1, t2, t3))
        tail = (a + c) + (b + d)
        gin[...] = tail[0:64]
        gslice[...] = tail[64:96, 0:64] + tail[64:96, 64:128]
        gq[...] = tail[64:96, 128:160]
        gk[...] = tail[64:96, 160:192]
        gv[...] = tail[64:96, 192:224]
        gsharp[...] = jnp.concatenate(
            [
                jnp.sum(tail[96:97, 0:128], 1, keepdims=True),
                jnp.sum(tail[96:97, 128:256], 1, keepdims=True),
            ],
            1,
        )
        g1[...] = tail[97:98]
        g2[...] = tail[98:99]
        gout[...] = tail[104:168]

        @pl.when(z[1] == 0)
        def _():
            gdown[...] = w0[...].T
            gup[...] = w1[...]

        @pl.when(z[1] == 1)
        def _():
            gdown[...] = w1[...].T
            gup[...] = w0[...]


def own_sums_kernel(pts, gain, w_in, spread_slices, sharp, out, acc, den):
    step = pl.program_id(0)

    @pl.when(step == 0)
    def _():
        acc[...] = jnp.zeros_like(acc)
        den[...] = jnp.zeros_like(den)

    normed, _ = norm_parts(pts[...].astype(F32))
    normed_in = (normed * gain[...].astype(F32)).astype(BF)
    middle = dot_nt(normed_in, w_in[...]).astype(BF)
    raw = dot_nt(spread_slices[:, 0:64], middle)
    rows = raw.shape[1]
    sharps = sharp[...]
    parts = [
        softmax_slices(raw[h * SLICES : (h + 1) * SLICES], sharp_row(sharps, h, rows))
        for h in range(GH)
    ]
    weights = jnp.concatenate(parts, 0)
    total = weights[:, 0:128]
    for j in range(1, rows // 128):
        total = total + weights[:, j * 128 : (j + 1) * 128]
    den[...] += total
    acc[...] += dot(weights.astype(BF), middle)

    @pl.when(step == pl.num_programs(0) - 1)
    def _():
        flipped = acc[...].T
        lane = lax.broadcasted_iota(jnp.int32, (HEAD_DIM, 128), 1)
        out[0:HEAD_DIM, :] = jnp.where(lane < SLICES, flipped[:HEAD_DIM], flipped[HEAD_DIM:])
        row = jnp.sum(den[...].T, 0, keepdims=True)
        out[HEAD_DIM : HEAD_DIM + 8, :] = jnp.broadcast_to(row, (8, 128))


def weights_kernel(z, pts, gain, in0, in1, in2, in3, spread_slices, s0, s1, s2, s3, *rest):
    wt, mid, w_in = rest

    @pl.when(pl.program_id(0) == 0)
    def _():
        for k, ref in enumerate((in0, in1, in2, in3)):
            w_in[k * 64 : (k + 1) * 64, :] = ref[...]

    normed, _ = norm_parts(pts[...].astype(F32))
    normed_in = (normed * gain[...].astype(F32)).astype(BF)
    middle = dot_nt(normed_in, w_in[...]).astype(BF)
    mid[...] = middle
    raw = dot_nt(spread_slices[...], middle)
    rows = raw.shape[1]
    for h in range(HEADS):
        sharp = sharp_row((s0, s1, s2, s3)[h // GH][...], h % GH, rows)
        wt[h * SLICES : (h + 1) * SLICES, :] = softmax_slices(
            raw[h * SLICES : (h + 1) * SLICES], sharp
        ).astype(BF)


def place_tokens(flat, tokens):
    flat[...] = jnp.zeros_like(flat)
    lane = lax.broadcasted_iota(jnp.int32, (HEAD_DIM, 128), 1)
    for k, ref in enumerate(tokens):
        t = ref[0:HEAD_DIM, :]
        flat[k * 64 : k * 64 + 32, k * 128 : (k + 1) * 128] = jnp.where(lane < SLICES, t, 0.0)
        flat[k * 64 + 32 : k * 64 + 64, k * 128 : (k + 1) * 128] = jnp.where(
            lane < SLICES, 0.0, t
        )


def own_block(flipped, k):
    lane = lax.broadcasted_iota(jnp.int32, (HEAD_DIM, 128), 1)
    block = flipped[k * 64 : (k + 1) * 64, k * 128 : (k + 1) * 128]
    return jnp.where(lane < SLICES, block[:HEAD_DIM], block[HEAD_DIM:])


def mlp_kernel(z, pts, cot, wt, *refs):
    tokens, refs = refs[:4], refs[4:]
    gain, refs = refs[0], refs[1:]
    ups, downs, outs, refs = refs[:4], refs[4:8], refs[8:12], refs[12:]
    mixed, gres, gspread, low_mixed, gt0, gt1, gt2, gt3, wg0, wg1, wg2, wg3, gout, g2 = refs[:14]
    flat, tok_t, w_out, acc_tok, acc_w = refs[14:]
    step = pl.program_id(0)

    @pl.when(step == 0)
    def _():
        place_tokens(flat, tokens)
        tok_t[...] = flat[...].astype(BF)
        for k, ref in enumerate(outs):
            w_out[k * 64 : (k + 1) * 64, :] = ref[...]
        acc_tok[...] = jnp.zeros_like(acc_tok)
        acc_w[...] = jnp.zeros_like(acc_w)
        gout[...] = jnp.zeros_like(gout)
        g2[...] = jnp.zeros_like(g2)

    weights = wt[...]
    spread_t = dot(tok_t[...], weights).astype(BF)
    spread = spread_t.T
    resid = pts[...].astype(F32) + dot(spread, w_out[...])
    normed, scale = norm_parts(resid)
    gain_row = gain[...].astype(F32)
    normed_mid = (normed * gain_row).astype(BF)
    cotangent = cot[...]
    total = resid
    gmid = None
    cot_t = cotangent.T
    normed_t = normed_mid.T
    for k in range(BLOCKS):
        up, down = ups[k][...], downs[k][...]
        hidden = dot_nt(normed_mid, up)
        square = hidden * hidden
        inner = jnp.tanh(hidden * (C0 + C1 * square))
        half = 0.5 + 0.5 * inner
        gelu = hidden * half
        active = gelu.astype(BF)
        total = total + dot(active, down)
        slope = half + gelu * (1.0 - half) * (2.0 * C0 + 6.0 * C1 * square)
        ghid = (dot_nt(cotangent, down) * slope).astype(BF)
        part = dot(ghid, up)
        gmid = part if gmid is None else gmid + part
        acc_w[k, 0:C, :] += dot(cot_t, active)
        acc_w[k, C : 2 * C, :] += dot(normed_t, ghid)
    mixed[...] = total
    grad = cotangent.astype(F32) + norm_back_rows(gmid, normed, scale, gain_row)
    low = grad.astype(BF)
    gres[...] = low
    gsp = dot_nt(low, w_out[...]).astype(BF)
    gspread[...] = gsp
    low_mixed[...] = total.astype(BF)
    acc_tok[...] += dot(weights, gsp)
    gout[...] += dot(spread_t, low)
    g2[...] += fold_rows(gmid * normed)

    @pl.when(step == pl.num_programs(0) - 1)
    def _():
        flipped = acc_tok[...].T
        for k, ref in enumerate((gt0, gt1, gt2, gt3)):
            ref[...] = own_block(flipped, k)
        for k, ref in enumerate((wg0, wg1, wg2, wg3)):
            ref[...] = acc_w[k].astype(ref.dtype)


def points_kernel(z, pts, wt, mid, gspread, gres, *refs):
    tokens, gnums, refs = refs[:4], refs[4:8], refs[8:]
    gain, slices_t, slices, refs = refs[0], refs[1], refs[2], refs[3:]
    ins, sharps, refs = refs[:4], refs[4:8], refs[8:]
    qkv, g2, gout, gpts, low_a, low_b, o0, o1, o2, o3 = refs[:10]
    flat, tok, gn_t, gn, gden, w_in, acc_in, acc_s, acc_g, acc_h = refs[10:]
    step = pl.program_id(0)

    @pl.when(step == 0)
    def _():
        place_tokens(flat, tokens)
        tok[...] = flat[...].T.astype(BF)
        place_tokens(flat, gnums)
        gn_t[...] = flat[...].astype(BF)
        gn[...] = flat[...].T.astype(BF)
        for k, ref in enumerate(gnums):
            row = ref[HEAD_DIM : HEAD_DIM + 1, :]
            gden[k * 128 : (k + 1) * 128, :] = jnp.broadcast_to(row, (128, 128)).T
        for k, ref in enumerate(ins):
            w_in[k * 64 : (k + 1) * 64, :] = ref[...]
        acc_in[...] = jnp.zeros_like(acc_in)
        acc_s[...] = jnp.zeros_like(acc_s)
        acc_g[...] = jnp.zeros_like(acc_g)
        acc_h[...] = jnp.zeros_like(acc_h)

    normed, scale = norm_parts(pts[...].astype(F32))
    gain_row = gain[...].astype(F32)
    weights = wt[...]
    middle = mid[...]
    rows = weights.shape[1]
    gw = dot_nt(tok[...], gspread[...]) + dot_nt(gn[...], middle)
    pieces, sharp_sums = [], []
    raw = dot_nt(slices_t[...], middle)
    for h in range(HEADS):
        at = slice(h * SLICES, (h + 1) * SLICES)
        sharp = sharp_row(sharps[h // GH][...], h % GH, rows)
        w = softmax_slices(raw[at], sharp)
        g = gw[at] + jnp.concatenate([gden[at, :]] * (rows // 128), axis=1)
        gl = w * (g - jnp.sum(w * g, 0, keepdims=True))
        pieces.append((gl * sharp).astype(BF))
        sharp_sums.append(jnp.sum(gl * raw[at], 0, keepdims=True))
    graw = jnp.concatenate(pieces, 0)
    gmid_t = (dot(gn_t[...], weights) + dot(slices[...], graw)).astype(BF)
    gmid = gmid_t.T
    gnormed = dot(gmid, w_in[...])
    result = gres[...].astype(F32) + norm_back_rows(gnormed, normed, scale, gain_row)
    gpts[...] = result

    @pl.when(step < pl.num_programs(0) // 2)
    def _():
        low_a[...] = result.astype(BF)

    @pl.when(step >= pl.num_programs(0) // 2)
    def _():
        low_b[...] = result.astype(BF)

    normed_in = (normed * gain_row).astype(BF)
    acc_in[...] += dot(gmid_t, normed_in)
    acc_s[...] += dot(graw, middle)
    acc_g[...] += fold_rows(gnormed * normed)
    acc_h[...] += jnp.concatenate(sharp_sums, 0)

    @pl.when(step == pl.num_programs(0) - 1)
    def _():
        flipped = acc_s[...].T
        gsharp = acc_h[:, 0:128]
        for j in range(1, rows // 128):
            gsharp = gsharp + acc_h[:, j * 128 : (j + 1) * 128]
        gslice = jnp.zeros((HEAD_DIM, 128), F32)
        for k in range(BLOCKS):
            gslice = gslice + own_block(flipped, k)
        gain1 = jnp.sum(acc_g[...], 0, keepdims=True)
        gain2 = jnp.sum(g2[...], 0, keepdims=True)
        for k, ref in enumerate((o0, o1, o2, o3)):
            ref[0:64, :] = acc_in[k * 64 : (k + 1) * 64, :].astype(ref.dtype)
            ref[64:96, 0:128] = gslice.astype(ref.dtype)
            ref[64:96, 128:256] = qkv[...].astype(ref.dtype)
            wide = jnp.concatenate([gsharp[2 * k : 2 * k + 1], gsharp[2 * k + 1 : 2 * k + 2]], 1)
            ref[96:104, :] = jnp.concatenate(
                [wide, gain1, gain2, jnp.zeros((5, C), F32)], 0
            ).astype(ref.dtype)
            ref[104:168, :] = gout[k * 64 : (k + 1) * 64, :].astype(ref.dtype)


def halves(value):
    high = value.astype(BF)
    return high, (value - high.astype(F32)).astype(BF)


def dot3(a, b, form=dot):
    (ah, al), (bh, bl) = halves(a), halves(b)
    return form(ah, bh) + (form(ah, bl) + form(al, bh))


def dot3_nt(a, b):
    return dot3(a, b, dot_nt)


def token_parts(nd, wq, wk, wv):
    padded = jnp.concatenate([nd, jnp.zeros((88, 128), F32)], 0).T
    denom = padded[:, HEAD_DIM : HEAD_DIM + 1]
    tok = padded[:, :HEAD_DIM] / denom
    q, k, v = dot3(tok, wq), dot3(tok, wk), dot3(tok, wv)
    scores = dot3_nt(q, k) * (1.0 / HEAD_DIM**0.5)
    row = lax.broadcasted_iota(jnp.int32, (128, 128), 0) < SLICES
    col = lax.broadcasted_iota(jnp.int32, (128, 128), 1) < SLICES
    same = row == col
    scores = jnp.where(same, scores, -jnp.inf)
    p = jnp.exp(scores - jnp.max(scores, -1, keepdims=True))
    p = p / jnp.sum(p, -1, keepdims=True)
    return denom, tok, q, k, v, p


def flip(value):
    n = value.shape[1]
    return jnp.concatenate([value, jnp.zeros((128, 128 - n), F32)], 1).T[:n]


def tokens_kernel(a, b, c, d, wq, wk, wv, total, tokens):
    nd = (a[...] + c[...]) + (b[...] + d[...])
    total[...] = nd
    _, _, _, _, v, p = token_parts(nd, *(w[...].astype(F32) for w in (wq, wk, wv)))
    mixed = dot3(p, v).astype(BF).astype(F32)
    tokens[...] = flip(mixed)


def tokens_back_kernel(scale, nd, a, b, c, d, wq, wk, wv, gn, qkv):
    gt = (a[...] + c[...]) + (b[...] + d[...])
    g = jnp.concatenate([gt, jnp.zeros((96, 128), F32)], 0).T[:, :HEAD_DIM]
    wq, wk, wv = (w[...].astype(F32) for w in (wq, wk, wv))
    denom, tok, q, k, v, p = token_parts(nd[...], wq, wk, wv)
    dv = dot3(p.T, g)
    dp = dot3_nt(g, v)
    ds = p * (dp - jnp.sum(p * dp, -1, keepdims=True)) * (1.0 / HEAD_DIM**0.5)
    dq = dot3(ds, k)
    dk = dot3(ds.T, q)
    gmt = dot3_nt(dq, wq) + dot3_nt(dk, wk) + dot3_nt(dv, wv)
    gnum = (gmt / denom).astype(BF).astype(F32)
    gden = -jnp.sum(gmt * tok, -1, keepdims=True) / denom
    gn[0:HEAD_DIM, :] = flip(gnum)
    gn[HEAD_DIM : HEAD_DIM + 8, :] = flip(jnp.broadcast_to(gden, (128, 8)))
    tok_t = flip(tok)
    qkv[...] = scale * jnp.concatenate(
        [dot3(tok_t, dq), dot3(tok_t, dk), dot3(tok_t, dv), jnp.zeros((32, 32), F32)],
        1,
    )


def full(shape):
    return pl.BlockSpec(shape, lambda *_: (0,) * len(shape))


def part(shape, row):
    return pl.BlockSpec(shape, lambda *_: (row, 0))


def shape_of(shape, dtype):
    return jax.ShapeDtypeStruct(shape, dtype)


def cost(us):
    return pl.CostEstimate(flops=int(us * 1.0e6), bytes_accessed=1024, transcendentals=0)


UP, DOWN, WIN, WOUT, SHARP = (256, 0), (256, 1), (64, 8), (64, 9), (16, 40)
WIDE, NARROW = 1024, 512
TAIL = 168


def pack_specs(kind):
    return [part((kind[0], C), kind[1])] * BLOCKS


def local(
    pts_size,
    points,
    cotangent,
    gain_one,
    w_in,
    slice_weight,
    sharp,
    w_query,
    w_key,
    w_value,
    w_out,
    gain_two,
    w_up,
    w_down,
):
    axes = ("pts", "head")
    rows = points.shape[0]
    quarter = rows // BLOCKS

    def pull(value, dx=0, dy=0, dc=0, dz=0):
        pairs = []
        for p in range(pts_size):
            x, y, c = p // 8, (p // 2) % 4, p % 2
            there = p
            if pts_size > 1:
                there = (((x + dx) % 4) * 4 + (y + dy) % 4) * 2 + (c + dc) % 2
            for z in range(BLOCKS):
                pairs.append((there * BLOCKS + (z + dz) % BLOCKS, p * BLOCKS + z))
        return lax.ppermute(value, axes, pairs)

    def pulls(value, axis):
        return [pull(value, **{axis: k}) for k in (1, 2, 3)]

    def tie(*values):
        return lax.optimization_barrier(values)

    def add4(a, r):
        return (a + r[1].astype(F32)) + (r[0].astype(F32) + r[2].astype(F32))

    def core_sum(value):
        return value + pull(value, dc=1) if pts_size > 1 else value

    def rounded(value):
        return lax.reduce_precision(value, 8, 7)

    def axis_peers(value, axis):
        if pts_size == 1:
            return [jnp.zeros_like(value)] * 3
        return pulls(value, axis)

    core = lax.axis_index("pts").astype(jnp.int32) % 2
    z = jnp.stack([lax.axis_index("head").astype(jnp.int32), core])

    def row_spec(size, away, first=0):
        n = quarter // size
        return pl.BlockSpec(
            (size, C), lambda i, z: (lax.rem(z[0] + away, BLOCKS) * n + first // size + i, 0)
        )

    def own_spec(size, first=0):
        return pl.BlockSpec((size, C), lambda i, z: (first // size + i, 0))

    def own_cols(size, first=0):
        return pl.BlockSpec((HM, size), lambda i, z: (0, first // size + i))

    def grid(steps, in_specs, out_specs, scratch=()):
        return pltpu.PrefetchScalarGridSpec(
            num_scalar_prefetch=1,
            grid=steps,
            in_specs=in_specs,
            out_specs=out_specs,
            scratch_shapes=scratch,
        )

    any_spec = pl.BlockSpec(memory_space=pl.ANY)
    params = pltpu.CompilerParams(vmem_limit_bytes=VMEM_LIMIT)

    wq, wk, wv = w_query, w_key, w_value
    pack, slices_t, slices, gain1, gain2 = pl.pallas_call(
        prep_kernel,
        out_shape=[shape_of((656, C), BF), shape_of((HM, C), BF), shape_of((C, HM), BF)]
        + [shape_of((1, C), F32)] * 2,
        scratch_shapes=[pltpu.VMEM((C, HM), F32)],
        compiler_params=params,
        cost_estimate=cost(2),
        name="prep",
    )(w_up, w_down, w_in.T, w_out, sharp, slice_weight, gain_one, gain_two)

    nd = pl.pallas_call(
        own_sums_kernel,
        grid=(rows // (2 * WIDE),),
        in_specs=[
            pl.BlockSpec((2 * WIDE, C), lambda i: (i, 0)),
            full((1, C)),
            part((64, C), WIN[1]),
            part((128, C), 0),
            part((16, C), SHARP[1]),
        ],
        out_specs=full((40, 128)),
        out_shape=shape_of((40, 128), F32),
        scratch_shapes=[pltpu.VMEM((128, 64), F32), pltpu.VMEM((128, 128), F32)],
        compiler_params=params,
        cost_estimate=cost(8),
        name="own_sums",
    )(points, gain1, pack, slices_t, pack)

    half = quarter // 2

    def weights_call():
        return pl.pallas_call(
            weights_kernel,
            grid_spec=grid(
                (quarter // WIDE,),
                [row_spec(WIDE, 0), full((1, C))]
                + pack_specs(WIN)
                + [full((HM, C))]
                + pack_specs(SHARP),
                [own_cols(WIDE), own_spec(WIDE)],
                [pltpu.VMEM((C, C), BF)],
            ),
            out_shape=[shape_of((HM, quarter), BF), shape_of((quarter, C), BF)],
            compiler_params=params,
            cost_estimate=cost(5),
            name="weights",
        )(z, points, gain1, *packs, slices_t, *packs)

    def mlp_call(tokens, wt):
        size = WIDE
        out_shape = [shape_of((rows, C), F32)] + [shape_of((quarter, C), BF)] * 3
        out_shape += [shape_of((HEAD_DIM, 128), F32)] * 4
        out_shape += [shape_of((2 * C, C), F32)] + [shape_of((2 * C, C), BF)] * 3
        out_shape += [shape_of((C, C), F32), shape_of((8, C), F32)]
        out_specs = [row_spec(size, 0)] + [own_spec(size)] * 3
        out_specs += [full((HEAD_DIM, 128))] * 4 + [full((2 * C, C))] * 4
        out_specs += [full((C, C)), full((8, C))]
        return pl.pallas_call(
            mlp_kernel,
            grid_spec=grid(
                (quarter // size,),
                [row_spec(size, 0), row_spec(size, 0), own_cols(size)]
                + [full((HEAD_DIM, 128))] * 4
                + [full((1, C))]
                + pack_specs(UP)
                + pack_specs(DOWN)
                + pack_specs(WOUT),
                out_specs,
                [
                    pltpu.VMEM((C, HM), F32),
                    pltpu.VMEM((C, HM), BF),
                    pltpu.VMEM((C, C), BF),
                    pltpu.VMEM((HM, C), F32),
                    pltpu.VMEM((BLOCKS, 2 * C, C), F32),
                ],
            ),
            out_shape=out_shape,
            compiler_params=params,
            cost_estimate=cost(16),
            name="mlp",
        )(z, points, cotangent, wt, *tokens, gain2, *packs, *packs, *packs)

    half = quarter // 2

    def points_call(tokens, gnums, wt, mid, gspread, gres, qkv, g2, gout):
        size = half
        steps = quarter // size
        halves = [full((half, C))] * 2
        return pl.pallas_call(
            points_kernel,
            grid_spec=grid(
                (steps,),
                [row_spec(size, 0), own_cols(size)]
                + [own_spec(size)] * 3
                + [full((HEAD_DIM, 128))] * 4
                + [full((40, 128))] * 4
                + [full((1, C)), full((HM, C)), full((C, HM))]
                + pack_specs(WIN)
                + pack_specs(SHARP)
                + [full((HEAD_DIM, 128)), full((8, C)), full((C, C))],
                [row_spec(size, 0)] + halves + [full((TAIL, C))] * 4,
                [
                    pltpu.VMEM((C, HM), F32),
                    pltpu.VMEM((HM, C), BF),
                    pltpu.VMEM((C, HM), BF),
                    pltpu.VMEM((HM, C), BF),
                    pltpu.VMEM((HM, 128), F32),
                    pltpu.VMEM((C, C), BF),
                    pltpu.VMEM((C, C), F32),
                    pltpu.VMEM((HM, C), F32),
                    pltpu.VMEM((8, C), F32),
                    pltpu.VMEM((HEADS, size), F32),
                ],
            ),
            out_shape=[shape_of((rows, C), F32)]
            + [shape_of((half, C), BF)] * 2
            + [shape_of((TAIL, C), F32)]
            + [shape_of((TAIL, C), BF)] * 3,
            compiler_params=params,
            cost_estimate=cost(12),
            name="points",
        )(
            z, points, wt, mid, gspread, gres, *tokens, *gnums, gain1, slices_t, slices,
            *packs, *packs, qkv, g2, gout
        )

    def fill_out(at):
        return pl.BlockSpec(
            (half, C), lambda i, z: (lax.rem(2 * z[0] + at(i), 2 * BLOCKS), 0)
        )

    def fill_call(at, parts, before):
        n = len(parts)
        return pl.pallas_call(
            fill_kernel,
            grid_spec=grid((n,), [s for _, s in parts] + [any_spec], fill_out(at)),
            out_shape=shape_of((rows, C), F32),
            input_output_aliases={n + 1: 0},
            compiler_params=params,
            cost_estimate=cost(3),
            name="fill",
        )(z, *[p for p, _ in parts], before)

    def halves_of(value):
        return [(value, part((half, C), 0)), (value, part((half, C), 1))]

    def whole(*values):
        return [(v, full((half, C))) for v in values]

    nd = core_sum(nd)
    nd, sent = tie(nd, pack)
    got = axis_peers(nd, "dx")
    packs = [pack, pull(sent, dz=1), None, pull(sent, dz=3)]
    nd = add4(nd, got)
    nd, sent = tie(nd, sent)
    got = axis_peers(nd, "dy")
    packs[2] = pull(sent, dz=2)
    nd, own_tokens = pl.pallas_call(
        tokens_kernel,
        out_shape=[shape_of((40, 128), F32), shape_of((HEAD_DIM, 128), F32)],
        compiler_params=params,
        cost_estimate=cost(3),
        name="tokens",
    )(nd, *got, wq, wk, wv)
    got = pulls(own_tokens, "dz")

    own_tokens, *packs = tie(own_tokens, *packs)
    wt, mid = weights_call()
    got, wt = tie(got, wt)
    tokens = [own_tokens] + list(got)

    result = mlp_call(tokens, wt)
    mixed, gres, gspread, send = result[:4]
    gts, wgs, (gout, g2) = result[4:8], result[8:12], result[12:]

    got = [pull(gts[BLOCKS - k], dz=k) for k in (1, 2, 3)]
    wgot = [pull(wgs[3], dz=1), pull(wgs[2], dz=2)]
    gt = add4(gts[0], got)
    gt, wg1 = tie(gt, wgs[1])
    wgot.append(pull(wg1, dz=3))
    gt = core_sum(gt)
    gt, send = tie(gt, send)
    got = axis_peers(gt, "dx")
    near = [pull(send, dz=1), pull(send, dz=3)]
    got, wgot = tie(got, wgot)
    gt = add4(gt, got)
    got = axis_peers(gt, "dy")
    wsum = add4(wgs[0], wgot)
    wlow = wsum.astype(BF)
    own_gn, qkv = pl.pallas_call(
        functools.partial(tokens_back_kernel, 1.0 / pts_size),
        out_shape=[shape_of((40, 128), F32), shape_of((HEAD_DIM, 128), F32)],
        compiler_params=params,
        cost_estimate=cost(4),
        name="tokens_back",
    )(nd, gt, *got, wq, wk, wv)
    got = pulls(own_gn, "dz")
    own_gn, wsum, wlow = tie(own_gn, wsum, wlow)
    if pts_size > 1:
        wsum = rounded(wsum) + pull(wlow, dc=1).astype(F32)
        wlow = lax.dynamic_slice_in_dim(wsum, core * C, C, 0).astype(BF)
    got, wlow = tie(got, wlow)
    wgot = axis_peers(wlow[:C], "dx")
    got, near = tie(got, near)
    near2 = [pull(near[0][:half], dz=1), pull(near[1][half:], dz=3)]
    gnums = [own_gn] + list(got)

    result = points_call(tokens, gnums, wt, mid, gspread, gres, qkv, g2, gout)
    gpts, low_a, low_b, outs = result[0], result[1], result[2], result[3:]
    gpts, outs, low_a, low_b, wgot, near2 = tie(gpts, outs, low_a, low_b, wgot, near2)

    got = [pull(outs[BLOCKS - k], dz=k) for k in (1, 2, 3)]
    a1, b3 = pull(low_a, dz=1), pull(low_b, dz=3)
    outs, mixed = tie(outs, mixed)
    mixed = fill_call(lambda i: 2 + i, halves_of(near[0]) + whole(*near2), mixed)
    got, mixed = tie(got, mixed)
    tail = core_sum(add4(outs[0], got))
    both = jnp.concatenate([tail, add4(wlow[:C].astype(F32), wgot)], 0).astype(BF)
    both, a1, b3 = tie(both, a1, b3)
    far2 = [pull(a1, dz=1), pull(b3, dz=3)]
    got = axis_peers(both, "dy")
    both, mixed = tie(both, mixed)
    mixed = fill_call(lambda i: 6 + i, halves_of(near[1]), mixed)
    got, mixed, far2 = tie(got, mixed, far2)
    both = add4(both.astype(F32), got)
    both, low_a, low_b = tie(both, low_a, low_b)
    b1, a3 = pull(low_b, dz=1), pull(low_a, dz=3)
    tail, wsum = both[:TAIL].astype(BF), both[TAIL:]
    if pts_size > 1:
        other = pull(wsum, dc=1)
    else:
        other = wlow[C:].astype(F32)
    wsum, other, tail = tie(wsum, other, tail)
    got = axis_peers(tail, "dx")
    tail, gpts = tie(tail, gpts)
    gpts = fill_call(
        lambda i: 2 + i + jnp.minimum(i, 1) + i // 3, whole(a1, *far2, b3), gpts
    )
    got, gpts, b1, a3 = tie(got, gpts, b1, a3)
    shapes = [(64, C), (32, 64), (1, GH), (32, 32), (32, 32), (32, 32)]
    shapes += [(64, C), (C, C), (C, C), (1, C), (1, C)]
    result = pl.pallas_call(
        finish_kernel,
        grid_spec=grid(
            (2,),
            [full((half, C))] * 2 + [any_spec] + [full((TAIL, C))] * 4 + [full((C, C))] * 2,
            [fill_out(lambda i: 3 + 3 * i)] + [full(s) for s in shapes],
        ),
        out_shape=[shape_of((rows, C), F32)] + [shape_of(s, F32) for s in shapes],
        input_output_aliases={3: 0},
        compiler_params=params,
        cost_estimate=cost(4),
        name="finish",
    )(z, b1, a3, gpts, tail, *got, wsum, other)
    gpts, gin, gslice, gsharp, gq, gk, gv, gout, gup, gdown, g1, g2 = result
    return (
        mixed, gpts, gin.T, gslice, gsharp.reshape(GH), gq, gk, gv, gout, gup, gdown,
        g1.reshape(C), g2.reshape(C),
    )


def solution(mesh):
    row, none, cols, heads = P("pts", None), P(), P(None, "head"), P("head")
    down = P("head", None)
    placed = (row, row, none, cols, none, heads, none, none, none, down, none, cols, down)
    given = (row, row, cols, none, heads, none, none, none, down, cols, down, none, none)
    return jax.shard_map(
        functools.partial(local, mesh.shape["pts"]),
        mesh=mesh,
        in_specs=placed,
        out_specs=given,
        check_vma=False,
    )
```

```python
import functools
import jax
import jax.numpy as jnp
from jax import lax
from jax.experimental import pallas as pl
from jax.experimental.pallas import tpu as pltpu
from jax.sharding import PartitionSpec as P

HEAD_DIM = 32
SLICES = 64
C = 256
HEADS = 8
BLOCKS = 4
GH = HEADS // BLOCKS
HM = HEADS * SLICES
C0 = 0.7978845608028654
C1 = 0.7978845608028654 * 0.044715
BF = jnp.bfloat16
F32 = jnp.float32
VMEM_LIMIT = 56 * 1024 * 1024


def dot(a, b, precision=None):
    return lax.dot_general(
        a, b, (((1,), (0,)), ((), ())), preferred_element_type=F32, precision=precision
    )


def dot_nt(a, b, precision=None):
    return lax.dot_general(
        a, b, (((1,), (1,)), ((), ())), preferred_element_type=F32, precision=precision
    )


def norm_parts(value):
    centred = value - jnp.mean(value, -1, keepdims=True)
    scale = lax.rsqrt(jnp.mean(centred * centred, -1, keepdims=True) + 1e-05)
    return centred * scale, scale


def norm_back_rows(grad, normed, scale, gain):
    scaled = grad * gain
    return scale * (
        scaled
        - jnp.mean(scaled, -1, keepdims=True)
        - normed * jnp.mean(scaled * normed, -1, keepdims=True)
    )


def sharp_row(block, which, width):
    row = block[which : which + 1, :].astype(F32)
    return jnp.concatenate([row] * (width // C), axis=1)


def softmax_slices(raw, sharp):
    logits = raw * sharp
    grown = jnp.exp(logits - jnp.max(logits, 0, keepdims=True))
    return grown * (1.0 / jnp.sum(grown, 0, keepdims=True))


def fold_rows(value):
    return jnp.sum(value.reshape(value.shape[0] // 8, 8, value.shape[1]), 0)


def prep_kernel(
    w_up, w_down, w_in, w_out, sharp, slice_weight, one, two, pack, slices_t, slices, gain1, gain2, s_scr
):
    gain1[...] = one[...].astype(F32).reshape(1, C)
    gain2[...] = two[...].astype(F32).reshape(1, C)
    pack[0:256, :] = w_up[...].T
    pack[256:512, :] = w_down[...]
    pack[512:576, :] = w_in[...]
    pack[576:640, :] = w_out[...]
    row = lax.broadcasted_iota(jnp.int32, (16, C), 0)
    both = sharp[...].astype(F32).reshape(1, GH)
    pack[640:656, :] = jnp.where(row == 0, both[:, 0:1], both[:, 1:2]).astype(BF)
    s_scr[...] = jnp.zeros_like(s_scr)
    weight = slice_weight[...].astype(F32)
    twice = jnp.concatenate([weight, weight], 1)
    lane = lax.broadcasted_iota(jnp.int32, (HEAD_DIM, 128), 1)
    for k in range(BLOCKS):
        at = slice(k * 128, (k + 1) * 128)
        s_scr[k * 64 : k * 64 + 32, at] = jnp.where(lane < SLICES, twice, 0.0)
        s_scr[k * 64 + 32 : k * 64 + 64, at] = jnp.where(lane < SLICES, 0.0, twice)
    slices[...] = s_scr[...].astype(BF)
    slices_t[...] = s_scr[...].T.astype(BF)


def fill_kernel(z, *refs):
    out = refs[-1]
    for k, ref in enumerate(refs[:-2]):

        @pl.when(pl.program_id(0) == k)
        def _():
            out[...] = ref[...].astype(F32)


def finish_kernel(z, first, second, before, t0, t1, t2, t3, w0, w1, *refs):
    out, gin, gslice, gsharp, gq, gk, gv, gout, gup, gdown, g1, g2 = refs
    fill_kernel(z, first, second, before, out)

    @pl.when(pl.program_id(0) == 0)
    def _():
        a, b, c, d = (t[...].astype(F32) for t in (t0, t1, t2, t3))
        tail = (a + c) + (b + d)
        gin[...] = tail[0:64]
        gslice[...] = tail[64:96, 0:64] + tail[64:96, 64:128]
        gq[...] = tail[64:96, 128:160]
        gk[...] = tail[64:96, 160:192]
        gv[...] = tail[64:96, 192:224]
        gsharp[...] = jnp.concatenate(
            [
                jnp.sum(tail[96:97, 0:128], 1, keepdims=True),
                jnp.sum(tail[96:97, 128:256], 1, keepdims=True),
            ],
            1,
        )
        g1[...] = tail[97:98]
        g2[...] = tail[98:99]
        gout[...] = tail[112:176]

        @pl.when(z[1] == 0)
        def _():
            gdown[...] = w0[...].T
            gup[...] = w1[...]

        @pl.when(z[1] == 1)
        def _():
            gdown[...] = w1[...].T
            gup[...] = w0[...]


def own_sums_kernel(pts, gain, w_in, spread_slices, sharp, out, acc, den):
    step = pl.program_id(0)

    @pl.when(step == 0)
    def _():
        acc[...] = jnp.zeros_like(acc)
        den[...] = jnp.zeros_like(den)

    normed, _ = norm_parts(pts[...].astype(F32))
    normed_in = (normed * gain[...].astype(F32)).astype(BF)
    middle = dot_nt(normed_in, w_in[...]).astype(BF)
    raw = dot_nt(spread_slices[:, 0:64], middle)
    rows = raw.shape[1]
    sharps = sharp[...]
    parts = [
        softmax_slices(raw[h * SLICES : (h + 1) * SLICES], sharp_row(sharps, h, rows))
        for h in range(GH)
    ]
    weights = jnp.concatenate(parts, 0)
    total = weights[:, 0:128]
    for j in range(1, rows // 128):
        total = total + weights[:, j * 128 : (j + 1) * 128]
    den[...] += total
    acc[...] += dot(weights.astype(BF), middle)

    @pl.when(step == pl.num_programs(0) - 1)
    def _():
        flipped = acc[...].T
        lane = lax.broadcasted_iota(jnp.int32, (HEAD_DIM, 128), 1)
        out[0:HEAD_DIM, :] = jnp.where(lane < SLICES, flipped[:HEAD_DIM], flipped[HEAD_DIM:])
        row = jnp.sum(den[...].T, 0, keepdims=True)
        out[HEAD_DIM : HEAD_DIM + 8, :] = jnp.broadcast_to(row, (8, 128))


def weights_kernel(z, pts, gain, in0, in1, in2, in3, spread_slices, s0, s1, s2, s3, *rest):
    wt, mid, w_in = rest

    @pl.when(pl.program_id(0) == 0)
    def _():
        for k, ref in enumerate((in0, in1, in2, in3)):
            w_in[k * 64 : (k + 1) * 64, :] = ref[...]

    normed, _ = norm_parts(pts[...].astype(F32))
    normed_in = (normed * gain[...].astype(F32)).astype(BF)
    middle = dot_nt(normed_in, w_in[...]).astype(BF)
    mid[...] = middle
    raw = dot_nt(spread_slices[...], middle)
    rows = raw.shape[1]
    for h in range(HEADS):
        sharp = sharp_row((s0, s1, s2, s3)[h // GH][...], h % GH, rows)
        wt[h * SLICES : (h + 1) * SLICES, :] = softmax_slices(
            raw[h * SLICES : (h + 1) * SLICES], sharp
        ).astype(BF)


def place_tokens(flat, tokens):
    flat[...] = jnp.zeros_like(flat)
    lane = lax.broadcasted_iota(jnp.int32, (HEAD_DIM, 128), 1)
    for k, ref in enumerate(tokens):
        t = ref[0:HEAD_DIM, :]
        flat[k * 64 : k * 64 + 32, k * 128 : (k + 1) * 128] = jnp.where(lane < SLICES, t, 0.0)
        flat[k * 64 + 32 : k * 64 + 64, k * 128 : (k + 1) * 128] = jnp.where(
            lane < SLICES, 0.0, t
        )


def own_block(flipped, k):
    lane = lax.broadcasted_iota(jnp.int32, (HEAD_DIM, 128), 1)
    block = flipped[k * 64 : (k + 1) * 64, k * 128 : (k + 1) * 128]
    return jnp.where(lane < SLICES, block[:HEAD_DIM], block[HEAD_DIM:])


def mlp_kernel(z, pts, cot, wt, *refs):
    tokens, refs = refs[:4], refs[4:]
    gain, refs = refs[0], refs[1:]
    ups, downs, outs, refs = refs[:4], refs[4:8], refs[8:12], refs[12:]
    mixed, gres, gspread, low_mixed, gt0, gt1, gt2, gt3, wg0, wg1, wg2, wg3, gout, g2 = refs[:14]
    flat, tok_t, w_out, acc_tok, acc_w = refs[14:]
    step = pl.program_id(0)

    @pl.when(step == 0)
    def _():
        place_tokens(flat, tokens)
        tok_t[...] = flat[...].astype(BF)
        for k, ref in enumerate(outs):
            w_out[k * 64 : (k + 1) * 64, :] = ref[...]
        acc_tok[...] = jnp.zeros_like(acc_tok)
        acc_w[...] = jnp.zeros_like(acc_w)
        gout[...] = jnp.zeros_like(gout)
        g2[...] = jnp.zeros_like(g2)

    weights = wt[...]
    spread_t = dot(tok_t[...], weights).astype(BF)
    spread = spread_t.T
    resid = pts[...].astype(F32) + dot(spread, w_out[...])
    normed, scale = norm_parts(resid)
    gain_row = gain[...].astype(F32)
    normed_mid = (normed * gain_row).astype(BF)
    cotangent = cot[...]
    total = resid
    gmid = None
    cot_t = cotangent.T
    normed_t = normed_mid.T
    for k in range(BLOCKS):
        up, down = ups[k][...], downs[k][...]
        hidden = dot_nt(normed_mid, up)
        square = hidden * hidden
        inner = jnp.tanh(hidden * (C0 + C1 * square))
        half = 0.5 + 0.5 * inner
        gelu = hidden * half
        active = gelu.astype(BF)
        total = total + dot(active, down)
        slope = half + gelu * (1.0 - half) * (2.0 * C0 + 6.0 * C1 * square)
        ghid = (dot_nt(cotangent, down) * slope).astype(BF)
        part = dot(ghid, up)
        gmid = part if gmid is None else gmid + part
        acc_w[k, 0:C, :] += dot(cot_t, active)
        acc_w[k, C : 2 * C, :] += dot(normed_t, ghid)
    mixed[...] = total
    grad = cotangent.astype(F32) + norm_back_rows(gmid, normed, scale, gain_row)
    low = grad.astype(BF)
    gres[...] = low
    gsp = dot_nt(low, w_out[...]).astype(BF)
    gspread[...] = gsp
    low_mixed[...] = total.astype(BF)
    acc_tok[...] += dot(weights, gsp)
    gout[...] += dot(spread_t, low)
    g2[...] += fold_rows(gmid * normed)

    @pl.when(step == pl.num_programs(0) - 1)
    def _():
        flipped = acc_tok[...].T
        for k, ref in enumerate((gt0, gt1, gt2, gt3)):
            ref[...] = own_block(flipped, k)
        for k, ref in enumerate((wg0, wg1, wg2, wg3)):
            ref[...] = acc_w[k].astype(ref.dtype)


def points_kernel(z, pts, wt, mid, gspread, gres, *refs):
    tokens, gnums, refs = refs[:4], refs[4:8], refs[8:]
    gain, slices_t, slices, refs = refs[0], refs[1], refs[2], refs[3:]
    ins, sharps, refs = refs[:4], refs[4:8], refs[8:]
    qkv, g2, gout, gpts, low_a, low_b, o0, o1, o2, o3 = refs[:10]
    flat, tok, gn_t, gn, gden, w_in, acc_in, acc_s, acc_g, acc_h = refs[10:]
    step = pl.program_id(0)

    @pl.when(step == 0)
    def _():
        place_tokens(flat, tokens)
        tok[...] = flat[...].T.astype(BF)
        place_tokens(flat, gnums)
        gn_t[...] = flat[...].astype(BF)
        gn[...] = flat[...].T.astype(BF)
        for k, ref in enumerate(gnums):
            row = ref[HEAD_DIM : HEAD_DIM + 1, :]
            gden[k * 128 : (k + 1) * 128, :] = jnp.broadcast_to(row, (128, 128)).T
        for k, ref in enumerate(ins):
            w_in[k * 64 : (k + 1) * 64, :] = ref[...]
        acc_in[...] = jnp.zeros_like(acc_in)
        acc_s[...] = jnp.zeros_like(acc_s)
        acc_g[...] = jnp.zeros_like(acc_g)
        acc_h[...] = jnp.zeros_like(acc_h)

    normed, scale = norm_parts(pts[...].astype(F32))
    gain_row = gain[...].astype(F32)
    weights = wt[...]
    middle = mid[...]
    rows = weights.shape[1]
    gw = dot_nt(tok[...], gspread[...]) + dot_nt(gn[...], middle)
    pieces, sharp_sums = [], []
    raw = dot_nt(slices_t[...], middle)
    for h in range(HEADS):
        at = slice(h * SLICES, (h + 1) * SLICES)
        sharp = sharp_row(sharps[h // GH][...], h % GH, rows)
        w = softmax_slices(raw[at], sharp)
        g = gw[at] + jnp.concatenate([gden[at, :]] * (rows // 128), axis=1)
        gl = w * (g - jnp.sum(w * g, 0, keepdims=True))
        pieces.append((gl * sharp).astype(BF))
        sharp_sums.append(jnp.sum(gl * raw[at], 0, keepdims=True))
    graw = jnp.concatenate(pieces, 0)
    gmid_t = (dot(gn_t[...], weights) + dot(slices[...], graw)).astype(BF)
    gmid = gmid_t.T
    gnormed = dot(gmid, w_in[...])
    result = gres[...].astype(F32) + norm_back_rows(gnormed, normed, scale, gain_row)
    gpts[...] = result

    @pl.when(step < pl.num_programs(0) // 2)
    def _():
        low_a[...] = result.astype(BF)

    @pl.when(step >= pl.num_programs(0) // 2)
    def _():
        low_b[...] = result.astype(BF)

    normed_in = (normed * gain_row).astype(BF)
    acc_in[...] += dot(gmid_t, normed_in)
    acc_s[...] += dot(graw, middle)
    acc_g[...] += fold_rows(gnormed * normed)
    acc_h[...] += jnp.concatenate(sharp_sums, 0)

    @pl.when(step == pl.num_programs(0) - 1)
    def _():
        flipped = acc_s[...].T
        gsharp = acc_h[:, 0:128]
        for j in range(1, rows // 128):
            gsharp = gsharp + acc_h[:, j * 128 : (j + 1) * 128]
        gslice = jnp.zeros((HEAD_DIM, 128), F32)
        for k in range(BLOCKS):
            gslice = gslice + own_block(flipped, k)
        gain1 = jnp.sum(acc_g[...], 0, keepdims=True)
        gain2 = jnp.sum(g2[...], 0, keepdims=True)
        for k, ref in enumerate((o0, o1, o2, o3)):
            ref[0:64, :] = acc_in[k * 64 : (k + 1) * 64, :].astype(ref.dtype)
            ref[64:96, 0:128] = gslice.astype(ref.dtype)
            ref[64:96, 128:256] = qkv[...].astype(ref.dtype)
            wide = jnp.concatenate([gsharp[2 * k : 2 * k + 1], gsharp[2 * k + 1 : 2 * k + 2]], 1)
            ref[96:112, :] = jnp.concatenate(
                [wide, gain1, gain2, jnp.zeros((13, C), F32)], 0
            ).astype(ref.dtype)
            ref[112:176, :] = gout[k * 64 : (k + 1) * 64, :].astype(ref.dtype)


def halves(value):
    high = value.astype(BF)
    return high, (value - high.astype(F32)).astype(BF)


def dot3(a, b, form=dot):
    (ah, al), (bh, bl) = halves(a), halves(b)
    return form(ah, bh) + (form(ah, bl) + form(al, bh))


def dot3_nt(a, b):
    return dot3(a, b, dot_nt)


def token_parts(nd, wq, wk, wv):
    padded = jnp.concatenate([nd, jnp.zeros((88, 128), F32)], 0).T
    denom = padded[:, HEAD_DIM : HEAD_DIM + 1]
    tok = padded[:, :HEAD_DIM] / denom
    q, k, v = dot3(tok, wq), dot3(tok, wk), dot3(tok, wv)
    scores = dot3_nt(q, k) * (1.0 / HEAD_DIM**0.5)
    row = lax.broadcasted_iota(jnp.int32, (128, 128), 0) < SLICES
    col = lax.broadcasted_iota(jnp.int32, (128, 128), 1) < SLICES
    same = row == col
    scores = jnp.where(same, scores, -jnp.inf)
    p = jnp.exp(scores - jnp.max(scores, -1, keepdims=True))
    p = p / jnp.sum(p, -1, keepdims=True)
    return denom, tok, q, k, v, p


def flip(value):
    n = value.shape[1]
    return jnp.concatenate([value, jnp.zeros((128, 128 - n), F32)], 1).T[:n]


def tokens_kernel(a, b, c, d, wq, wk, wv, total, tokens):
    nd = (a[...] + c[...]) + (b[...] + d[...])
    total[...] = nd
    _, _, _, _, v, p = token_parts(nd, *(w[...].astype(F32) for w in (wq, wk, wv)))
    mixed = dot3(p, v).astype(BF).astype(F32)
    tokens[...] = flip(mixed)


def tokens_back_kernel(scale, nd, a, b, c, d, wq, wk, wv, gn, qkv):
    gt = (a[...] + c[...]) + (b[...] + d[...])
    g = jnp.concatenate([gt, jnp.zeros((96, 128), F32)], 0).T[:, :HEAD_DIM]
    wq, wk, wv = (w[...].astype(F32) for w in (wq, wk, wv))
    denom, tok, q, k, v, p = token_parts(nd[...], wq, wk, wv)
    dv = dot3(p.T, g)
    dp = dot3_nt(g, v)
    ds = p * (dp - jnp.sum(p * dp, -1, keepdims=True)) * (1.0 / HEAD_DIM**0.5)
    dq = dot3(ds, k)
    dk = dot3(ds.T, q)
    gmt = dot3_nt(dq, wq) + dot3_nt(dk, wk) + dot3_nt(dv, wv)
    gnum = (gmt / denom).astype(BF).astype(F32)
    gden = -jnp.sum(gmt * tok, -1, keepdims=True) / denom
    gn[0:HEAD_DIM, :] = flip(gnum)
    gn[HEAD_DIM : HEAD_DIM + 8, :] = flip(jnp.broadcast_to(gden, (128, 8)))
    tok_t = flip(tok)
    qkv[...] = scale * jnp.concatenate(
        [dot3(tok_t, dq), dot3(tok_t, dk), dot3(tok_t, dv), jnp.zeros((32, 32), F32)],
        1,
    )


def full(shape):
    return pl.BlockSpec(shape, lambda *_: (0,) * len(shape))


def part(shape, row):
    return pl.BlockSpec(shape, lambda *_: (row, 0))


def shape_of(shape, dtype):
    return jax.ShapeDtypeStruct(shape, dtype)


def cost(us):
    return pl.CostEstimate(flops=int(us * 1.0e6), bytes_accessed=1024, transcendentals=0)


UP, DOWN, WIN, WOUT, SHARP = (256, 0), (256, 1), (64, 8), (64, 9), (16, 40)
WIDE, NARROW = 1024, 512
TAIL = 176


def pack_specs(kind):
    return [part((kind[0], C), kind[1])] * BLOCKS


def local(
    pts_size,
    points,
    cotangent,
    gain_one,
    w_in,
    slice_weight,
    sharp,
    w_query,
    w_key,
    w_value,
    w_out,
    gain_two,
    w_up,
    w_down,
):
    axes = ("pts", "head")
    rows = points.shape[0]
    quarter = rows // BLOCKS

    def pull(value, dx=0, dy=0, dc=0, dz=0):
        pairs = []
        for p in range(pts_size):
            x, y, c = p // 8, (p // 2) % 4, p % 2
            there = p
            if pts_size > 1:
                there = (((x + dx) % 4) * 4 + (y + dy) % 4) * 2 + (c + dc) % 2
            for z in range(BLOCKS):
                pairs.append((there * BLOCKS + (z + dz) % BLOCKS, p * BLOCKS + z))
        return lax.ppermute(value, axes, pairs)

    def pulls(value, axis):
        return [pull(value, **{axis: k}) for k in (1, 2, 3)]

    def tie(*values):
        return lax.optimization_barrier(values)

    def add4(a, r):
        return (a + r[1].astype(F32)) + (r[0].astype(F32) + r[2].astype(F32))

    def core_sum(value):
        return value + pull(value, dc=1) if pts_size > 1 else value

    def rounded(value):
        return lax.reduce_precision(value, 8, 7)

    def axis_peers(value, axis):
        if pts_size == 1:
            return [jnp.zeros_like(value)] * 3
        return pulls(value, axis)

    core = lax.axis_index("pts").astype(jnp.int32) % 2
    z = jnp.stack([lax.axis_index("head").astype(jnp.int32), core])

    def row_spec(size, away, first=0):
        n = quarter // size
        return pl.BlockSpec(
            (size, C), lambda i, z: (lax.rem(z[0] + away, BLOCKS) * n + first // size + i, 0)
        )

    def own_spec(size, first=0):
        return pl.BlockSpec((size, C), lambda i, z: (first // size + i, 0))

    def own_cols(size, first=0):
        return pl.BlockSpec((HM, size), lambda i, z: (0, first // size + i))

    def grid(steps, in_specs, out_specs, scratch=()):
        return pltpu.PrefetchScalarGridSpec(
            num_scalar_prefetch=1,
            grid=steps,
            in_specs=in_specs,
            out_specs=out_specs,
            scratch_shapes=scratch,
        )

    any_spec = pl.BlockSpec(memory_space=pl.ANY)
    params = pltpu.CompilerParams(vmem_limit_bytes=VMEM_LIMIT)

    wq, wk, wv = w_query, w_key, w_value
    pack, slices_t, slices, gain1, gain2 = pl.pallas_call(
        prep_kernel,
        out_shape=[shape_of((656, C), BF), shape_of((HM, C), BF), shape_of((C, HM), BF)]
        + [shape_of((1, C), F32)] * 2,
        scratch_shapes=[pltpu.VMEM((C, HM), F32)],
        compiler_params=params,
        cost_estimate=cost(2),
        name="prep",
    )(w_up, w_down, w_in.T, w_out, sharp, slice_weight, gain_one, gain_two)

    nd = pl.pallas_call(
        own_sums_kernel,
        grid=(rows // (2 * WIDE),),
        in_specs=[
            pl.BlockSpec((2 * WIDE, C), lambda i: (i, 0)),
            full((1, C)),
            part((64, C), WIN[1]),
            part((128, C), 0),
            part((16, C), SHARP[1]),
        ],
        out_specs=full((40, 128)),
        out_shape=shape_of((40, 128), F32),
        scratch_shapes=[pltpu.VMEM((128, 64), F32), pltpu.VMEM((128, 128), F32)],
        compiler_params=params,
        cost_estimate=cost(8),
        name="own_sums",
    )(points, gain1, pack, slices_t, pack)

    half = quarter // 2

    def weights_call():
        return pl.pallas_call(
            weights_kernel,
            grid_spec=grid(
                (quarter // WIDE,),
                [row_spec(WIDE, 0), full((1, C))]
                + pack_specs(WIN)
                + [full((HM, C))]
                + pack_specs(SHARP),
                [own_cols(WIDE), own_spec(WIDE)],
                [pltpu.VMEM((C, C), BF)],
            ),
            out_shape=[shape_of((HM, quarter), BF), shape_of((quarter, C), BF)],
            compiler_params=params,
            cost_estimate=cost(5),
            name="weights",
        )(z, points, gain1, *packs, slices_t, *packs)

    def mlp_call(tokens, wt):
        size = WIDE
        out_shape = [shape_of((rows, C), F32)] + [shape_of((quarter, C), BF)] * 3
        out_shape += [shape_of((HEAD_DIM, 128), F32)] * 4
        out_shape += [shape_of((2 * C, C), F32)] + [shape_of((2 * C, C), BF)] * 3
        out_shape += [shape_of((C, C), F32), shape_of((8, C), F32)]
        out_specs = [row_spec(size, 0)] + [own_spec(size)] * 3
        out_specs += [full((HEAD_DIM, 128))] * 4 + [full((2 * C, C))] * 4
        out_specs += [full((C, C)), full((8, C))]
        return pl.pallas_call(
            mlp_kernel,
            grid_spec=grid(
                (quarter // size,),
                [row_spec(size, 0), row_spec(size, 0), own_cols(size)]
                + [full((HEAD_DIM, 128))] * 4
                + [full((1, C))]
                + pack_specs(UP)
                + pack_specs(DOWN)
                + pack_specs(WOUT),
                out_specs,
                [
                    pltpu.VMEM((C, HM), F32),
                    pltpu.VMEM((C, HM), BF),
                    pltpu.VMEM((C, C), BF),
                    pltpu.VMEM((HM, C), F32),
                    pltpu.VMEM((BLOCKS, 2 * C, C), F32),
                ],
            ),
            out_shape=out_shape,
            compiler_params=params,
            cost_estimate=cost(16),
            name="mlp",
        )(z, points, cotangent, wt, *tokens, gain2, *packs, *packs, *packs)

    half = quarter // 2

    def points_call(tokens, gnums, wt, mid, gspread, gres, qkv, g2, gout):
        size = half
        steps = quarter // size
        halves = [full((half, C))] * 2
        return pl.pallas_call(
            points_kernel,
            grid_spec=grid(
                (steps,),
                [row_spec(size, 0), own_cols(size)]
                + [own_spec(size)] * 3
                + [full((HEAD_DIM, 128))] * 4
                + [full((40, 128))] * 4
                + [full((1, C)), full((HM, C)), full((C, HM))]
                + pack_specs(WIN)
                + pack_specs(SHARP)
                + [full((HEAD_DIM, 128)), full((8, C)), full((C, C))],
                [row_spec(size, 0)] + halves + [full((TAIL, C))] * 4,
                [
                    pltpu.VMEM((C, HM), F32),
                    pltpu.VMEM((HM, C), BF),
                    pltpu.VMEM((C, HM), BF),
                    pltpu.VMEM((HM, C), BF),
                    pltpu.VMEM((HM, 128), F32),
                    pltpu.VMEM((C, C), BF),
                    pltpu.VMEM((C, C), F32),
                    pltpu.VMEM((HM, C), F32),
                    pltpu.VMEM((8, C), F32),
                    pltpu.VMEM((HEADS, size), F32),
                ],
            ),
            out_shape=[shape_of((rows, C), F32)]
            + [shape_of((half, C), BF)] * 2
            + [shape_of((TAIL, C), F32)]
            + [shape_of((TAIL, C), BF)] * 3,
            compiler_params=params,
            cost_estimate=cost(12),
            name="points",
        )(
            z, points, wt, mid, gspread, gres, *tokens, *gnums, gain1, slices_t, slices,
            *packs, *packs, qkv, g2, gout
        )

    def fill_out(at):
        return pl.BlockSpec(
            (half, C), lambda i, z: (lax.rem(2 * z[0] + at(i), 2 * BLOCKS), 0)
        )

    def fill_call(at, parts, before):
        n = len(parts)
        return pl.pallas_call(
            fill_kernel,
            grid_spec=grid((n,), [s for _, s in parts] + [any_spec], fill_out(at)),
            out_shape=shape_of((rows, C), F32),
            input_output_aliases={n + 1: 0},
            compiler_params=params,
            cost_estimate=cost(3),
            name="fill",
        )(z, *[p for p, _ in parts], before)

    def halves_of(value):
        return [(value, part((half, C), 0)), (value, part((half, C), 1))]

    def whole(*values):
        return [(v, full((half, C))) for v in values]

    nd = core_sum(nd)
    nd, sent = tie(nd, pack)
    got = axis_peers(nd, "dx")
    packs = [pack, pull(sent, dz=1), None, pull(sent, dz=3)]
    nd = add4(nd, got)
    nd, sent = tie(nd, sent)
    got = axis_peers(nd, "dy")
    packs[2] = pull(sent, dz=2)
    nd, own_tokens = pl.pallas_call(
        tokens_kernel,
        out_shape=[shape_of((40, 128), F32), shape_of((HEAD_DIM, 128), F32)],
        compiler_params=params,
        cost_estimate=cost(3),
        name="tokens",
    )(nd, *got, wq, wk, wv)
    got = pulls(own_tokens, "dz")

    own_tokens, *packs = tie(own_tokens, *packs)
    wt, mid = weights_call()
    got, wt = tie(got, wt)
    tokens = [own_tokens] + list(got)

    result = mlp_call(tokens, wt)
    mixed, gres, gspread, send = result[:4]
    gts, wgs, (gout, g2) = result[4:8], result[8:12], result[12:]

    got = [pull(gts[BLOCKS - k], dz=k) for k in (1, 2, 3)]
    wgot = [pull(wgs[3], dz=1), pull(wgs[2], dz=2)]
    gt = add4(gts[0], got)
    gt, wg1 = tie(gt, wgs[1])
    wgot.append(pull(wg1, dz=3))
    gt = core_sum(gt)
    gt, send = tie(gt, send)
    got = axis_peers(gt, "dx")
    near = [pull(send, dz=1), pull(send, dz=3)]
    got, wgot = tie(got, wgot)
    gt = add4(gt, got)
    got = axis_peers(gt, "dy")
    wsum = add4(wgs[0], wgot)
    wlow = wsum.astype(BF)
    own_gn, qkv = pl.pallas_call(
        functools.partial(tokens_back_kernel, 1.0 / pts_size),
        out_shape=[shape_of((40, 128), F32), shape_of((HEAD_DIM, 128), F32)],
        compiler_params=params,
        cost_estimate=cost(4),
        name="tokens_back",
    )(nd, gt, *got, wq, wk, wv)
    got = pulls(own_gn, "dz")
    own_gn, wsum, wlow = tie(own_gn, wsum, wlow)
    if pts_size > 1:
        wsum = rounded(wsum) + pull(wlow, dc=1).astype(F32)
        wlow = lax.dynamic_slice_in_dim(wsum, core * C, C, 0).astype(BF)
    got, wlow = tie(got, wlow)
    wgot = axis_peers(wlow[:C], "dx")
    got, near = tie(got, near)
    near2 = [pull(near[0][:half], dz=1), pull(near[1][half:], dz=3)]
    gnums = [own_gn] + list(got)

    result = points_call(tokens, gnums, wt, mid, gspread, gres, qkv, g2, gout)
    gpts, low_a, low_b, outs = result[0], result[1], result[2], result[3:]
    gpts, outs, low_a, low_b, wgot, near2 = tie(gpts, outs, low_a, low_b, wgot, near2)

    got = [pull(outs[BLOCKS - k], dz=k) for k in (1, 2, 3)]
    a1, b3 = pull(low_a, dz=1), pull(low_b, dz=3)
    outs, mixed = tie(outs, mixed)
    mixed = fill_call(lambda i: 2 + i, halves_of(near[0]) + whole(*near2), mixed)
    got, mixed = tie(got, mixed)
    tail = core_sum(add4(outs[0], got))
    both = jnp.concatenate([tail, add4(wlow[:C].astype(F32), wgot)], 0).astype(BF)
    both, a1, b3 = tie(both, a1, b3)
    far2 = [pull(a1, dz=1), pull(b3, dz=3)]
    got = axis_peers(both, "dy")
    both, mixed = tie(both, mixed)
    mixed = fill_call(lambda i: 6 + i, halves_of(near[1]), mixed)
    got, mixed, far2 = tie(got, mixed, far2)
    both = add4(both.astype(F32), got)
    both, low_a, low_b = tie(both, low_a, low_b)
    b1, a3 = pull(low_b, dz=1), pull(low_a, dz=3)
    tail, wsum = both[:TAIL].astype(BF), both[TAIL:]
    if pts_size > 1:
        other = pull(wsum, dc=1)
    else:
        other = wlow[C:].astype(F32)
    wsum, other, tail = tie(wsum, other, tail)
    got = axis_peers(tail, "dx")
    tail, gpts = tie(tail, gpts)
    gpts = fill_call(
        lambda i: 2 + i + jnp.minimum(i, 1) + i // 3, whole(a1, *far2, b3), gpts
    )
    got, gpts, b1, a3 = tie(got, gpts, b1, a3)
    shapes = [(64, C), (32, 64), (1, GH), (32, 32), (32, 32), (32, 32)]
    shapes += [(64, C), (C, C), (C, C), (1, C), (1, C)]
    result = pl.pallas_call(
        finish_kernel,
        grid_spec=grid(
            (2,),
            [full((half, C))] * 2 + [any_spec] + [full((TAIL, C))] * 4 + [full((C, C))] * 2,
            [fill_out(lambda i: 3 + 3 * i)] + [full(s) for s in shapes],
        ),
        out_shape=[shape_of((rows, C), F32)] + [shape_of(s, F32) for s in shapes],
        input_output_aliases={3: 0},
        compiler_params=params,
        cost_estimate=cost(4),
        name="finish",
    )(z, b1, a3, gpts, tail, *got, wsum, other)
    gpts, gin, gslice, gsharp, gq, gk, gv, gout, gup, gdown, g1, g2 = result
    return (
        mixed, gpts, gin.T, gslice, gsharp.reshape(GH), gq, gk, gv, gout, gup, gdown,
        g1.reshape(C), g2.reshape(C),
    )


def solution(mesh):
    row, none, cols, heads = P("pts", None), P(), P(None, "head"), P("head")
    down = P("head", None)
    placed = (row, row, none, cols, none, heads, none, none, none, down, none, cols, down)
    given = (row, row, cols, none, heads, none, none, none, down, cols, down, none, none)
    return jax.shard_map(
        functools.partial(local, mesh.shape["pts"]),
        mesh=mesh,
        in_specs=placed,
        out_specs=given,
        check_vma=False,
    )
```

```python
import functools
import jax
import jax.numpy as jnp
from jax import lax
from jax.experimental import pallas as pl
from jax.experimental.pallas import tpu as pltpu
from jax.sharding import PartitionSpec as P

HEAD_DIM = 32
SLICES = 64
C = 256
HEADS = 8
BLOCKS = 4
GH = HEADS // BLOCKS
HM = HEADS * SLICES
C0 = 0.7978845608028654
C1 = 0.7978845608028654 * 0.044715
BF = jnp.bfloat16
F32 = jnp.float32
VMEM_LIMIT = 56 * 1024 * 1024


def dot(a, b, precision=None):
    return lax.dot_general(
        a, b, (((1,), (0,)), ((), ())), preferred_element_type=F32, precision=precision
    )


def dot_nt(a, b, precision=None):
    return lax.dot_general(
        a, b, (((1,), (1,)), ((), ())), preferred_element_type=F32, precision=precision
    )


def norm_parts(value):
    centred = value - jnp.mean(value, -1, keepdims=True)
    scale = lax.rsqrt(jnp.mean(centred * centred, -1, keepdims=True) + 1e-05)
    return centred * scale, scale


def norm_back_rows(grad, normed, scale, gain):
    scaled = grad * gain
    return scale * (
        scaled
        - jnp.mean(scaled, -1, keepdims=True)
        - normed * jnp.mean(scaled * normed, -1, keepdims=True)
    )


def sharp_row(block, which, width):
    row = block[which : which + 1, :].astype(F32)
    return jnp.concatenate([row] * (width // C), axis=1)


def softmax_slices(raw, sharp):
    logits = raw * sharp
    grown = jnp.exp(logits - jnp.max(logits, 0, keepdims=True))
    return grown * (1.0 / jnp.sum(grown, 0, keepdims=True))


def fold_rows(value):
    return jnp.sum(value.reshape(value.shape[0] // 8, 8, value.shape[1]), 0)


def prep_kernel(
    w_up, w_down, w_in, w_out, sharp, slice_weight, one, two, pack, slices_t, slices, gain1, gain2, s_scr
):
    gain1[...] = one[...].astype(F32).reshape(1, C)
    gain2[...] = two[...].astype(F32).reshape(1, C)
    pack[0:256, :] = w_up[...].T
    pack[256:512, :] = w_down[...]
    pack[512:576, :] = w_in[...]
    pack[576:640, :] = w_out[...]
    row = lax.broadcasted_iota(jnp.int32, (16, C), 0)
    both = sharp[...].astype(F32).reshape(1, GH)
    pack[640:656, :] = jnp.where(row == 0, both[:, 0:1], both[:, 1:2]).astype(BF)
    s_scr[...] = jnp.zeros_like(s_scr)
    weight = slice_weight[...].astype(F32)
    twice = jnp.concatenate([weight, weight], 1)
    lane = lax.broadcasted_iota(jnp.int32, (HEAD_DIM, 128), 1)
    for k in range(BLOCKS):
        at = slice(k * 128, (k + 1) * 128)
        s_scr[k * 64 : k * 64 + 32, at] = jnp.where(lane < SLICES, twice, 0.0)
        s_scr[k * 64 + 32 : k * 64 + 64, at] = jnp.where(lane < SLICES, 0.0, twice)
    slices[...] = s_scr[...].astype(BF)
    slices_t[...] = s_scr[...].T.astype(BF)


def fill_kernel(z, *refs):
    out = refs[-1]
    for k, ref in enumerate(refs[:-2]):

        @pl.when(pl.program_id(0) == k)
        def _():
            out[...] = ref[...].astype(F32)


def finish_kernel(z, first, second, before, t0, t1, t2, t3, w0, w1, *refs):
    out, gin, gslice, gsharp, gq, gk, gv, gout, gup, gdown, g1, g2 = refs
    fill_kernel(z, first, second, before, out)

    @pl.when(pl.program_id(0) == 0)
    def _():
        a, b, c, d = (t[...].astype(F32) for t in (t0, t1, t2, t3))
        tail = (a + c) + (b + d)
        gin[...] = tail[0:64]
        gslice[...] = tail[64:96, 0:64] + tail[64:96, 64:128]
        gq[...] = tail[64:96, 128:160]
        gk[...] = tail[64:96, 160:192]
        gv[...] = tail[64:96, 192:224]
        gsharp[...] = jnp.concatenate(
            [
                jnp.sum(tail[96:97, 0:128], 1, keepdims=True),
                jnp.sum(tail[96:97, 128:256], 1, keepdims=True),
            ],
            1,
        )
        g1[...] = tail[97:98]
        g2[...] = tail[98:99]
        gout[...] = tail[112:176]

        @pl.when(z[1] == 0)
        def _():
            gdown[...] = w0[...].T
            gup[...] = w1[...]

        @pl.when(z[1] == 1)
        def _():
            gdown[...] = w1[...].T
            gup[...] = w0[...]


def own_sums_kernel(pts, gain, w_in, spread_slices, sharp, out, acc, den):
    step = pl.program_id(0)

    @pl.when(step == 0)
    def _():
        acc[...] = jnp.zeros_like(acc)
        den[...] = jnp.zeros_like(den)

    normed, _ = norm_parts(pts[...].astype(F32))
    normed_in = (normed * gain[...].astype(F32)).astype(BF)
    middle = dot_nt(normed_in, w_in[...]).astype(BF)
    raw = dot_nt(spread_slices[:, 0:64], middle)
    rows = raw.shape[1]
    sharps = sharp[...]
    parts = [
        softmax_slices(raw[h * SLICES : (h + 1) * SLICES], sharp_row(sharps, h, rows))
        for h in range(GH)
    ]
    weights = jnp.concatenate(parts, 0)
    total = weights[:, 0:128]
    for j in range(1, rows // 128):
        total = total + weights[:, j * 128 : (j + 1) * 128]
    den[...] += total
    acc[...] += dot(weights.astype(BF), middle)

    @pl.when(step == pl.num_programs(0) - 1)
    def _():
        flipped = acc[...].T
        lane = lax.broadcasted_iota(jnp.int32, (HEAD_DIM, 128), 1)
        out[0:HEAD_DIM, :] = jnp.where(lane < SLICES, flipped[:HEAD_DIM], flipped[HEAD_DIM:])
        row = jnp.sum(den[...].T, 0, keepdims=True)
        out[HEAD_DIM : HEAD_DIM + 8, :] = jnp.broadcast_to(row, (8, 128))


def weights_kernel(z, pts, gain, in0, in1, in2, in3, spread_slices, s0, s1, s2, s3, *rest):
    wt, mid, w_in = rest

    @pl.when(pl.program_id(0) == 0)
    def _():
        for k, ref in enumerate((in0, in1, in2, in3)):
            w_in[k * 64 : (k + 1) * 64, :] = ref[...]

    normed, _ = norm_parts(pts[...].astype(F32))
    normed_in = (normed * gain[...].astype(F32)).astype(BF)
    middle = dot_nt(normed_in, w_in[...]).astype(BF)
    mid[...] = middle
    raw = dot_nt(spread_slices[...], middle)
    rows = raw.shape[1]
    for h in range(HEADS):
        sharp = sharp_row((s0, s1, s2, s3)[h // GH][...], h % GH, rows)
        wt[h * SLICES : (h + 1) * SLICES, :] = softmax_slices(
            raw[h * SLICES : (h + 1) * SLICES], sharp
        ).astype(BF)


def place_tokens(flat, tokens):
    flat[...] = jnp.zeros_like(flat)
    lane = lax.broadcasted_iota(jnp.int32, (HEAD_DIM, 128), 1)
    for k, ref in enumerate(tokens):
        t = ref[0:HEAD_DIM, :]
        flat[k * 64 : k * 64 + 32, k * 128 : (k + 1) * 128] = jnp.where(lane < SLICES, t, 0.0)
        flat[k * 64 + 32 : k * 64 + 64, k * 128 : (k + 1) * 128] = jnp.where(
            lane < SLICES, 0.0, t
        )


def own_block(flipped, k):
    lane = lax.broadcasted_iota(jnp.int32, (HEAD_DIM, 128), 1)
    block = flipped[k * 64 : (k + 1) * 64, k * 128 : (k + 1) * 128]
    return jnp.where(lane < SLICES, block[:HEAD_DIM], block[HEAD_DIM:])


def mlp_kernel(z, pts, cot, wt, *refs):
    tokens, refs = refs[:4], refs[4:]
    gain, refs = refs[0], refs[1:]
    ups, downs, outs, refs = refs[:4], refs[4:8], refs[8:12], refs[12:]
    mixed, gres, gspread, low_mixed, gt0, gt1, gt2, gt3, wg0, wg1, wg2, wg3, gout, g2 = refs[:14]
    flat, tok_t, w_out, acc_tok, acc_w = refs[14:]
    step = pl.program_id(0)

    @pl.when(step == 0)
    def _():
        place_tokens(flat, tokens)
        tok_t[...] = flat[...].astype(BF)
        for k, ref in enumerate(outs):
            w_out[k * 64 : (k + 1) * 64, :] = ref[...]
        acc_tok[...] = jnp.zeros_like(acc_tok)
        acc_w[...] = jnp.zeros_like(acc_w)
        gout[...] = jnp.zeros_like(gout)
        g2[...] = jnp.zeros_like(g2)

    weights = wt[...]
    spread_t = dot(tok_t[...], weights).astype(BF)
    spread = spread_t.T
    resid = pts[...].astype(F32) + dot(spread, w_out[...])
    normed, scale = norm_parts(resid)
    gain_row = gain[...].astype(F32)
    normed_mid = (normed * gain_row).astype(BF)
    cotangent = cot[...]
    total = resid
    gmid = None
    cot_t = cotangent.T
    normed_t = normed_mid.T
    for k in range(BLOCKS):
        up, down = ups[k][...], downs[k][...]
        hidden = dot_nt(normed_mid, up).astype(BF)
        square = hidden * hidden
        inner = jnp.tanh(hidden * (C0 + C1 * square))
        half = 0.5 + 0.5 * inner
        gelu = hidden * half
        active = gelu
        total = total + dot(active, down)
        slope = half + gelu * (1.0 - half) * (2.0 * C0 + 6.0 * C1 * square)
        ghid = dot_nt(cotangent, down).astype(BF) * slope
        part = dot(ghid, up)
        gmid = part if gmid is None else gmid + part
        acc_w[k, 0:C, :] += dot(cot_t, active)
        acc_w[k, C : 2 * C, :] += dot(normed_t, ghid)
    mixed[...] = total
    grad = cotangent.astype(F32) + norm_back_rows(gmid, normed, scale, gain_row)
    low = grad.astype(BF)
    gres[...] = low
    gsp = dot_nt(low, w_out[...]).astype(BF)
    gspread[...] = gsp
    low_mixed[...] = total.astype(BF)
    acc_tok[...] += dot(weights, gsp)
    gout[...] += dot(spread_t, low)
    g2[...] += fold_rows(gmid * normed)

    @pl.when(step == pl.num_programs(0) - 1)
    def _():
        flipped = acc_tok[...].T
        for k, ref in enumerate((gt0, gt1, gt2, gt3)):
            ref[...] = own_block(flipped, k)
        for k, ref in enumerate((wg0, wg1, wg2, wg3)):
            ref[...] = acc_w[k].astype(ref.dtype)


def points_kernel(z, pts, wt, mid, gspread, gres, *refs):
    tokens, gnums, refs = refs[:4], refs[4:8], refs[8:]
    gain, slices_t, slices, refs = refs[0], refs[1], refs[2], refs[3:]
    ins, sharps, refs = refs[:4], refs[4:8], refs[8:]
    qkv, g2, gout, gpts, low_a, low_b, o0, o1, o2, o3 = refs[:10]
    flat, tok, gn_t, gn, gden, w_in, acc_in, acc_s, acc_g, acc_h = refs[10:]
    step = pl.program_id(0)

    @pl.when(step == 0)
    def _():
        place_tokens(flat, tokens)
        tok[...] = flat[...].T.astype(BF)
        place_tokens(flat, gnums)
        gn_t[...] = flat[...].astype(BF)
        gn[...] = flat[...].T.astype(BF)
        for k, ref in enumerate(gnums):
            row = ref[HEAD_DIM : HEAD_DIM + 1, :]
            gden[k * 128 : (k + 1) * 128, :] = jnp.broadcast_to(row, (128, 128)).T
        for k, ref in enumerate(ins):
            w_in[k * 64 : (k + 1) * 64, :] = ref[...]
        acc_in[...] = jnp.zeros_like(acc_in)
        acc_s[...] = jnp.zeros_like(acc_s)
        acc_g[...] = jnp.zeros_like(acc_g)
        acc_h[...] = jnp.zeros_like(acc_h)

    normed, scale = norm_parts(pts[...].astype(F32))
    gain_row = gain[...].astype(F32)
    weights = wt[...]
    middle = mid[...]
    rows = weights.shape[1]
    gw = dot_nt(tok[...], gspread[...]) + dot_nt(gn[...], middle)
    pieces, sharp_sums = [], []
    raw = dot_nt(slices_t[...], middle)
    for h in range(HEADS):
        at = slice(h * SLICES, (h + 1) * SLICES)
        sharp = sharp_row(sharps[h // GH][...], h % GH, rows)
        w = softmax_slices(raw[at], sharp)
        g = gw[at] + jnp.concatenate([gden[at, :]] * (rows // 128), axis=1)
        gl = w * (g - jnp.sum(w * g, 0, keepdims=True))
        pieces.append((gl * sharp).astype(BF))
        sharp_sums.append(jnp.sum(gl * raw[at], 0, keepdims=True))
    graw = jnp.concatenate(pieces, 0)
    gmid_t = (dot(gn_t[...], weights) + dot(slices[...], graw)).astype(BF)
    gmid = gmid_t.T
    gnormed = dot(gmid, w_in[...])
    result = gres[...].astype(F32) + norm_back_rows(gnormed, normed, scale, gain_row)
    gpts[...] = result

    @pl.when(step < pl.num_programs(0) // 2)
    def _():
        low_a[...] = result.astype(BF)

    @pl.when(step >= pl.num_programs(0) // 2)
    def _():
        low_b[...] = result.astype(BF)

    normed_in = (normed * gain_row).astype(BF)
    acc_in[...] += dot(gmid_t, normed_in)
    acc_s[...] += dot(graw, middle)
    acc_g[...] += fold_rows(gnormed * normed)
    acc_h[...] += jnp.concatenate(sharp_sums, 0)

    @pl.when(step == pl.num_programs(0) - 1)
    def _():
        flipped = acc_s[...].T
        gsharp = acc_h[:, 0:128]
        for j in range(1, rows // 128):
            gsharp = gsharp + acc_h[:, j * 128 : (j + 1) * 128]
        gslice = jnp.zeros((HEAD_DIM, 128), F32)
        for k in range(BLOCKS):
            gslice = gslice + own_block(flipped, k)
        gain1 = jnp.sum(acc_g[...], 0, keepdims=True)
        gain2 = jnp.sum(g2[...], 0, keepdims=True)
        for k, ref in enumerate((o0, o1, o2, o3)):
            ref[0:64, :] = acc_in[k * 64 : (k + 1) * 64, :].astype(ref.dtype)
            ref[64:96, 0:128] = gslice.astype(ref.dtype)
            ref[64:96, 128:256] = qkv[...].astype(ref.dtype)
            wide = jnp.concatenate([gsharp[2 * k : 2 * k + 1], gsharp[2 * k + 1 : 2 * k + 2]], 1)
            ref[96:112, :] = jnp.concatenate(
                [wide, gain1, gain2, jnp.zeros((13, C), F32)], 0
            ).astype(ref.dtype)
            ref[112:176, :] = gout[k * 64 : (k + 1) * 64, :].astype(ref.dtype)


def halves(value):
    high = value.astype(BF)
    return high, (value - high.astype(F32)).astype(BF)


def dot3(a, b, form=dot):
    (ah, al), (bh, bl) = halves(a), halves(b)
    return form(ah, bh) + (form(ah, bl) + form(al, bh))


def dot3_nt(a, b):
    return dot3(a, b, dot_nt)


def token_parts(nd, wq, wk, wv):
    padded = jnp.concatenate([nd, jnp.zeros((88, 128), F32)], 0).T
    denom = padded[:, HEAD_DIM : HEAD_DIM + 1]
    tok = padded[:, :HEAD_DIM] / denom
    q, k, v = dot3(tok, wq), dot3(tok, wk), dot3(tok, wv)
    scores = dot3_nt(q, k) * (1.0 / HEAD_DIM**0.5)
    row = lax.broadcasted_iota(jnp.int32, (128, 128), 0) < SLICES
    col = lax.broadcasted_iota(jnp.int32, (128, 128), 1) < SLICES
    same = row == col
    scores = jnp.where(same, scores, -jnp.inf)
    p = jnp.exp(scores - jnp.max(scores, -1, keepdims=True))
    p = p / jnp.sum(p, -1, keepdims=True)
    return denom, tok, q, k, v, p


def flip(value):
    n = value.shape[1]
    return jnp.concatenate([value, jnp.zeros((128, 128 - n), F32)], 1).T[:n]


def tokens_kernel(a, b, c, d, wq, wk, wv, total, tokens):
    nd = (a[...] + c[...]) + (b[...] + d[...])
    total[...] = nd
    _, _, _, _, v, p = token_parts(nd, *(w[...].astype(F32) for w in (wq, wk, wv)))
    mixed = dot3(p, v).astype(BF).astype(F32)
    tokens[...] = flip(mixed)


def tokens_back_kernel(scale, nd, a, b, c, d, wq, wk, wv, gn, qkv):
    gt = (a[...] + c[...]) + (b[...] + d[...])
    g = jnp.concatenate([gt, jnp.zeros((96, 128), F32)], 0).T[:, :HEAD_DIM]
    wq, wk, wv = (w[...].astype(F32) for w in (wq, wk, wv))
    denom, tok, q, k, v, p = token_parts(nd[...], wq, wk, wv)
    dv = dot3(p.T, g)
    dp = dot3_nt(g, v)
    ds = p * (dp - jnp.sum(p * dp, -1, keepdims=True)) * (1.0 / HEAD_DIM**0.5)
    dq = dot3(ds, k)
    dk = dot3(ds.T, q)
    gmt = dot3_nt(dq, wq) + dot3_nt(dk, wk) + dot3_nt(dv, wv)
    gnum = (gmt / denom).astype(BF).astype(F32)
    gden = -jnp.sum(gmt * tok, -1, keepdims=True) / denom
    gn[0:HEAD_DIM, :] = flip(gnum)
    gn[HEAD_DIM : HEAD_DIM + 8, :] = flip(jnp.broadcast_to(gden, (128, 8)))
    tok_t = flip(tok)
    qkv[...] = scale * jnp.concatenate(
        [dot3(tok_t, dq), dot3(tok_t, dk), dot3(tok_t, dv), jnp.zeros((32, 32), F32)],
        1,
    )


def full(shape):
    return pl.BlockSpec(shape, lambda *_: (0,) * len(shape))


def part(shape, row):
    return pl.BlockSpec(shape, lambda *_: (row, 0))


def shape_of(shape, dtype):
    return jax.ShapeDtypeStruct(shape, dtype)


def cost(us):
    return pl.CostEstimate(flops=int(us * 1.0e6), bytes_accessed=1024, transcendentals=0)


UP, DOWN, WIN, WOUT, SHARP = (256, 0), (256, 1), (64, 8), (64, 9), (16, 40)
WIDE, NARROW = 1024, 512
TAIL = 176


def pack_specs(kind):
    return [part((kind[0], C), kind[1])] * BLOCKS


def local(
    pts_size,
    points,
    cotangent,
    gain_one,
    w_in,
    slice_weight,
    sharp,
    w_query,
    w_key,
    w_value,
    w_out,
    gain_two,
    w_up,
    w_down,
):
    axes = ("pts", "head")
    rows = points.shape[0]
    quarter = rows // BLOCKS

    def pull(value, dx=0, dy=0, dc=0, dz=0):
        pairs = []
        for p in range(pts_size):
            x, y, c = p // 8, (p // 2) % 4, p % 2
            there = p
            if pts_size > 1:
                there = (((x + dx) % 4) * 4 + (y + dy) % 4) * 2 + (c + dc) % 2
            for z in range(BLOCKS):
                pairs.append((there * BLOCKS + (z + dz) % BLOCKS, p * BLOCKS + z))
        return lax.ppermute(value, axes, pairs)

    def pulls(value, axis):
        return [pull(value, **{axis: k}) for k in (1, 2, 3)]

    def tie(*values):
        return lax.optimization_barrier(values)

    def add4(a, r):
        return (a + r[1].astype(F32)) + (r[0].astype(F32) + r[2].astype(F32))

    def core_sum(value):
        return value + pull(value, dc=1) if pts_size > 1 else value

    def rounded(value):
        return lax.reduce_precision(value, 8, 7)

    def axis_peers(value, axis):
        if pts_size == 1:
            return [jnp.zeros_like(value)] * 3
        return pulls(value, axis)

    core = lax.axis_index("pts").astype(jnp.int32) % 2
    z = jnp.stack([lax.axis_index("head").astype(jnp.int32), core])

    def row_spec(size, away, first=0):
        n = quarter // size
        return pl.BlockSpec(
            (size, C), lambda i, z: (lax.rem(z[0] + away, BLOCKS) * n + first // size + i, 0)
        )

    def own_spec(size, first=0):
        return pl.BlockSpec((size, C), lambda i, z: (first // size + i, 0))

    def own_cols(size, first=0):
        return pl.BlockSpec((HM, size), lambda i, z: (0, first // size + i))

    def grid(steps, in_specs, out_specs, scratch=()):
        return pltpu.PrefetchScalarGridSpec(
            num_scalar_prefetch=1,
            grid=steps,
            in_specs=in_specs,
            out_specs=out_specs,
            scratch_shapes=scratch,
        )

    any_spec = pl.BlockSpec(memory_space=pl.ANY)
    params = pltpu.CompilerParams(vmem_limit_bytes=VMEM_LIMIT)

    wq, wk, wv = w_query, w_key, w_value
    pack, slices_t, slices, gain1, gain2 = pl.pallas_call(
        prep_kernel,
        out_shape=[shape_of((656, C), BF), shape_of((HM, C), BF), shape_of((C, HM), BF)]
        + [shape_of((1, C), F32)] * 2,
        scratch_shapes=[pltpu.VMEM((C, HM), F32)],
        compiler_params=params,
        cost_estimate=cost(2),
        name="prep",
    )(w_up, w_down, w_in.T, w_out, sharp, slice_weight, gain_one, gain_two)

    nd = pl.pallas_call(
        own_sums_kernel,
        grid=(rows // (2 * WIDE),),
        in_specs=[
            pl.BlockSpec((2 * WIDE, C), lambda i: (i, 0)),
            full((1, C)),
            part((64, C), WIN[1]),
            part((128, C), 0),
            part((16, C), SHARP[1]),
        ],
        out_specs=full((40, 128)),
        out_shape=shape_of((40, 128), F32),
        scratch_shapes=[pltpu.VMEM((128, 64), F32), pltpu.VMEM((128, 128), F32)],
        compiler_params=params,
        cost_estimate=cost(8),
        name="own_sums",
    )(points, gain1, pack, slices_t, pack)

    half = quarter // 2

    def weights_call():
        return pl.pallas_call(
            weights_kernel,
            grid_spec=grid(
                (quarter // WIDE,),
                [row_spec(WIDE, 0), full((1, C))]
                + pack_specs(WIN)
                + [full((HM, C))]
                + pack_specs(SHARP),
                [own_cols(WIDE), own_spec(WIDE)],
                [pltpu.VMEM((C, C), BF)],
            ),
            out_shape=[shape_of((HM, quarter), BF), shape_of((quarter, C), BF)],
            compiler_params=params,
            cost_estimate=cost(5),
            name="weights",
        )(z, points, gain1, *packs, slices_t, *packs)

    def mlp_call(tokens, wt):
        size = WIDE
        out_shape = [shape_of((rows, C), F32)] + [shape_of((quarter, C), BF)] * 3
        out_shape += [shape_of((HEAD_DIM, 128), F32)] * 4
        out_shape += [shape_of((2 * C, C), F32)] + [shape_of((2 * C, C), BF)] * 3
        out_shape += [shape_of((C, C), F32), shape_of((8, C), F32)]
        out_specs = [row_spec(size, 0)] + [own_spec(size)] * 3
        out_specs += [full((HEAD_DIM, 128))] * 4 + [full((2 * C, C))] * 4
        out_specs += [full((C, C)), full((8, C))]
        return pl.pallas_call(
            mlp_kernel,
            grid_spec=grid(
                (quarter // size,),
                [row_spec(size, 0), row_spec(size, 0), own_cols(size)]
                + [full((HEAD_DIM, 128))] * 4
                + [full((1, C))]
                + pack_specs(UP)
                + pack_specs(DOWN)
                + pack_specs(WOUT),
                out_specs,
                [
                    pltpu.VMEM((C, HM), F32),
                    pltpu.VMEM((C, HM), BF),
                    pltpu.VMEM((C, C), BF),
                    pltpu.VMEM((HM, C), F32),
                    pltpu.VMEM((BLOCKS, 2 * C, C), F32),
                ],
            ),
            out_shape=out_shape,
            compiler_params=params,
            cost_estimate=cost(16),
            name="mlp",
        )(z, points, cotangent, wt, *tokens, gain2, *packs, *packs, *packs)

    half = quarter // 2

    def points_call(tokens, gnums, wt, mid, gspread, gres, qkv, g2, gout):
        size = half
        steps = quarter // size
        halves = [full((half, C))] * 2
        return pl.pallas_call(
            points_kernel,
            grid_spec=grid(
                (steps,),
                [row_spec(size, 0), own_cols(size)]
                + [own_spec(size)] * 3
                + [full((HEAD_DIM, 128))] * 4
                + [full((40, 128))] * 4
                + [full((1, C)), full((HM, C)), full((C, HM))]
                + pack_specs(WIN)
                + pack_specs(SHARP)
                + [full((HEAD_DIM, 128)), full((8, C)), full((C, C))],
                [row_spec(size, 0)] + halves + [full((TAIL, C))] * 4,
                [
                    pltpu.VMEM((C, HM), F32),
                    pltpu.VMEM((HM, C), BF),
                    pltpu.VMEM((C, HM), BF),
                    pltpu.VMEM((HM, C), BF),
                    pltpu.VMEM((HM, 128), F32),
                    pltpu.VMEM((C, C), BF),
                    pltpu.VMEM((C, C), F32),
                    pltpu.VMEM((HM, C), F32),
                    pltpu.VMEM((8, C), F32),
                    pltpu.VMEM((HEADS, size), F32),
                ],
            ),
            out_shape=[shape_of((rows, C), F32)]
            + [shape_of((half, C), BF)] * 2
            + [shape_of((TAIL, C), F32)]
            + [shape_of((TAIL, C), BF)] * 3,
            compiler_params=params,
            cost_estimate=cost(12),
            name="points",
        )(
            z, points, wt, mid, gspread, gres, *tokens, *gnums, gain1, slices_t, slices,
            *packs, *packs, qkv, g2, gout
        )

    def fill_out(at):
        return pl.BlockSpec(
            (half, C), lambda i, z: (lax.rem(2 * z[0] + at(i), 2 * BLOCKS), 0)
        )

    def fill_call(at, parts, before):
        n = len(parts)
        return pl.pallas_call(
            fill_kernel,
            grid_spec=grid((n,), [s for _, s in parts] + [any_spec], fill_out(at)),
            out_shape=shape_of((rows, C), F32),
            input_output_aliases={n + 1: 0},
            compiler_params=params,
            cost_estimate=cost(3),
            name="fill",
        )(z, *[p for p, _ in parts], before)

    def halves_of(value):
        return [(value, part((half, C), 0)), (value, part((half, C), 1))]

    def whole(*values):
        return [(v, full((half, C))) for v in values]

    nd = core_sum(nd)
    nd, sent = tie(nd, pack)
    got = axis_peers(nd, "dx")
    packs = [pack, pull(sent, dz=1), None, pull(sent, dz=3)]
    nd = add4(nd, got)
    nd, sent = tie(nd, sent)
    got = axis_peers(nd, "dy")
    packs[2] = pull(sent, dz=2)
    nd, own_tokens = pl.pallas_call(
        tokens_kernel,
        out_shape=[shape_of((40, 128), F32), shape_of((HEAD_DIM, 128), F32)],
        compiler_params=params,
        cost_estimate=cost(3),
        name="tokens",
    )(nd, *got, wq, wk, wv)
    got = pulls(own_tokens, "dz")

    own_tokens, *packs = tie(own_tokens, *packs)
    wt, mid = weights_call()
    got, wt = tie(got, wt)
    tokens = [own_tokens] + list(got)

    result = mlp_call(tokens, wt)
    mixed, gres, gspread, send = result[:4]
    gts, wgs, (gout, g2) = result[4:8], result[8:12], result[12:]

    got = [pull(gts[BLOCKS - k], dz=k) for k in (1, 2, 3)]
    wgot = [pull(wgs[3], dz=1), pull(wgs[2], dz=2)]
    gt = add4(gts[0], got)
    gt, wg1 = tie(gt, wgs[1])
    wgot.append(pull(wg1, dz=3))
    gt = core_sum(gt)
    gt, send = tie(gt, send)
    got = axis_peers(gt, "dx")
    near = [pull(send, dz=1), pull(send, dz=3)]
    got, wgot = tie(got, wgot)
    gt = add4(gt, got)
    got = axis_peers(gt, "dy")
    wsum = add4(wgs[0], wgot)
    wlow = wsum.astype(BF)
    own_gn, qkv = pl.pallas_call(
        functools.partial(tokens_back_kernel, 1.0 / pts_size),
        out_shape=[shape_of((40, 128), F32), shape_of((HEAD_DIM, 128), F32)],
        compiler_params=params,
        cost_estimate=cost(4),
        name="tokens_back",
    )(nd, gt, *got, wq, wk, wv)
    got = pulls(own_gn, "dz")
    own_gn, wsum, wlow = tie(own_gn, wsum, wlow)
    if pts_size > 1:
        wsum = rounded(wsum) + pull(wlow, dc=1).astype(F32)
        wlow = lax.dynamic_slice_in_dim(wsum, core * C, C, 0).astype(BF)
    got, wlow = tie(got, wlow)
    wgot = axis_peers(wlow[:C], "dx")
    got, near = tie(got, near)
    near2 = [pull(near[0][:half], dz=1), pull(near[1][half:], dz=3)]
    gnums = [own_gn] + list(got)

    result = points_call(tokens, gnums, wt, mid, gspread, gres, qkv, g2, gout)
    gpts, low_a, low_b, outs = result[0], result[1], result[2], result[3:]
    gpts, outs, low_a, low_b, wgot, near2 = tie(gpts, outs, low_a, low_b, wgot, near2)

    got = [pull(outs[BLOCKS - k], dz=k) for k in (1, 2, 3)]
    a1, b3 = pull(low_a, dz=1), pull(low_b, dz=3)
    outs, mixed = tie(outs, mixed)
    mixed = fill_call(lambda i: 2 + i, halves_of(near[0]) + whole(*near2), mixed)
    got, mixed = tie(got, mixed)
    tail = core_sum(add4(outs[0], got))
    both = jnp.concatenate([tail, add4(wlow[:C].astype(F32), wgot)], 0).astype(BF)
    both, a1, b3 = tie(both, a1, b3)
    far2 = [pull(a1, dz=1), pull(b3, dz=3)]
    got = axis_peers(both, "dy")
    both, mixed = tie(both, mixed)
    mixed = fill_call(lambda i: 6 + i, halves_of(near[1]), mixed)
    got, mixed, far2 = tie(got, mixed, far2)
    both = add4(both.astype(F32), got)
    both, low_a, low_b = tie(both, low_a, low_b)
    b1, a3 = pull(low_b, dz=1), pull(low_a, dz=3)
    tail, wsum = both[:TAIL].astype(BF), both[TAIL:]
    if pts_size > 1:
        other = pull(wsum, dc=1)
    else:
        other = wlow[C:].astype(F32)
    wsum, other, tail = tie(wsum, other, tail)
    got = axis_peers(tail, "dx")
    tail, gpts = tie(tail, gpts)
    gpts = fill_call(
        lambda i: 2 + i + jnp.minimum(i, 1) + i // 3, whole(a1, *far2, b3), gpts
    )
    got, gpts, b1, a3 = tie(got, gpts, b1, a3)
    shapes = [(64, C), (32, 64), (1, GH), (32, 32), (32, 32), (32, 32)]
    shapes += [(64, C), (C, C), (C, C), (1, C), (1, C)]
    result = pl.pallas_call(
        finish_kernel,
        grid_spec=grid(
            (2,),
            [full((half, C))] * 2 + [any_spec] + [full((TAIL, C))] * 4 + [full((C, C))] * 2,
            [fill_out(lambda i: 3 + 3 * i)] + [full(s) for s in shapes],
        ),
        out_shape=[shape_of((rows, C), F32)] + [shape_of(s, F32) for s in shapes],
        input_output_aliases={3: 0},
        compiler_params=params,
        cost_estimate=cost(4),
        name="finish",
    )(z, b1, a3, gpts, tail, *got, wsum, other)
    gpts, gin, gslice, gsharp, gq, gk, gv, gout, gup, gdown, g1, g2 = result
    return (
        mixed, gpts, gin.T, gslice, gsharp.reshape(GH), gq, gk, gv, gout, gup, gdown,
        g1.reshape(C), g2.reshape(C),
    )


def solution(mesh):
    row, none, cols, heads = P("pts", None), P(), P(None, "head"), P("head")
    down = P("head", None)
    placed = (row, row, none, cols, none, heads, none, none, none, down, none, cols, down)
    given = (row, row, cols, none, heads, none, none, none, down, cols, down, none, none)
    return jax.shard_map(
        functools.partial(local, mesh.shape["pts"]),
        mesh=mesh,
        in_specs=placed,
        out_specs=given,
        check_vma=False,
    )
```
